32 devices in a mesh: batch: 32 (over z, y, x, core).
Axes of the slice: x: 2, y: 2, z: 4, core: 2. Of those that a mesh axis runs over, the one named last changes fastest.
Arguments:
- params: float32 [2473984], P('batch')
- moment1: float32 [2473984], P('batch')
- moment2: float32 [2473984], P('batch'), as said below
- ema_params: float32 [2473984], P('batch')
- trajectories: float32 [2, 64, 384, 6], P(None, 'batch'), may hold values from -6 to 6
- noise_draw: float32 [2, 64, 384, 6], P(None, 'batch'), may hold values from -6 to 6
- timesteps: int32 [2, 64], P(None, 'batch'), may hold values from 0 to 255
- lengths: int32 [2, 64], P(None, 'batch'), may hold values from 96 to 384, as said below
Outputs:
- new_params: float32 [2473984], P('batch')
- new_moment1: float32 [2473984], P('batch')
- new_moment2: float32 [2473984], P('batch')
- new_ema: float32 [2473984], P('batch')
- low_params: bfloat16 [2473984], P('batch')
- grad_norm: float32 [], replicated
- loss_sum: float32 [], replicated
- frame_count: float32 [], replicated
The draws below stay inside these ranges and needn't reach their ends.
Inputs may be any that keep to these rules, and one draw needn't show every extreme that they name: `lengths`: in each micro-batch some horizon has all 384 frames valid. `moment2`: second moments are positive.
All inputs are finite; a program needn't handle non-finite values.
Results may differ from the reference program's by a relative error of at most 0.0068.
Values may be sent and summed in bfloat16 or wider, within the bound.
No kernel may reach another device: no remote copies, remote signals or barrier semaphores. Data moves between devices by JAX's collectives and lax.ppermute only.
A program may use at most 128 MiB of HBM per device.

```python
import math
import jax
import jax.numpy as jnp
from jax import lax

D = 256
TE = 128
CH = 6
GROUPS = 8
K = 5
L = 384
MB = 2
DIFF = 256
STEP = 10
HOR = 64
P_RAW = 2471942
PARAMS = 2473984


def kind_table():
    entries = [(TE, D, TE), (1, D, 0), (D, D, D), (1, D, 0), (K * CH, D, K * CH), (1, D, 0)]
    for width_in, with_res in ((D, False), (2 * D, True)):
        entries += [(K * width_in, D, K * width_in), (1, D, 0), (1, D, -1), (1, D, 0), (D, D, D), (1, D, 0), (K * D, D, K * D), (1, D, 0), (1, D, -1), (1, D, 0)]
        if with_res:
            entries += [(width_in, D, width_in), (1, D, 0)]
        if not with_res:
            entries += [(3 * D, D, 3 * D), (1, D, 0), (4 * D, D, 2 * D), (1, D, 0)]
    entries += [(D, CH, D), (1, CH, 0)]
    return entries


def weight_pieces(key):
    parts = []
    used = 0
    for index_number, (row_count, col_count, fan_in) in enumerate(kind_table()):
        normal_part = jax.random.normal(jax.random.fold_in(key, index_number), (row_count * col_count,), jnp.float32)
        if fan_in > 0:
            parts.append(normal_part * fan_in ** (-0.5))
        elif fan_in < 0:
            parts.append(1.0 + 0.1 * normal_part)
        else:
            parts.append(0.1 * normal_part)
        used += row_count * col_count
    parts.append(0.1 * jax.random.normal(jax.random.fold_in(key, 999), (PARAMS - used,), jnp.float32))
    return jnp.concatenate(parts)


def grad_scales():
    scales = []
    used = 0
    base = 0.05 / P_RAW ** 0.5
    for row_count, col_count, fan_in in kind_table():
        factor = base if fan_in > 0 else 4.0 * base
        scales.append(jnp.full((row_count * col_count,), factor, jnp.float32))
        used += row_count * col_count
    scales.append(jnp.full((PARAMS - used,), 4.0 * base, jnp.float32))
    return jnp.concatenate(scales)


def draw_params(key, part):
    key = jax.random.fold_in(key, 11)
    return weight_pieces(key)


def draw_ema_params(key, part):
    key = jax.random.fold_in(key, 12)
    return weight_pieces(key)


def draw_moment1(key, part):
    key = jax.random.fold_in(key, 13)
    return 0.1 / 0.9 * grad_scales() * jax.random.normal(key, (PARAMS,), jnp.float32)


def draw_moment2(key, part):
    key = jax.random.fold_in(key, 14)
    spread = jax.random.uniform(key, (PARAMS,), jnp.float32, 1.0, 4.0)
    scales = grad_scales()
    return spread * (0.05 / 0.95) * scales * scales


def draw_lengths(key, part):
    key = jax.random.fold_in(key, 15)
    first_key, second_key = jax.random.split(key)
    drawn = jax.random.randint(first_key, (MB, HOR), L // 4, L + 1, jnp.int32)
    chosen = jax.random.randint(second_key, (MB, 1), 0, HOR, jnp.int32)
    columns = jnp.arange(HOR, dtype=jnp.int32)[None, :]
    return jnp.where(columns == chosen, jnp.int32(L), drawn)


def touch_ends(values, own_key, smallest, high):
    longest = values.shape.index(max(values.shape))
    spots = []
    for shift in (0, 1):
        where = [jax.random.randint(jax.random.fold_in(own_key, axis), (), 0, length) for axis, length in enumerate(values.shape)]
        where[longest] = (where[longest] + shift) % values.shape[longest]
        spots.append(tuple(where))
    return values.at[spots[0]].set(smallest).at[spots[1]].set(high)


def level_of(rng, dims, cuts, smallest, top_value):
    gain = 1.0
    for position, shards_of in cuts:
        draws = jax.random.uniform(jax.random.fold_in(jax.random.fold_in(rng, 6), position), (shards_of,), jnp.float32, smallest / len(cuts), top_value / len(cuts))
        gain = gain * jnp.repeat(jnp.exp(draws), dims[position] // shards_of).reshape((-1,) + (1,) * (len(dims) - 1 - position))
    return gain


def scatter_about(key, extent, deviation, limit, cuts=(), kind=jnp.bfloat16):
    level = level_of(key, extent, cuts, -0.22, 0.18) if cuts else 1.0
    values = jax.random.normal(key, extent, jnp.float32) * deviation * level
    return jnp.minimum(jnp.maximum(values, -limit), limit).astype(kind)


def setup_inputs(seed: int = 0) -> dict:
    splits = jax.random.split(jax.random.key(seed), 9)
    return {
        "params": draw_params(jax.random.fold_in(splits[8], 71), 0),
        "moment1": draw_moment1(jax.random.fold_in(splits[8], 71), 0),
        "moment2": draw_moment2(jax.random.fold_in(splits[8], 71), 0),
        "ema_params": draw_ema_params(jax.random.fold_in(splits[8], 71), 0),
        "trajectories": scatter_about(splits[4], (MB, HOR, L, CH), 1.0, 6.0, ((1, 32),), jnp.float32),
        "noise_draw": scatter_about(splits[5], (MB, HOR, L, CH), 1.0, 6.0, ((1, 32),), jnp.float32),
        "timesteps": touch_ends(jax.random.randint(splits[6], (MB, HOR), 0, DIFF), jax.random.fold_in(splits[6], 1), 0, DIFF - 1).astype(jnp.int32),
        "lengths": draw_lengths(jax.random.fold_in(splits[8], 71), 0),
    }


@jax.custom_vjp
def low(v):
    return lax.optimization_barrier(v.astype(jnp.bfloat16)).astype(jnp.float32)

@jax.custom_vjp
def low_back(v):
    return v

def low_keep(v):
    return (low(v), None)

def low_pass(kept, grad):
    return (grad,)

def back_keep(v):
    return (v, None)

def back_low(kept, grad):
    return (low(grad),)
low.defvjp(low_keep, low_pass)
low_back.defvjp(back_keep, back_low)
HIGH = lax.Precision.HIGHEST
clip_limit = 0.05

def block_entries(entries, prefix, width_in, with_res):
    entries.append((prefix + '_conv1', K * width_in, D))
    entries.append((prefix + '_bias1', 1, D))
    entries.append((prefix + '_gain1', 1, D))
    entries.append((prefix + '_shift1', 1, D))
    entries.append((prefix + '_time', D, D))
    entries.append((prefix + '_time_bias', 1, D))
    entries.append((prefix + '_conv2', K * D, D))
    entries.append((prefix + '_bias2', 1, D))
    entries.append((prefix + '_gain2', 1, D))
    entries.append((prefix + '_shift2', 1, D))
    if with_res:
        entries.append((prefix + '_res', width_in, D))
        entries.append((prefix + '_res_bias', 1, D))

def layout():
    entries = [('time_first', TE, D), ('time_first_bias', 1, D), ('time_second', D, D), ('time_second_bias', 1, D), ('input_conv', K * CH, D), ('input_bias', 1, D)]
    block_entries(entries, 'down', D, False)
    entries += [('down_sample', 3 * D, D), ('down_sample_bias', 1, D), ('up_sample', 4 * D, D), ('up_sample_bias', 1, D)]
    block_entries(entries, 'up', 2 * D, True)
    entries += [('head', D, CH), ('head_bias', 1, CH)]
    return entries

def unpack(flat_weights):
    pieces = {}
    offset = 0
    for label, row_count, col_count in layout():
        piece = flat_weights[offset:offset + row_count * col_count]
        pieces[label] = piece.reshape(row_count, col_count) if row_count > 1 else piece
        offset += row_count * col_count
    return pieces

def rounded(values):
    return low_back(low(values))

def mish(values):
    return values * jnp.tanh(jax.nn.softplus(values))

def product(values, weight):
    return jnp.einsum('...c,cd->...d', values, weight, precision=HIGH)

def conv(values, weight, bias_row):
    tap_count = weight.shape[0] // values.shape[2]
    length = values.shape[1]
    padded = jnp.pad(values, ((0, 0), (tap_count // 2, tap_count // 2), (0, 0)))
    columns = jnp.concatenate([padded[:, tap_index:tap_index + length] for tap_index in range(tap_count)], axis=2)
    return product(columns, weight) + bias_row

def group_norm(values, gain_row, shift_row):
    horizons, length, channels = values.shape
    grouped = values.reshape(horizons, length, GROUPS, channels // GROUPS)
    center = lax.optimization_barrier(jnp.mean(grouped, axis=(1, 3), keepdims=True))
    spread = lax.optimization_barrier(jnp.mean((grouped - center) ** 2, axis=(1, 3), keepdims=True))
    normed = ((grouped - center) * lax.rsqrt(spread + 1e-05)).reshape(horizons, length, channels)
    return normed * gain_row + shift_row

def res_block(values, timing, pieces, prefix, with_res):
    entered = rounded(values)
    hidden = mish(group_norm(conv(entered, pieces[prefix + '_conv1'], pieces[prefix + '_bias1']), pieces[prefix + '_gain1'], pieces[prefix + '_shift1']))
    hidden = hidden + (product(timing, pieces[prefix + '_time']) + pieces[prefix + '_time_bias'])[:, None, :]
    hidden = mish(group_norm(conv(rounded(hidden), pieces[prefix + '_conv2'], pieces[prefix + '_bias2']), pieces[prefix + '_gain2'], pieces[prefix + '_shift2']))
    if with_res:
        return hidden + product(entered, pieces[prefix + '_res']) + pieces[prefix + '_res_bias']
    return hidden + values

def horizon_loss(flat_weights, trajectory, noise_part, diffusion_steps, lengths):
    pieces = unpack(flat_weights)
    horizons, length, channels = trajectory.shape
    frames = jnp.arange(length, dtype=jnp.int32)
    valid = (frames[None, :] < lengths[:, None]).astype(jnp.float32)
    times = diffusion_steps.astype(jnp.float32)
    angle_now = ((times + 1.0) / DIFF + 0.008) / 1.008 * (math.pi / 2)
    angle_zero = 0.008 / 1.008 * (math.pi / 2)
    share = jnp.cos(angle_now) ** 2 / math.cos(angle_zero) ** 2
    noisy = (jnp.sqrt(share)[:, None, None] * trajectory + jnp.sqrt(1.0 - share)[:, None, None] * noise_part) * valid[:, :, None]
    half_width = TE // 2
    frequency = jnp.exp(-math.log(10000.0) * jnp.arange(half_width, dtype=jnp.float32) / (half_width - 1))
    angles = times[:, None] * frequency[None, :]
    embedding = jnp.concatenate([jnp.sin(angles), jnp.cos(angles)], axis=1)
    timing = mish(product(rounded(embedding), pieces['time_first']) + pieces['time_first_bias'])
    timing = product(rounded(timing), pieces['time_second']) + pieces['time_second_bias']
    timing = rounded(mish(timing))
    entry = conv(rounded(noisy), pieces['input_conv'], pieces['input_bias'])
    skipped = res_block(entry, timing, pieces, 'down', False)
    padded = jnp.pad(rounded(skipped), ((0, 0), (1, 1), (0, 0)))
    columns = jnp.concatenate([padded[:, 0:length:2], padded[:, 1:length + 1:2], padded[:, 2:length + 2:2]], axis=2)
    coarse = product(columns, pieces['down_sample']) + pieces['down_sample_bias']
    half_len = length // 2
    lifted = jnp.pad(rounded(coarse), ((0, 0), (1, 1), (0, 0)))
    earlier, current, later = (lifted[:, 0:half_len], lifted[:, 1:half_len + 1], lifted[:, 2:half_len + 2])
    kernel = pieces['up_sample'].reshape(4, D, D)
    even_rows = product(jnp.concatenate([current, earlier], axis=2), jnp.concatenate([kernel[1], kernel[3]], axis=0))
    odd_rows = product(jnp.concatenate([later, current], axis=2), jnp.concatenate([kernel[0], kernel[2]], axis=0))
    raised = jnp.stack([even_rows, odd_rows], axis=2).reshape(horizons, length, D) + pieces['up_sample_bias']
    joined = jnp.concatenate([raised, skipped], axis=2)
    top = res_block(joined, timing, pieces, 'up', True)
    prediction = product(rounded(top), pieces['head']) + pieces['head_bias']
    error = (prediction - noise_part) * valid[:, :, None]
    return jnp.sum(error * error)

def adam_update(params, moment1, moment2, ema_params, clipped):
    new_moment1 = 0.9 * moment1 + 0.1 * clipped
    new_moment2 = 0.95 * moment2 + 0.05 * clipped * clipped
    first_hat = new_moment1 / (1.0 - 0.9 ** STEP)
    second_hat = new_moment2 / (1.0 - 0.95 ** STEP)
    new_params = params - 0.01 * (first_hat / (jnp.sqrt(second_hat) + 1e-08) + 0.01 * params)
    new_ema = 0.8 * ema_params + 0.2 * new_params
    return (new_params, new_moment1, new_moment2, new_ema)

def reference(params, moment1, moment2, ema_params, trajectories, noise_draw, timesteps, lengths):
    weights = lax.optimization_barrier(params.astype(jnp.bfloat16)).astype(jnp.float32)
    per_block = 8
    blocks = MB * HOR // per_block
    data = (trajectories.reshape(blocks, per_block, L, CH), noise_draw.reshape(blocks, per_block, L, CH), timesteps.reshape(blocks, per_block), lengths.reshape(blocks, per_block))

    def advance(carry, portion):
        sums, total_loss = carry
        portion_loss, pullback = jax.vjp(lambda flat_weights: horizon_loss(flat_weights, *portion), weights)
        gradient, = pullback(jnp.ones((), jnp.float32))
        return ((sums + gradient, total_loss + portion_loss), None)
    (sums, loss_sum), _ = lax.scan(advance, (jnp.zeros_like(weights), jnp.zeros((), jnp.float32)), data)
    frame_count = jnp.sum(lengths).astype(jnp.float32) * CH
    grad_norm = jnp.sqrt(jnp.sum(sums * sums)) / frame_count
    clipped = sums / frame_count * jnp.minimum(1.0, clip_limit / (grad_norm + 1e-06))
    new_params, new_moment1, new_moment2, new_ema = adam_update(params, moment1, moment2, ema_params, clipped)
    return (new_params, new_moment1, new_moment2, new_ema, new_params.astype(jnp.bfloat16), grad_norm, loss_sum, frame_count)
```

```python
import math

import jax
import jax.numpy as jnp
from jax import lax
from jax.experimental import pallas as pl
from jax.experimental.pallas import tpu as pltpu
from jax.sharding import PartitionSpec as P

D = 256
TE = 128
CH = 6
GROUPS = 8
K = 5
DIFF = 256
STEP = 10

CHUNK = 64
HEAD = 8
clip_limit = 0.05

F32 = jnp.float32
BF16 = jnp.bfloat16


def block_entries(entries, prefix, width_in, with_res):
    entries.append((prefix + "_conv1", K * width_in))
    entries.append((prefix + "_bias1", 1))
    entries.append((prefix + "_gain1", 1))
    entries.append((prefix + "_shift1", 1))
    entries.append((prefix + "_time", D))
    entries.append((prefix + "_time_bias", 1))
    entries.append((prefix + "_conv2", K * D))
    entries.append((prefix + "_bias2", 1))
    entries.append((prefix + "_gain2", 1))
    entries.append((prefix + "_shift2", 1))
    if with_res:
        entries.append((prefix + "_res", width_in))
        entries.append((prefix + "_res_bias", 1))


def layout():
    entries = [
        ("time_first", TE),
        ("time_first_bias", 1),
        ("time_second", D),
        ("time_second_bias", 1),
        ("input_conv", K * CH),
        ("input_bias", 1),
    ]
    block_entries(entries, "down", D, False)
    entries += [
        ("down_sample", 3 * D),
        ("down_sample_bias", 1),
        ("up_sample", 4 * D),
        ("up_sample_bias", 1),
    ]
    block_entries(entries, "up", 2 * D, True)
    entries += [("head", CH), ("head_bias", 1)]
    rows = {}
    offset = 0
    for label, count in entries:
        rows[label] = (offset, count)
        offset += count
    return rows


ROWS = layout()
MATS = (
    "time_first",
    "time_second",
    "input_conv",
    "down_conv1",
    "down_time",
    "down_conv2",
    "down_sample",
    "up_sample",
    "up_conv1",
    "up_time",
    "up_conv2",
    "up_res",
)
SUMS = (
    "input_bias",
    "down_bias1",
    "down_gain1",
    "down_shift1",
    "down_bias2",
    "down_gain2",
    "down_shift2",
    "down_sample_bias",
    "up_sample_bias",
    "up_bias1",
    "up_gain1",
    "up_shift1",
    "up_bias2",
    "up_gain2",
    "up_shift2",
    "up_res_bias",
)
NORMS = ("down1", "down2", "up1", "up2")


def up_to(value, step):
    return -(-value // step) * step


def mm(left, right):
    return jnp.dot(left, right, preferred_element_type=F32)


def mm_nt(left, right):
    return lax.dot_general(left, right, (((1,), (1,)), ((), ())), preferred_element_type=F32)


def mm_tn(left, right):
    return lax.dot_general(left, right, (((0,), (0,)), ((), ())), preferred_element_type=F32)


def mish_pair(v):
    c = jnp.minimum(v, 20.0)
    e = jnp.exp(c)
    n = e * (e + 2.0)
    r = 1.0 / (n + 2.0)
    t = n * r
    return v * t, t + (4.0 * c) * (e * (1.0 + e)) * (r * r)


def fold(values):
    rows, cols = values.shape
    return jnp.sum(values.reshape(rows // 8, 8, cols), axis=0)


def pad_get(pad, start, size, stride=1):
    where = pl.ds(start, size, stride=stride) if stride > 1 else pl.ds(start, size)
    return jnp.concatenate([pad[0, where, :], pad[1, where, :]], axis=1)


def pad_set(pad, start, value, stride=1):
    size = value.shape[0]
    where = pl.ds(start, size, stride=stride) if stride > 1 else pl.ds(start, size)
    pad[0, where, :] = value[:, : D // 2]
    pad[1, where, :] = value[:, D // 2 :]


def group_sums(parts, ones):
    stacked = []
    for part in parts:
        high = part.astype(BF16).astype(F32)
        rest = part - high
        mid = rest.astype(BF16).astype(F32)
        stacked += [high, mid, rest - mid, jnp.zeros_like(part)]
    summed = mm(jnp.concatenate(stacked, axis=0).astype(BF16), ones)
    return [jnp.sum(summed[32 * i : 32 * i + 32], axis=0, keepdims=True) for i in range(len(parts))]


def make_kernel(n, shard_rows, pads, horizons, length):
    half = length // 2
    count_inv = 1.0 / (length * (D // GROUPS))
    blocks = n // 2
    total_rows = n * shard_rows
    pad_rows = sum(pads)
    rows_all = horizons * length
    halves_all = horizons * half
    chunks = [slice(i, i + CHUNK) for i in range(0, length, CHUNK)]

    def kernel(
        tab_a, tab_b, lens, xin, noise, emb,
        a0, a1, b0, b1,
        ga0, ga1, gb0, gb1, loss_out,
        stage, flat, ones, padA, padS, padR, padY, cols, cbuf, dbuf, rbuf,
        entry, topb, dy1, dy2, dy4, dyc, dent, xt,
        x_d1, x_d2, x_e, x_o, x_y, x_j, x_u2,
        xhat, mp, dskip, rstds, temb_d, temb_u, dtemb_d, dtemb_u, headT, dheadT, sums, hsum,
        w_tf, w_ts, w_in, w_d1, w_dt, w_d2, w_ds, w_us, w_u1, w_ut, w_u2, w_res,
        t_d1, t_d2, t_ds, t_us, t_u1, t_u2,
        sem,
    ):
        w = dict(zip(MATS, (w_tf, w_ts, w_in, w_d1, w_dt, w_d2, w_ds, w_us, w_u1, w_ut, w_u2, w_res)))

        def row(label):
            return flat[ROWS[label][0] : ROWS[label][0] + 1, :]

        def moves(refs_a, refs_b, inward):
            made = []
            for part, (refs, tab) in enumerate(((refs_a, tab_a), (refs_b, tab_b))):
                low = pads[0] * part
                for r in range(n):
                    far = refs[r // blocks].at[r % blocks]
                    near = stage.at[tab[r], pl.ds(low, pads[part]), :]
                    made.append(
                        pltpu.make_async_copy(far, near, sem) if inward else pltpu.make_async_copy(near, far, sem)
                    )
            return made

        inward = moves((a0, a1), (b0, b1), True)
        for move in inward:
            move.start()
        group_row = lax.broadcasted_iota(jnp.int32, (D, D), 0) // (D // GROUPS)
        group_col = lax.broadcasted_iota(jnp.int32, (D, D), 1) // (D // GROUPS)
        ones[...] = (group_row == group_col).astype(F32).astype(BF16)
        zero8 = jnp.zeros((8, D), F32)
        for pad, rows in ((padA, length), (padS, length), (padR, length), (padY, half)):
            pad_set(pad, 0, zero8)
            pad_set(pad, rows + 8, zero8)
        sums[...] = jnp.zeros_like(sums)
        dheadT[...] = jnp.zeros_like(dheadT)
        hsum[...] = jnp.zeros_like(hsum)
        loss_out[...] = jnp.zeros_like(loss_out)
        dtemb_d[...] = jnp.zeros_like(dtemb_d)
        dtemb_u[...] = jnp.zeros_like(dtemb_u)
        for move in inward:
            move.wait()

        for s in range(n):
            flat[s * shard_rows : s * shard_rows + pad_rows, :] = stage[s].astype(F32)
        for label in MATS:
            first, count = ROWS[label]
            count = up_to(count, 32)
            for i in range(0, count, CHUNK):
                size = min(CHUNK, count - i)
                w[label][i : i + size, :] = flat[first + i : first + i + size, :].astype(BF16)
        for source, target, taps in ((w_d1, t_d1, K), (w_d2, t_d2, K), (w_us, t_us, 4), (w_u2, t_u2, K)):
            for k in range(taps):
                target[k * D : k * D + D, :] = source[k * D : k * D + D, :].T
        for k, source in enumerate((0, 2, 1)):
            t_ds[k * D : k * D + D, :] = w_ds[source * D : source * D + D, :].T
        for k in range(K):
            for j in range(2):
                t_u1[k * D : k * D + D, j * D : j * D + D] = w_u1[(2 * k + j) * D : (2 * k + j + 1) * D, :].T
        for j in range(2):
            t_u1[K * D : K * D + D, j * D : j * D + D] = w_res[j * D : j * D + D, :].T

        first = ROWS["head"][0]
        head_rows = flat[first : first + 8, :].astype(BF16)
        at_row = lax.broadcasted_iota(jnp.int32, (D, D), 0)
        at_col = lax.broadcasted_iota(jnp.int32, (D, D), 1)
        sub_row = lax.broadcasted_iota(jnp.int32, (8, D), 0)
        sub_col = lax.broadcasted_iota(jnp.int32, (8, D), 1)
        headT[...] = jnp.zeros_like(headT)

        def picker(j):
            return ((at_col * CH + j) % D == at_row).astype(F32).astype(BF16)

        def picked(j):
            return (sub_col * CH + j) // D == sub_row

        for j in range(CH):
            spread = mm(head_rows, picker(j))
            headT[j : j + 1, :] = jnp.sum(jnp.where(picked(j), spread, 0.0), axis=0, keepdims=True)
        head_b = headT[...].astype(BF16)
        head_bias = row("head_bias")[:, :HEAD]
        head_bias = jnp.where(lax.broadcasted_iota(jnp.int32, (1, HEAD), 1) < CH, head_bias, 0.0)

        emb_b = emb[...]
        z1 = mm(emb_b, w_tf[...]) + row("time_first_bias")
        t1, slope1 = mish_pair(z1)
        t1 = t1.astype(BF16)
        z2 = mm(t1, w_ts[...]) + row("time_second_bias")
        t2, slope2 = mish_pair(z2)
        timing = t2.astype(BF16)
        temb_d[...] = mm(timing, w_dt[...]) + row("down_time_bias")
        temb_u[...] = mm(timing, w_ut[...]) + row("up_time_bias")

        def add_sum(label, value):
            i = SUMS.index(label)
            sums[i] = sums[i] + value

        def shifted(target, base, step, size, sign):
            for k in range(K):
                start = 8 + sign * (k - K // 2)
                for c in range(0, length, CHUNK):
                    target[pl.ds(base + c, CHUNK), step * k : step * k + D] = pad_get(padA, start + c, CHUNK).astype(BF16)

        def norm_forward(which, index, h, gain, shift, write):
            total = zero8
            for c in chunks:
                total = total + fold(cbuf[c, :])
            (mean,) = group_sums([total], ones[...])
            mean = mean * count_inv
            total = zero8
            for c in chunks:
                off = cbuf[c, :] - mean
                total = total + fold(off * off)
            (var,) = group_sums([total], ones[...])
            rstd = lax.rsqrt(var * count_inv + 1e-05)
            rstds[index, pl.ds(h, 1), :] = rstd
            for c in chunks:
                xh = (cbuf[c, :] - mean) * rstd
                value, slope = mish_pair(xh * gain + shift)
                xhat[which, c, :] = xh
                mp[which, c, :] = slope
                write(c, value)

        def norm_backward(which, index, h, prefix, number):
            gain = row(prefix + "_gain" + number)
            one = zero8
            two = zero8
            for c in chunks:
                dv = dbuf[c, :] * mp[which, c, :]
                one = one + fold(dv)
                two = two + fold(dv * xhat[which, c, :])
                dbuf[c, :] = dv
            add_sum(prefix + "_shift" + number, one)
            add_sum(prefix + "_gain" + number, two)
            mean1, mean2 = group_sums([one * gain, two * gain], ones[...])
            rstd = rstds[index, pl.ds(h, 1), :]
            scale = rstd * gain
            mean1 = rstd * (mean1 * count_inv)
            mean2 = rstd * (mean2 * count_inv)
            total = zero8
            for c in chunks:
                dc = dbuf[c, :] * scale - mean1 - xhat[which, c, :] * mean2
                pad_set(padA, c.start + 8, dc)
                total = total + fold(dc)
            add_sum(prefix + "_bias" + number, total)

        def rounded_to_dbuf(value):
            dbuf[...] = value.astype(BF16).astype(F32)

        def column_sum():
            total = zero8
            for c in chunks:
                total = total + fold(dbuf[c, :])
            return total

        @pl.loop(0, horizons)
        def _(h):
            base = pl.multiple_of(h * length, CHUNK)
            base2 = pl.multiple_of(h * half, CHUNK)
            rows = pl.ds(base, length)
            rows2 = pl.ds(base2, half)
            entry[...] = mm(xin[h], w_in[...]) + row("input_bias")
            for c in chunks:
                value = entry[c, :]
                pad_set(padA, c.start + 8, value)
                x_d1[pl.ds(base + c.start, CHUNK), :] = value.astype(BF16)
            shifted(cols, 0, D, K * D, 1)
            cbuf[...] = mm(cols[:, : K * D], w_d1[...]) + row("down_bias1")
            time_row = temb_d[pl.ds(h, 1), :]

            def write_d1(c, value):
                value = value + time_row
                pad_set(padA, c.start + 8, value)
                x_d2[pl.ds(base + c.start, CHUNK), :] = value.astype(BF16)

            norm_forward(2 + 2 * h, 0, h, row("down_gain1"), row("down_shift1"), write_d1)
            shifted(cols, 0, D, K * D, 1)
            cbuf[...] = mm(cols[:, : K * D], w_d2[...]) + row("down_bias2")

            def write_d2(c, value):
                pad_set(padS, c.start + 8, value + entry[c, :])

            norm_forward(3 + 2 * h, 1, h, row("down_gain2"), row("down_shift2"), write_d2)
            odd_before = pad_get(padS, 7, half, 2).astype(BF16)
            even = pad_get(padS, 8, half, 2).astype(BF16)
            odd = pad_get(padS, 9, half, 2).astype(BF16)
            x_e[rows2, :] = even
            x_o[rows2, :] = odd
            coarse = mm(jnp.concatenate([odd_before, even, odd], axis=1), w_ds[...]) + row("down_sample_bias")
            pad_set(padY, 8, coarse)
            now = coarse.astype(BF16)
            x_y[rows2, :] = now
            before = pad_get(padY, 7, half).astype(BF16)
            after = pad_get(padY, 9, half).astype(BF16)
            up_bias = row("up_sample_bias")
            pad_set(padR, 8, mm(now, w_us[D : 2 * D, :]) + mm(before, w_us[3 * D : 4 * D, :]) + up_bias, 2)
            pad_set(padR, 9, mm(after, w_us[0:D, :]) + mm(now, w_us[2 * D : 3 * D, :]) + up_bias, 2)
            for k in range(K):
                start = 8 + k - K // 2
                for c in chunks:
                    cols[c, 2 * k * D : 2 * k * D + D] = pad_get(padR, start + c.start, CHUNK).astype(BF16)
                    cols[c, 2 * k * D + D : 2 * k * D + 2 * D] = pad_get(padS, start + c.start, CHUNK).astype(BF16)
            middle = 2 * (K // 2) * D
            x_j[rows, :] = cols[:, middle : middle + 2 * D]
            rbuf[...] = mm(cols[:, middle : middle + 2 * D], w_res[...]) + row("up_res_bias")
            cbuf[...] = mm(cols[...], w_u1[...]) + row("up_bias1")
            time_up = temb_u[pl.ds(h, 1), :]

            def write_u1(c, value):
                value = value + time_up
                pad_set(padA, c.start + 8, value)
                x_u2[pl.ds(base + c.start, CHUNK), :] = value.astype(BF16)

            norm_forward(0, 2, h, row("up_gain1"), row("up_shift1"), write_u1)
            shifted(cols, 0, D, K * D, 1)
            cbuf[...] = mm(cols[:, : K * D], w_u2[...]) + row("up_bias2")

            def write_u2(c, value):
                topb[c, :] = (value + rbuf[c, :]).astype(BF16)

            norm_forward(1, 3, h, row("up_gain2"), row("up_shift2"), write_u2)
            prediction = mm_nt(topb[...], head_b) + head_bias
            frame = lax.broadcasted_iota(jnp.int32, (length, HEAD), 0)
            error = jnp.where(frame < lens[h], prediction - noise[h], 0.0)
            loss_out[...] = loss_out[...] + fold(error * error)
            error = 2.0 * error
            hsum[...] = hsum[...] + fold(error)
            error = error.astype(BF16)
            dheadT[...] = dheadT[...] + mm_tn(error, topb[...])
            dtop = mm(error, head_b).astype(BF16)
            dy1[rows, K * D : (K + 1) * D] = dtop
            dbuf[...] = dtop.astype(F32)
            add_sum("up_res_bias", column_sum())
            norm_backward(1, 3, h, "up", "2")
            shifted(dy2, base, D, K * D, -1)
            rounded_to_dbuf(mm(dy2[rows, :], t_u2[...]))
            dtemb_u[pl.ds(h, 1), :] = jnp.sum(column_sum(), axis=0, keepdims=True)
            norm_backward(0, 2, h, "up", "1")
            shifted(dy1, base, D, K * D, -1)
            dbuf[...] = mm(dy1[rows, :], t_u1[:, D:]).astype(BF16).astype(F32)
            pad_set(padR, 8, mm(dy1[rows, :], t_u1[:, :D]).astype(BF16).astype(F32))
            total = zero8
            for c in chunks:
                total = total + fold(pad_get(padR, c.start + 8, CHUNK))
            add_sum("up_sample_bias", total)
            dy4[rows2, 0:D] = pad_get(padR, 7, half, 2).astype(BF16)
            dy4[rows2, D : 2 * D] = pad_get(padR, 8, half, 2).astype(BF16)
            dy4[rows2, 2 * D : 3 * D] = pad_get(padR, 9, half, 2).astype(BF16)
            dy4[rows2, 3 * D : 4 * D] = pad_get(padR, 10, half, 2).astype(BF16)
            dcoarse = mm(dy4[rows2, :], t_us[...]).astype(BF16)
            dcoarse32 = dcoarse.astype(F32)
            pad_set(padY, 8, dcoarse32)
            add_sum("down_sample_bias", fold(dcoarse32))
            dyc[rows2, 0:D] = pad_get(padY, 9, half).astype(BF16)
            dyc[rows2, D : 2 * D] = dcoarse
            dodd = mm(dyc[rows2, :], t_ds[0 : 2 * D, :]).astype(BF16).astype(F32)
            deven = mm(dcoarse, t_ds[2 * D : 3 * D, :]).astype(BF16).astype(F32)
            pad_set(padA, 8, deven, 2)
            pad_set(padA, 9, dodd, 2)
            for c in chunks:
                dskip[h, c, :] = dbuf[c, :] + pad_get(padA, c.start + 8, CHUNK)

        def put(label, offset, value):
            first = ROWS[label][0] + offset
            flat[first : first + value.shape[0], :] = value

        def weight_grads(source, width, rows, dy, targets):
            for j in range(width // D):
                xt[j * D : j * D + D, 0:rows] = source[:, j * D : j * D + D].T
            for label, offset, block in targets:
                put(label, offset, mm(xt[0:width, 0:rows], dy[:, block * D : block * D + D]))

        weight_grads(
            x_j, 2 * D, rows_all, dy1, [("up_conv1", 2 * k * D, k) for k in range(K)] + [("up_res", 0, K)]
        )
        weight_grads(x_u2, D, rows_all, dy2, [("up_conv2", k * D, k) for k in range(K)])
        weight_grads(x_y, D, halves_all, dy4, [("up_sample", k * D, k) for k in range(4)])
        weight_grads(x_o, D, halves_all, dyc, [("down_sample", 0, 0), ("down_sample", 2 * D, 1)])
        weight_grads(x_e, D, halves_all, dyc, [("down_sample", D, 1)])

        @pl.loop(0, horizons)
        def _(h):
            base = pl.multiple_of(h * length, CHUNK)
            rows = pl.ds(base, length)
            dbuf[...] = dskip[h]
            norm_backward(3 + 2 * h, 1, h, "down", "2")
            shifted(dy2, base, D, K * D, -1)
            rounded_to_dbuf(mm(dy2[rows, :], t_d2[...]))
            dtemb_d[pl.ds(h, 1), :] = jnp.sum(column_sum(), axis=0, keepdims=True)
            norm_backward(2 + 2 * h, 0, h, "down", "1")
            shifted(dy1, base, D, K * D, -1)
            rounded_to_dbuf(mm(dy1[rows, : K * D], t_d1[...]))
            total = zero8
            for c in chunks:
                value = dbuf[c, :] + dskip[h, c, :]
                total = total + fold(value)
                dent[pl.ds(base + c.start, CHUNK), :] = value.astype(BF16)
            add_sum("input_bias", total)

        weight_grads(x_d2, D, rows_all, dy2, [("down_conv2", k * D, k) for k in range(K)])
        weight_grads(x_d1, D, rows_all, dy1, [("down_conv1", k * D, k) for k in range(K)])
        inputs = zero8
        for h in range(horizons):
            part = mm_tn(xin[h], dent[h * length : h * length + length, :])
            inputs = part if h == 0 else inputs + part
        put("input_conv", 0, inputs[: K * CH])

        down_b = dtemb_d[...].astype(BF16)
        up_b = dtemb_u[...].astype(BF16)
        put("down_time", 0, mm_tn(timing, down_b))
        put("up_time", 0, mm_tn(timing, up_b))
        dtiming = (mm_nt(down_b, w_dt[...]) + mm_nt(up_b, w_ut[...])).astype(BF16).astype(F32)
        dz2 = dtiming * slope2
        dz2_b = dz2.astype(BF16)
        put("time_second", 0, mm_tn(t1, dz2_b))
        dz1 = mm_nt(dz2_b, w_ts[...]).astype(BF16).astype(F32) * slope1
        put("time_first", 0, mm_tn(emb_b, dz1.astype(BF16)))
        for label, value in (
            ("time_first_bias", dz1),
            ("time_second_bias", dz2),
            ("down_time_bias", dtemb_d[...]),
            ("up_time_bias", dtemb_u[...]),
        ):
            put(label, 0, jnp.sum(value, axis=0, keepdims=True))
        for i, label in enumerate(SUMS):
            put(label, 0, jnp.sum(sums[i], axis=0, keepdims=True))

        tail = ROWS["head"][0]
        flat[tail : total_rows + 16, :] = jnp.zeros((total_rows + 16 - tail, D), F32)
        packed = jnp.zeros((8, D), F32)
        for j in range(CH):
            spread = jnp.where(picked(j), jnp.broadcast_to(dheadT[j : j + 1, :], (8, D)), 0.0)
            packed = packed + mm_nt(spread.astype(BF16), picker(j))
        put("head", 0, packed[:CH])
        first = ROWS["head_bias"][0]
        flat[first : first + 1, 0:HEAD] = jnp.sum(hsum[...], axis=0, keepdims=True)

        for s in range(n):
            stage[s] = flat[s * shard_rows : s * shard_rows + pad_rows, :].astype(BF16)
        outward = moves((ga0, ga1), (gb0, gb1), False)
        for move in outward:
            move.start()
        for move in outward:
            move.wait()

    vm = pltpu.VMEM
    scratch = [
        vm((n, pad_rows, D), BF16),
        vm((total_rows + pad_rows, D), F32),
        vm((D, D), BF16),
        vm((2, length + 16, D // 2), F32),
        vm((2, length + 16, D // 2), F32),
        vm((2, length + 16, D // 2), F32),
        vm((2, half + 16, D // 2), F32),
        vm((length, 2 * K * D), BF16),
        vm((length, D), F32),
        vm((length, D), F32),
        vm((length, D), F32),
        vm((length, D), F32),
        vm((length, D), BF16),
        vm((rows_all, (K + 1) * D), BF16),
        vm((rows_all, K * D), BF16),
        vm((halves_all, 4 * D), BF16),
        vm((halves_all, 2 * D), BF16),
        vm((rows_all, D), BF16),
        vm((2 * D, rows_all), BF16),
        vm((rows_all, D), BF16),
        vm((rows_all, D), BF16),
        vm((halves_all, D), BF16),
        vm((halves_all, D), BF16),
        vm((halves_all, D), BF16),
        vm((rows_all, 2 * D), BF16),
        vm((rows_all, D), BF16),
        vm((2 + 2 * horizons, length, D), F32),
        vm((2 + 2 * horizons, length, D), F32),
        vm((horizons, length, D), F32),
        vm((len(NORMS), 8, D), F32),
        vm((16, D), F32),
        vm((16, D), F32),
        vm((16, D), F32),
        vm((16, D), F32),
        vm((HEAD, D), F32),
        vm((HEAD, D), F32),
        vm((len(SUMS), 8, D), F32),
        vm((8, HEAD), F32),
    ]
    scratch += [vm((up_to(ROWS[label][1], 32), D), BF16) for label in MATS]
    scratch += [
        vm((K * D, D), BF16),
        vm((K * D, D), BF16),
        vm((3 * D, D), BF16),
        vm((4 * D, D), BF16),
        vm(((K + 1) * D, 2 * D), BF16),
        vm((K * D, D), BF16),
        pltpu.SemaphoreType.DMA,
    ]
    shapes = [
        jax.ShapeDtypeStruct((blocks, rows, D), BF16) for rows in (pads[0], pads[0], pads[1], pads[1])
    ] + [jax.ShapeDtypeStruct((8, HEAD), F32)]
    smem = pl.BlockSpec(memory_space=pltpu.SMEM)
    local = pl.BlockSpec(memory_space=pltpu.VMEM)
    remote = pl.BlockSpec(memory_space=pl.ANY)
    flops = 6 * 2100000 * rows_all
    return pl.pallas_call(
        kernel,
        out_shape=shapes,
        in_specs=[smem] * 3 + [local] * 3 + [remote] * 4,
        out_specs=[remote] * 4 + [local],
        scratch_shapes=scratch,
        compiler_params=pltpu.CompilerParams(vmem_limit_bytes=63 * 1024 * 1024),
        cost_estimate=pl.CostEstimate(flops=flops, bytes_accessed=10000000, transcendentals=3000000),
        name="train_step",
    )


def device_dims(n):
    known = {32: (4, 2, 2), 256: (4, 8, 4)}
    return known.get(n, (n // 2, 1, 1))


class Ring:
    def __init__(self, n):
        self.n = n
        self.dims = device_dims(n) + (2,)
        strides = [1]
        for size in self.dims[:0:-1]:
            strides.insert(0, strides[0] * size)
        self.strides = strides

    def moved(self, index, axis, step):
        at = index // self.strides[axis] % self.dims[axis]
        return index + ((at + step) % self.dims[axis] - at) * self.strides[axis]

    def send(self, values, axis, step):
        return lax.ppermute(values, "batch", [(i, self.moved(i, axis, step)) for i in range(self.n)])

    def table(self, me, order):
        result = jnp.zeros((1,), jnp.int32) + me
        for axis in order:
            result = jnp.stack([self.moved(result, axis, step) for step in range(self.dims[axis])], axis=1).reshape(-1)
        return result

    def gather(self, own, order):
        blocks = own[None]
        for axis in order[:0:-1]:
            size = self.dims[axis]
            arrived = [blocks] + [self.send(blocks, axis, size - step) for step in range(1, size)]
            blocks = jnp.concatenate(arrived, axis=0) if size > 1 else blocks
        axis = order[0]
        return blocks, self.send(blocks, axis, 1)

    def scatter(self, keep, away, order):
        terms = [keep, self.send(away, order[0], 1)]
        for axis in order[1:]:
            size = self.dims[axis]
            if size == 1:
                continue
            cut = [term.reshape((size, term.shape[0] // size) + term.shape[1:]) for term in terms]
            arrived = []
            for step in range(1, size):
                part = sum(term[step].astype(F32) for term in cut).astype(BF16)
                arrived.append(self.send(part, axis, step))
            terms = [term[0] for term in cut] + arrived
        return sum(term[0].astype(F32) for term in terms)

    def total(self, values):
        for axis in (3, 2, 1, 0):
            size = self.dims[axis]
            if size == 4:
                one, two, three = (self.send(values, axis, step) for step in (1, 2, 3))
                values = (values + two) + (one + three)
                continue
            while size > 1:
                size //= 2
                values = values + self.send(values, axis, size)
        return values


def prepare(trajectories, noise_draw, timesteps, lengths):
    horizons = trajectories.shape[0] * trajectories.shape[1]
    length = trajectories.shape[2]
    trajectory = trajectories.reshape(horizons, length, CH)
    noise_part = noise_draw.reshape(horizons, length, CH)
    lens = lengths.reshape(horizons)
    frames = jnp.arange(length, dtype=jnp.int32)
    valid = (frames[None, :] < lens[:, None]).astype(F32)
    times = timesteps.reshape(horizons).astype(F32)
    angle_now = ((times + 1.0) / DIFF + 0.008) / 1.008 * (math.pi / 2)
    angle_zero = 0.008 / 1.008 * (math.pi / 2)
    share = jnp.cos(angle_now) ** 2 / math.cos(angle_zero) ** 2
    noisy = (
        jnp.sqrt(share)[:, None, None] * trajectory + jnp.sqrt(1.0 - share)[:, None, None] * noise_part
    ) * valid[:, :, None]
    padded = jnp.pad(noisy.astype(BF16), ((0, 0), (K // 2, K // 2), (0, 0)))
    taps = [padded[:, k : k + length] for k in range(K)]
    taps.append(jnp.zeros((horizons, length, 32 - K * CH), BF16))
    xin = jnp.concatenate(taps, axis=2)
    half_width = TE // 2
    frequency = jnp.exp(-math.log(10000.0) * jnp.arange(half_width, dtype=F32) / (half_width - 1))
    angles = times[:, None] * frequency[None, :]
    embedding = jnp.concatenate([jnp.sin(angles), jnp.cos(angles)], axis=1).astype(BF16)
    embedding = jnp.pad(embedding, ((0, 16 - horizons), (0, 0)))
    noise8 = jnp.pad(noise_part, ((0, 0), (0, 0), (0, HEAD - CH)))
    return lens, xin, noise8, embedding


def solution(mesh):
    n = mesh.shape["batch"]

    def shards(params, moment1, moment2, ema_params, trajectories, noise_draw, timesteps, lengths):
        me = lax.axis_index("batch")
        ring = Ring(n)
        shard_rows = params.shape[0] // D
        pad_rows = up_to(shard_rows, 32)
        if pad_rows - shard_rows >= 16:
            pad_rows -= 16
        low_rows = up_to(pad_rows // 2, 16)
        pads = (low_rows, pad_rows - low_rows)
        order_a = (3, 2, 1, 0)
        order_b = (3, 1, 2, 0)
        low_copy = jnp.pad(params.astype(BF16).reshape(shard_rows, D), ((0, pad_rows - shard_rows), (0, 0)))
        a0, a1 = ring.gather(low_copy[:low_rows], order_a)
        b0, b1 = ring.gather(low_copy[low_rows:], order_b)
        lens, xin, noise8, embedding = prepare(trajectories, noise_draw, timesteps, lengths)
        horizons, length = noise8.shape[:2]
        call = make_kernel(n, shard_rows, pads, horizons, length)
        ga0, ga1, gb0, gb1, loss_parts = call(
            ring.table(me, order_a), ring.table(me, order_b), lens, xin, noise8, embedding, a0, a1, b0, b1
        )
        summed = jnp.concatenate([ring.scatter(ga0, ga1, order_a), ring.scatter(gb0, gb1, order_b)], axis=0)
        summed = summed[:shard_rows].reshape(-1)
        local_count = jnp.sum(lengths).astype(F32) * CH
        lane = jnp.arange(128)[None, :]
        loss_count = jnp.where(lane == 0, jnp.sum(loss_parts), jnp.where(lane == 1, local_count, 0.0))
        loss_count = ring.total(jnp.broadcast_to(loss_count, (8, 128)))
        loss_sum = loss_count[0, 0]
        frame_count = loss_count[0, 1]
        squares = ring.total(jnp.broadcast_to(jnp.sum(summed * summed), (8, 128)))[0, 0]
        grad_norm = jnp.sqrt(squares) / frame_count
        clipped = summed / frame_count * jnp.minimum(1.0, clip_limit / (grad_norm + 1e-06))
        new_moment1 = 0.9 * moment1 + 0.1 * clipped
        new_moment2 = 0.95 * moment2 + 0.05 * clipped * clipped
        first_hat = new_moment1 / (1.0 - 0.9**STEP)
        second_hat = new_moment2 / (1.0 - 0.95**STEP)
        new_params = params - 0.01 * (first_hat / (jnp.sqrt(second_hat) + 1e-08) + 0.01 * params)
        new_ema = 0.8 * ema_params + 0.2 * new_params
        return (
            new_params,
            new_moment1,
            new_moment2,
            new_ema,
            new_params.astype(BF16),
            grad_norm,
            loss_sum,
            frame_count,
        )

    flat = P("batch")
    wide = P(None, "batch", None, None)
    narrow = P(None, "batch")
    return jax.shard_map(
        shards,
        mesh=mesh,
        in_specs=(flat, flat, flat, flat, wide, wide, narrow, narrow),
        out_specs=(flat, flat, flat, flat, flat, P(), P(), P()),
        check_vma=False,
    )
```

```python
import math

import jax
import jax.numpy as jnp
from jax import lax
from jax.experimental import pallas as pl
from jax.experimental.pallas import tpu as pltpu
from jax.sharding import PartitionSpec as P

D = 256
TE = 128
CH = 6
GROUPS = 8
K = 5
DIFF = 256
STEP = 10

CHUNK = 64
HEAD = 8
clip_limit = 0.05

F32 = jnp.float32
BF16 = jnp.bfloat16


TIME_FIRST, TIME_FIRST_BIAS, TIME_SECOND, TIME_SECOND_BIAS, INPUT_CONV, INPUT_BIAS = range(6)
DOWN = 6
DOWN_SAMPLE, DOWN_SAMPLE_BIAS, UP_SAMPLE, UP_SAMPLE_BIAS = range(16, 20)
UP = 20
UP_RES, UP_RES_BIAS, HEAD_MAT, HEAD_BIAS = range(30, 34)
CONV1, BIAS1, GAIN1, SHIFT1, TIME, TIME_BIAS, CONV2, BIAS2, GAIN2, SHIFT2 = range(10)


def layout():
    counts = [TE, 1, D, 1, K * CH, 1]
    counts += [K * D, 1, 1, 1, D, 1, K * D, 1, 1, 1]
    counts += [3 * D, 1, 4 * D, 1]
    counts += [2 * K * D, 1, 1, 1, D, 1, K * D, 1, 1, 1, 2 * D, 1]
    counts += [CH, 1]
    return [(sum(counts[:i]), count) for i, count in enumerate(counts)]


ROWS = layout()
MATS = (
    TIME_FIRST,
    TIME_SECOND,
    INPUT_CONV,
    DOWN + CONV1,
    DOWN + TIME,
    DOWN + CONV2,
    DOWN_SAMPLE,
    UP_SAMPLE,
    UP + CONV1,
    UP + TIME,
    UP + CONV2,
    UP_RES,
)
SUMS = (INPUT_BIAS, DOWN_SAMPLE_BIAS, UP_SAMPLE_BIAS, UP_RES_BIAS) + tuple(
    block + piece for block in (DOWN, UP) for piece in (BIAS1, GAIN1, SHIFT1, BIAS2, GAIN2, SHIFT2)
)
NORMS = 4


def up_to(value, step):
    return -(-value // step) * step


def mm(left, right):
    return jnp.dot(left, right, preferred_element_type=F32)


def mm_nt(left, right):
    return lax.dot_general(left, right, (((1,), (1,)), ((), ())), preferred_element_type=F32)


def mm_tn(left, right):
    return lax.dot_general(left, right, (((0,), (0,)), ((), ())), preferred_element_type=F32)


def mish_pair(v):
    c = jnp.minimum(v, 20.0)
    e = jnp.exp(c)
    n = e * (e + 2.0)
    r = 1.0 / (n + 2.0)
    t = n * r
    return v * t, t + (4.0 * c) * (e * (1.0 + e)) * (r * r)


def fold(values):
    rows, cols = values.shape
    return jnp.sum(values.reshape(rows // 8, 8, cols), axis=0)


def pad_get(pad, start, size, stride=1):
    where = pl.ds(start, size, stride=stride) if stride > 1 else pl.ds(start, size)
    return jnp.concatenate([pad[0, where, :], pad[1, where, :]], axis=1)


def pad_set(pad, start, value, stride=1):
    size = value.shape[0]
    where = pl.ds(start, size, stride=stride) if stride > 1 else pl.ds(start, size)
    pad[0, where, :] = value[:, : D // 2]
    pad[1, where, :] = value[:, D // 2 :]


def group_sums(parts, ones):
    stacked = []
    for part in parts:
        high = part.astype(BF16).astype(F32)
        rest = part - high
        mid = rest.astype(BF16).astype(F32)
        stacked += [high, mid, rest - mid, jnp.zeros_like(part)]
    summed = mm(jnp.concatenate(stacked, axis=0).astype(BF16), ones)
    return [jnp.sum(summed[32 * i : 32 * i + 32], axis=0, keepdims=True) for i in range(len(parts))]


def make_kernel(n, shard_rows, pads, horizons, length):
    half = length // 2
    count_inv = 1.0 / (length * (D // GROUPS))
    blocks = n // 2
    total_rows = n * shard_rows
    pad_rows = sum(pads)
    rows_all = horizons * length
    halves_all = horizons * half
    chunks = [slice(i, i + CHUNK) for i in range(0, length, CHUNK)]

    def kernel(
        tab_a, tab_b, lens, xin, noise, emb,
        a0, a1, b0, b1,
        ga0, ga1, gb0, gb1, loss_out,
        stage, flat, ones, padA, padS, padR, padY, cols, cbuf, dbuf, rbuf,
        entry, topb, dy1, dy2, dy4, dyc, dent, xt,
        x_d1, x_d2, x_e, x_o, x_y, x_j, x_u2,
        xhat, mp, dskip, rstds, temb_d, temb_u, dtemb_d, dtemb_u, headT, dheadT, sums, hsum,
        w_tf, w_ts, w_in, w_d1, w_dt, w_d2, w_ds, w_us, w_u1, w_ut, w_u2, w_res,
        t_d1, t_d2, t_ds, t_us, t_u1, t_u2,
        sem,
    ):
        w = dict(zip(MATS, (w_tf, w_ts, w_in, w_d1, w_dt, w_d2, w_ds, w_us, w_u1, w_ut, w_u2, w_res)))

        def row(label):
            return flat[ROWS[label][0] : ROWS[label][0] + 1, :]

        def moves(refs_a, refs_b, inward):
            made = []
            for part, (refs, tab) in enumerate(((refs_a, tab_a), (refs_b, tab_b))):
                low = pads[0] * part
                for r in range(n):
                    far = refs[r // blocks].at[r % blocks]
                    near = stage.at[tab[r], pl.ds(low, pads[part]), :]
                    made.append(
                        pltpu.make_async_copy(far, near, sem) if inward else pltpu.make_async_copy(near, far, sem)
                    )
            return made

        inward = moves((a0, a1), (b0, b1), True)
        for move in inward:
            move.start()
        group_row = lax.broadcasted_iota(jnp.int32, (D, D), 0) // (D // GROUPS)
        group_col = lax.broadcasted_iota(jnp.int32, (D, D), 1) // (D // GROUPS)
        ones[...] = (group_row == group_col).astype(F32).astype(BF16)
        zero8 = jnp.zeros((8, D), F32)
        for pad, rows in ((padA, length), (padS, length), (padR, length), (padY, half)):
            pad_set(pad, 0, zero8)
            pad_set(pad, rows + 8, zero8)
        sums[...] = jnp.zeros_like(sums)
        dheadT[...] = jnp.zeros_like(dheadT)
        hsum[...] = jnp.zeros_like(hsum)
        loss_out[...] = jnp.zeros_like(loss_out)
        dtemb_d[...] = jnp.zeros_like(dtemb_d)
        dtemb_u[...] = jnp.zeros_like(dtemb_u)
        for move in inward:
            move.wait()

        for s in range(n):
            flat[s * shard_rows : s * shard_rows + pad_rows, :] = stage[s].astype(F32)
        for label in MATS:
            first, count = ROWS[label]
            count = up_to(count, 32)
            for i in range(0, count, CHUNK):
                size = min(CHUNK, count - i)
                w[label][i : i + size, :] = flat[first + i : first + i + size, :].astype(BF16)
        for source, target, taps in ((w_d1, t_d1, K), (w_d2, t_d2, K), (w_us, t_us, 4), (w_u2, t_u2, K)):
            for k in range(taps):
                target[k * D : k * D + D, :] = source[k * D : k * D + D, :].T
        for k, source in enumerate((0, 2, 1)):
            t_ds[k * D : k * D + D, :] = w_ds[source * D : source * D + D, :].T
        for k in range(K):
            for j in range(2):
                t_u1[k * D : k * D + D, j * D : j * D + D] = w_u1[(2 * k + j) * D : (2 * k + j + 1) * D, :].T
        for j in range(2):
            t_u1[K * D : K * D + D, j * D : j * D + D] = w_res[j * D : j * D + D, :].T

        first = ROWS[HEAD_MAT][0]
        head_rows = flat[first : first + 8, :].astype(BF16)
        at_row = lax.broadcasted_iota(jnp.int32, (D, D), 0)
        at_col = lax.broadcasted_iota(jnp.int32, (D, D), 1)
        sub_row = lax.broadcasted_iota(jnp.int32, (8, D), 0)
        sub_col = lax.broadcasted_iota(jnp.int32, (8, D), 1)
        headT[...] = jnp.zeros_like(headT)

        def picker(j):
            return ((at_col * CH + j) % D == at_row).astype(F32).astype(BF16)

        def picked(j):
            return (sub_col * CH + j) // D == sub_row

        for j in range(CH):
            spread = mm(head_rows, picker(j))
            headT[j : j + 1, :] = jnp.sum(jnp.where(picked(j), spread, 0.0), axis=0, keepdims=True)
        head_b = headT[...].astype(BF16)
        head_bias = row(HEAD_BIAS)[:, :HEAD]
        head_bias = jnp.where(lax.broadcasted_iota(jnp.int32, (1, HEAD), 1) < CH, head_bias, 0.0)

        emb_b = emb[...]
        z1 = mm(emb_b, w_tf[...]) + row(TIME_FIRST_BIAS)
        t1, slope1 = mish_pair(z1)
        t1 = t1.astype(BF16)
        z2 = mm(t1, w_ts[...]) + row(TIME_SECOND_BIAS)
        t2, slope2 = mish_pair(z2)
        timing = t2.astype(BF16)
        temb_d[...] = mm(timing, w_dt[...]) + row(DOWN + TIME_BIAS)
        temb_u[...] = mm(timing, w_ut[...]) + row(UP + TIME_BIAS)

        def add_sum(label, value):
            i = SUMS.index(label)
            sums[i] = sums[i] + value

        def shifted(target, base, step, size, sign):
            for k in range(K):
                start = 8 + sign * (k - K // 2)
                for c in range(0, length, CHUNK):
                    target[pl.ds(base + c, CHUNK), step * k : step * k + D] = pad_get(padA, start + c, CHUNK).astype(BF16)

        def norm_forward(which, index, h, gain, shift, write):
            total = zero8
            for c in chunks:
                total = total + fold(cbuf[c, :])
            (mean,) = group_sums([total], ones[...])
            mean = mean * count_inv
            total = zero8
            for c in chunks:
                off = cbuf[c, :] - mean
                total = total + fold(off * off)
            (var,) = group_sums([total], ones[...])
            rstd = lax.rsqrt(var * count_inv + 1e-05)
            rstds[index, pl.ds(h, 1), :] = rstd
            for c in chunks:
                xh = (cbuf[c, :] - mean) * rstd
                value, slope = mish_pair(xh * gain + shift)
                xhat[which, c, :] = xh
                mp[which, c, :] = slope
                write(c, value)

        def norm_backward(which, index, h, block, second):
            gain = row(block + GAIN1 + second)
            one = zero8
            two = zero8
            for c in chunks:
                dv = dbuf[c, :] * mp[which, c, :]
                one = one + fold(dv)
                two = two + fold(dv * xhat[which, c, :])
                dbuf[c, :] = dv
            add_sum(block + SHIFT1 + second, one)
            add_sum(block + GAIN1 + second, two)
            mean1, mean2 = group_sums([one * gain, two * gain], ones[...])
            rstd = rstds[index, pl.ds(h, 1), :]
            scale = rstd * gain
            mean1 = rstd * (mean1 * count_inv)
            mean2 = rstd * (mean2 * count_inv)
            total = zero8
            for c in chunks:
                dc = dbuf[c, :] * scale - mean1 - xhat[which, c, :] * mean2
                pad_set(padA, c.start + 8, dc)
                total = total + fold(dc)
            add_sum(block + BIAS1 + second, total)

        def rounded_to_dbuf(value):
            dbuf[...] = value.astype(BF16).astype(F32)

        def column_sum():
            total = zero8
            for c in chunks:
                total = total + fold(dbuf[c, :])
            return total

        @pl.loop(0, horizons)
        def _(h):
            base = pl.multiple_of(h * length, CHUNK)
            base2 = pl.multiple_of(h * half, CHUNK)
            rows = pl.ds(base, length)
            rows2 = pl.ds(base2, half)
            entry[...] = mm(xin[h], w_in[...]) + row(INPUT_BIAS)
            for c in chunks:
                value = entry[c, :]
                pad_set(padA, c.start + 8, value)
                x_d1[pl.ds(base + c.start, CHUNK), :] = value.astype(BF16)
            shifted(cols, 0, D, K * D, 1)
            cbuf[...] = mm(cols[:, : K * D], w_d1[...]) + row(DOWN + BIAS1)
            time_row = temb_d[pl.ds(h, 1), :]

            def write_d1(c, value):
                value = value + time_row
                pad_set(padA, c.start + 8, value)
                x_d2[pl.ds(base + c.start, CHUNK), :] = value.astype(BF16)

            norm_forward(2 + 2 * h, 0, h, row(DOWN + GAIN1), row(DOWN + SHIFT1), write_d1)
            shifted(cols, 0, D, K * D, 1)
            cbuf[...] = mm(cols[:, : K * D], w_d2[...]) + row(DOWN + BIAS2)

            def write_d2(c, value):
                pad_set(padS, c.start + 8, value + entry[c, :])

            norm_forward(3 + 2 * h, 1, h, row(DOWN + GAIN2), row(DOWN + SHIFT2), write_d2)
            odd_before = pad_get(padS, 7, half, 2).astype(BF16)
            even = pad_get(padS, 8, half, 2).astype(BF16)
            odd = pad_get(padS, 9, half, 2).astype(BF16)
            x_e[rows2, :] = even
            x_o[rows2, :] = odd
            coarse = mm(jnp.concatenate([odd_before, even, odd], axis=1), w_ds[...]) + row(DOWN_SAMPLE_BIAS)
            pad_set(padY, 8, coarse)
            now = coarse.astype(BF16)
            x_y[rows2, :] = now
            before = pad_get(padY, 7, half).astype(BF16)
            after = pad_get(padY, 9, half).astype(BF16)
            up_bias = row(UP_SAMPLE_BIAS)
            pad_set(padR, 8, mm(now, w_us[D : 2 * D, :]) + mm(before, w_us[3 * D : 4 * D, :]) + up_bias, 2)
            pad_set(padR, 9, mm(after, w_us[0:D, :]) + mm(now, w_us[2 * D : 3 * D, :]) + up_bias, 2)
            for k in range(K):
                start = 8 + k - K // 2
                for c in chunks:
                    cols[c, 2 * k * D : 2 * k * D + D] = pad_get(padR, start + c.start, CHUNK).astype(BF16)
                    cols[c, 2 * k * D + D : 2 * k * D + 2 * D] = pad_get(padS, start + c.start, CHUNK).astype(BF16)
            middle = 2 * (K // 2) * D
            x_j[rows, :] = cols[:, middle : middle + 2 * D]
            rbuf[...] = mm(cols[:, middle : middle + 2 * D], w_res[...]) + row(UP_RES_BIAS)
            cbuf[...] = mm(cols[...], w_u1[...]) + row(UP + BIAS1)
            time_up = temb_u[pl.ds(h, 1), :]

            def write_u1(c, value):
                value = value + time_up
                pad_set(padA, c.start + 8, value)
                x_u2[pl.ds(base + c.start, CHUNK), :] = value.astype(BF16)

            norm_forward(0, 2, h, row(UP + GAIN1), row(UP + SHIFT1), write_u1)
            shifted(cols, 0, D, K * D, 1)
            cbuf[...] = mm(cols[:, : K * D], w_u2[...]) + row(UP + BIAS2)

            def write_u2(c, value):
                topb[c, :] = (value + rbuf[c, :]).astype(BF16)

            norm_forward(1, 3, h, row(UP + GAIN2), row(UP + SHIFT2), write_u2)
            prediction = mm_nt(topb[...], head_b) + head_bias
            frame = lax.broadcasted_iota(jnp.int32, (length, HEAD), 0)
            error = jnp.where(frame < lens[h], prediction - noise[h], 0.0)
            loss_out[...] = loss_out[...] + fold(error * error)
            error = 2.0 * error
            hsum[...] = hsum[...] + fold(error)
            error = error.astype(BF16)
            dheadT[...] = dheadT[...] + mm_tn(error, topb[...])
            dtop = mm(error, head_b).astype(BF16)
            dy1[rows, K * D : (K + 1) * D] = dtop
            dbuf[...] = dtop.astype(F32)
            add_sum(UP_RES_BIAS, column_sum())
            norm_backward(1, 3, h, UP, CONV2)
            shifted(dy2, base, D, K * D, -1)
            rounded_to_dbuf(mm(dy2[rows, :], t_u2[...]))
            dtemb_u[pl.ds(h, 1), :] = jnp.sum(column_sum(), axis=0, keepdims=True)
            norm_backward(0, 2, h, UP, 0)
            shifted(dy1, base, D, K * D, -1)
            dbuf[...] = mm(dy1[rows, :], t_u1[:, D:]).astype(BF16).astype(F32)
            pad_set(padR, 8, mm(dy1[rows, :], t_u1[:, :D]).astype(BF16).astype(F32))
            total = zero8
            for c in chunks:
                total = total + fold(pad_get(padR, c.start + 8, CHUNK))
            add_sum(UP_SAMPLE_BIAS, total)
            dy4[rows2, 0:D] = pad_get(padR, 7, half, 2).astype(BF16)
            dy4[rows2, D : 2 * D] = pad_get(padR, 8, half, 2).astype(BF16)
            dy4[rows2, 2 * D : 3 * D] = pad_get(padR, 9, half, 2).astype(BF16)
            dy4[rows2, 3 * D : 4 * D] = pad_get(padR, 10, half, 2).astype(BF16)
            dcoarse = mm(dy4[rows2, :], t_us[...]).astype(BF16)
            dcoarse32 = dcoarse.astype(F32)
            pad_set(padY, 8, dcoarse32)
            add_sum(DOWN_SAMPLE_BIAS, fold(dcoarse32))
            dyc[rows2, 0:D] = pad_get(padY, 9, half).astype(BF16)
            dyc[rows2, D : 2 * D] = dcoarse
            dodd = mm(dyc[rows2, :], t_ds[0 : 2 * D, :]).astype(BF16).astype(F32)
            deven = mm(dcoarse, t_ds[2 * D : 3 * D, :]).astype(BF16).astype(F32)
            pad_set(padA, 8, deven, 2)
            pad_set(padA, 9, dodd, 2)
            for c in chunks:
                dskip[h, c, :] = dbuf[c, :] + pad_get(padA, c.start + 8, CHUNK)

        def put(label, offset, value):
            first = ROWS[label][0] + offset
            flat[first : first + value.shape[0], :] = value

        def weight_grads(source, width, rows, dy, targets):
            for j in range(width // D):
                xt[j * D : j * D + D, 0:rows] = source[:, j * D : j * D + D].T
            for label, offset, block in targets:
                put(label, offset, mm(xt[0:width, 0:rows], dy[:, block * D : block * D + D]))

        weight_grads(
            x_j, 2 * D, rows_all, dy1, [(UP + CONV1, 2 * k * D, k) for k in range(K)] + [(UP_RES, 0, K)]
        )
        weight_grads(x_u2, D, rows_all, dy2, [(UP + CONV2, k * D, k) for k in range(K)])
        weight_grads(x_y, D, halves_all, dy4, [(UP_SAMPLE, k * D, k) for k in range(4)])
        weight_grads(x_o, D, halves_all, dyc, [(DOWN_SAMPLE, 0, 0), (DOWN_SAMPLE, 2 * D, 1)])
        weight_grads(x_e, D, halves_all, dyc, [(DOWN_SAMPLE, D, 1)])

        @pl.loop(0, horizons)
        def _(h):
            base = pl.multiple_of(h * length, CHUNK)
            rows = pl.ds(base, length)
            dbuf[...] = dskip[h]
            norm_backward(3 + 2 * h, 1, h, DOWN, CONV2)
            shifted(dy2, base, D, K * D, -1)
            rounded_to_dbuf(mm(dy2[rows, :], t_d2[...]))
            dtemb_d[pl.ds(h, 1), :] = jnp.sum(column_sum(), axis=0, keepdims=True)
            norm_backward(2 + 2 * h, 0, h, DOWN, 0)
            shifted(dy1, base, D, K * D, -1)
            rounded_to_dbuf(mm(dy1[rows, : K * D], t_d1[...]))
            total = zero8
            for c in chunks:
                value = dbuf[c, :] + dskip[h, c, :]
                total = total + fold(value)
                dent[pl.ds(base + c.start, CHUNK), :] = value.astype(BF16)
            add_sum(INPUT_BIAS, total)

        weight_grads(x_d2, D, rows_all, dy2, [(DOWN + CONV2, k * D, k) for k in range(K)])
        weight_grads(x_d1, D, rows_all, dy1, [(DOWN + CONV1, k * D, k) for k in range(K)])
        inputs = zero8
        for h in range(horizons):
            part = mm_tn(xin[h], dent[h * length : h * length + length, :])
            inputs = part if h == 0 else inputs + part
        put(INPUT_CONV, 0, inputs[: K * CH])

        down_b = dtemb_d[...].astype(BF16)
        up_b = dtemb_u[...].astype(BF16)
        put(DOWN + TIME, 0, mm_tn(timing, down_b))
        put(UP + TIME, 0, mm_tn(timing, up_b))
        dtiming = (mm_nt(down_b, w_dt[...]) + mm_nt(up_b, w_ut[...])).astype(BF16).astype(F32)
        dz2 = dtiming * slope2
        dz2_b = dz2.astype(BF16)
        put(TIME_SECOND, 0, mm_tn(t1, dz2_b))
        dz1 = mm_nt(dz2_b, w_ts[...]).astype(BF16).astype(F32) * slope1
        put(TIME_FIRST, 0, mm_tn(emb_b, dz1.astype(BF16)))
        for label, value in (
            (TIME_FIRST_BIAS, dz1),
            (TIME_SECOND_BIAS, dz2),
            (DOWN + TIME_BIAS, dtemb_d[...]),
            (UP + TIME_BIAS, dtemb_u[...]),
        ):
            put(label, 0, jnp.sum(value, axis=0, keepdims=True))
        for i, label in enumerate(SUMS):
            put(label, 0, jnp.sum(sums[i], axis=0, keepdims=True))

        tail = ROWS[HEAD_MAT][0]
        flat[tail : total_rows + 16, :] = jnp.zeros((total_rows + 16 - tail, D), F32)
        packed = jnp.zeros((8, D), F32)
        for j in range(CH):
            spread = jnp.where(picked(j), jnp.broadcast_to(dheadT[j : j + 1, :], (8, D)), 0.0)
            packed = packed + mm_nt(spread.astype(BF16), picker(j))
        put(HEAD_MAT, 0, packed[:CH])
        first = ROWS[HEAD_BIAS][0]
        flat[first : first + 1, 0:HEAD] = jnp.sum(hsum[...], axis=0, keepdims=True)

        for s in range(n):
            stage[s] = flat[s * shard_rows : s * shard_rows + pad_rows, :].astype(BF16)
        outward = moves((ga0, ga1), (gb0, gb1), False)
        for move in outward:
            move.start()
        for move in outward:
            move.wait()

    vm = pltpu.VMEM
    scratch = [
        vm((n, pad_rows, D), BF16),
        vm((total_rows + pad_rows, D), F32),
        vm((D, D), BF16),
        vm((2, length + 16, D // 2), F32),
        vm((2, length + 16, D // 2), F32),
        vm((2, length + 16, D // 2), F32),
        vm((2, half + 16, D // 2), F32),
        vm((length, 2 * K * D), BF16),
        vm((length, D), F32),
        vm((length, D), F32),
        vm((length, D), F32),
        vm((length, D), F32),
        vm((length, D), BF16),
        vm((rows_all, (K + 1) * D), BF16),
        vm((rows_all, K * D), BF16),
        vm((halves_all, 4 * D), BF16),
        vm((halves_all, 2 * D), BF16),
        vm((rows_all, D), BF16),
        vm((2 * D, rows_all), BF16),
        vm((rows_all, D), BF16),
        vm((rows_all, D), BF16),
        vm((halves_all, D), BF16),
        vm((halves_all, D), BF16),
        vm((halves_all, D), BF16),
        vm((rows_all, 2 * D), BF16),
        vm((rows_all, D), BF16),
        vm((2 + 2 * horizons, length, D), F32),
        vm((2 + 2 * horizons, length, D), F32),
        vm((horizons, length, D), F32),
        vm((NORMS, 8, D), F32),
        vm((16, D), F32),
        vm((16, D), F32),
        vm((16, D), F32),
        vm((16, D), F32),
        vm((HEAD, D), F32),
        vm((HEAD, D), F32),
        vm((len(SUMS), 8, D), F32),
        vm((8, HEAD), F32),
    ]
    scratch += [vm((up_to(ROWS[label][1], 32), D), BF16) for label in MATS]
    scratch += [
        vm((K * D, D), BF16),
        vm((K * D, D), BF16),
        vm((3 * D, D), BF16),
        vm((4 * D, D), BF16),
        vm(((K + 1) * D, 2 * D), BF16),
        vm((K * D, D), BF16),
        pltpu.SemaphoreType.DMA,
    ]
    shapes = [
        jax.ShapeDtypeStruct((blocks, rows, D), BF16) for rows in (pads[0], pads[0], pads[1], pads[1])
    ] + [jax.ShapeDtypeStruct((8, HEAD), F32)]
    smem = pl.BlockSpec(memory_space=pltpu.SMEM)
    local = pl.BlockSpec(memory_space=pltpu.VMEM)
    remote = pl.BlockSpec(memory_space=pl.ANY)
    flops = 6 * 2100000 * rows_all
    return pl.pallas_call(
        kernel,
        out_shape=shapes,
        in_specs=[smem] * 3 + [local] * 3 + [remote] * 4,
        out_specs=[remote] * 4 + [local],
        scratch_shapes=scratch,
        compiler_params=pltpu.CompilerParams(vmem_limit_bytes=63 * 1024 * 1024),
        cost_estimate=pl.CostEstimate(flops=flops, bytes_accessed=10000000, transcendentals=3000000),
        name="step",
    )


def device_dims(n):
    known = {32: (4, 2, 2), 256: (4, 8, 4)}
    return known.get(n, (n // 2, 1, 1))


class Ring:
    def __init__(self, n):
        self.n = n
        self.dims = device_dims(n) + (2,)
        strides = [1]
        for size in self.dims[:0:-1]:
            strides.insert(0, strides[0] * size)
        self.strides = strides

    def moved(self, index, axis, step):
        at = index // self.strides[axis] % self.dims[axis]
        return index + ((at + step) % self.dims[axis] - at) * self.strides[axis]

    def send(self, values, axis, step):
        return lax.ppermute(values, "batch", [(i, self.moved(i, axis, step)) for i in range(self.n)])

    def table(self, me, order):
        result = jnp.zeros((1,), jnp.int32) + me
        for axis in order:
            result = jnp.stack([self.moved(result, axis, step) for step in range(self.dims[axis])], axis=1).reshape(-1)
        return result

    def gather(self, own, order):
        blocks = own[None]
        for axis in order[:0:-1]:
            size = self.dims[axis]
            arrived = [blocks] + [self.send(blocks, axis, size - step) for step in range(1, size)]
            blocks = jnp.concatenate(arrived, axis=0) if size > 1 else blocks
        axis = order[0]
        return blocks, self.send(blocks, axis, 1)

    def scatter(self, keep, away, order):
        terms = [keep, self.send(away, order[0], 1)]
        for axis in order[1:]:
            size = self.dims[axis]
            if size == 1:
                continue
            cut = [term.reshape((size, term.shape[0] // size) + term.shape[1:]) for term in terms]
            arrived = []
            for step in range(1, size):
                part = sum(term[step].astype(F32) for term in cut).astype(BF16)
                arrived.append(self.send(part, axis, step))
            terms = [term[0] for term in cut] + arrived
        return sum(term[0].astype(F32) for term in terms)

    def total(self, values):
        for axis in (3, 2, 1, 0):
            size = self.dims[axis]
            if size == 4:
                one, two, three = (self.send(values, axis, step) for step in (1, 2, 3))
                values = (values + two) + (one + three)
                continue
            while size > 1:
                size //= 2
                values = values + self.send(values, axis, size)
        return values


def prepare(trajectories, noise_draw, timesteps, lengths):
    horizons = trajectories.shape[0] * trajectories.shape[1]
    length = trajectories.shape[2]
    trajectory = trajectories.reshape(horizons, length, CH)
    noise_part = noise_draw.reshape(horizons, length, CH)
    lens = lengths.reshape(horizons)
    frames = jnp.arange(length, dtype=jnp.int32)
    valid = (frames[None, :] < lens[:, None]).astype(F32)
    times = timesteps.reshape(horizons).astype(F32)
    angle_now = ((times + 1.0) / DIFF + 0.008) / 1.008 * (math.pi / 2)
    angle_zero = 0.008 / 1.008 * (math.pi / 2)
    share = jnp.cos(angle_now) ** 2 / math.cos(angle_zero) ** 2
    noisy = (
        jnp.sqrt(share)[:, None, None] * trajectory + jnp.sqrt(1.0 - share)[:, None, None] * noise_part
    ) * valid[:, :, None]
    padded = jnp.pad(noisy.astype(BF16), ((0, 0), (K // 2, K // 2), (0, 0)))
    taps = [padded[:, k : k + length] for k in range(K)]
    taps.append(jnp.zeros((horizons, length, 32 - K * CH), BF16))
    xin = jnp.concatenate(taps, axis=2)
    half_width = TE // 2
    frequency = jnp.exp(-math.log(10000.0) * jnp.arange(half_width, dtype=F32) / (half_width - 1))
    angles = times[:, None] * frequency[None, :]
    embedding = jnp.concatenate([jnp.sin(angles), jnp.cos(angles)], axis=1).astype(BF16)
    embedding = jnp.pad(embedding, ((0, 16 - horizons), (0, 0)))
    noise8 = jnp.pad(noise_part, ((0, 0), (0, 0), (0, HEAD - CH)))
    return lens, xin, noise8, embedding


def solution(mesh):
    n = mesh.shape["batch"]

    def shards(params, moment1, moment2, ema_params, trajectories, noise_draw, timesteps, lengths):
        me = lax.axis_index("batch")
        ring = Ring(n)
        shard_rows = params.shape[0] // D
        pad_rows = up_to(shard_rows, 32)
        if pad_rows - shard_rows >= 16:
            pad_rows -= 16
        low_rows = up_to(pad_rows // 2, 16)
        pads = (low_rows, pad_rows - low_rows)
        order_a = (3, 2, 1, 0)
        order_b = (3, 1, 2, 0)
        low_copy = jnp.pad(params.astype(BF16).reshape(shard_rows, D), ((0, pad_rows - shard_rows), (0, 0)))
        a0, a1 = ring.gather(low_copy[:low_rows], order_a)
        b0, b1 = ring.gather(low_copy[low_rows:], order_b)
        lens, xin, noise8, embedding = prepare(trajectories, noise_draw, timesteps, lengths)
        horizons, length = noise8.shape[:2]
        call = make_kernel(n, shard_rows, pads, horizons, length)
        ga0, ga1, gb0, gb1, loss_parts = call(
            ring.table(me, order_a), ring.table(me, order_b), lens, xin, noise8, embedding, a0, a1, b0, b1
        )
        summed = jnp.concatenate([ring.scatter(ga0, ga1, order_a), ring.scatter(gb0, gb1, order_b)], axis=0)
        summed = summed[:shard_rows].reshape(-1)
        local_count = jnp.sum(lengths).astype(F32) * CH
        lane = jnp.arange(128)[None, :]
        loss_count = jnp.where(lane == 0, jnp.sum(loss_parts), jnp.where(lane == 1, local_count, 0.0))
        loss_count = ring.total(jnp.broadcast_to(loss_count, (8, 128)))
        loss_sum = loss_count[0, 0]
        frame_count = loss_count[0, 1]
        squares = ring.total(jnp.broadcast_to(jnp.sum(summed * summed), (8, 128)))[0, 0]
        grad_norm = jnp.sqrt(squares) / frame_count
        clipped = summed / frame_count * jnp.minimum(1.0, clip_limit / (grad_norm + 1e-06))
        new_moment1 = 0.9 * moment1 + 0.1 * clipped
        new_moment2 = 0.95 * moment2 + 0.05 * clipped * clipped
        first_hat = new_moment1 / (1.0 - 0.9**STEP)
        second_hat = new_moment2 / (1.0 - 0.95**STEP)
        new_params = params - 0.01 * (first_hat / (jnp.sqrt(second_hat) + 1e-08) + 0.01 * params)
        new_ema = 0.8 * ema_params + 0.2 * new_params
        return (
            new_params,
            new_moment1,
            new_moment2,
            new_ema,
            new_params.astype(BF16),
            grad_norm,
            loss_sum,
            frame_count,
        )

    flat = P("batch")
    wide = P(None, "batch", None, None)
    narrow = P(None, "batch")
    return jax.shard_map(
        shards,
        mesh=mesh,
        in_specs=(flat, flat, flat, flat, wide, wide, narrow, narrow),
        out_specs=(flat, flat, flat, flat, flat, P(), P(), P()),
        check_vma=False,
    )
```

```python
import math

import jax
import jax.numpy as jnp
import numpy as np
from jax import lax
from jax.experimental import pallas as pl
from jax.experimental.pallas import tpu as pltpu
from jax.sharding import PartitionSpec as P

D = 256
TE = 128
CH = 6
GROUPS = 8
K = 5
DIFF = 256
STEP = 10

CHUNK = 64
HEAD = 8
clip_limit = 0.05

F32 = jnp.float32
BF16 = jnp.bfloat16


TIME_FIRST, TIME_FIRST_BIAS, TIME_SECOND, TIME_SECOND_BIAS, INPUT_CONV, INPUT_BIAS = range(6)
DOWN = 6
DOWN_SAMPLE, DOWN_SAMPLE_BIAS, UP_SAMPLE, UP_SAMPLE_BIAS = range(16, 20)
UP = 20
UP_RES, UP_RES_BIAS, HEAD_MAT, HEAD_BIAS = range(30, 34)
CONV1, BIAS1, GAIN1, SHIFT1, TIME, TIME_BIAS, CONV2, BIAS2, GAIN2, SHIFT2 = range(10)


def layout():
    counts = [TE, 1, D, 1, K * CH, 1]
    counts += [K * D, 1, 1, 1, D, 1, K * D, 1, 1, 1]
    counts += [3 * D, 1, 4 * D, 1]
    counts += [2 * K * D, 1, 1, 1, D, 1, K * D, 1, 1, 1, 2 * D, 1]
    counts += [CH, 1]
    return [(sum(counts[:i]), count) for i, count in enumerate(counts)]


ROWS = layout()
MATS = (
    TIME_FIRST,
    TIME_SECOND,
    DOWN + CONV1,
    DOWN + TIME,
    DOWN + CONV2,
    DOWN_SAMPLE,
    UP_SAMPLE,
    UP + CONV1,
    UP + TIME,
    UP + CONV2,
    UP_RES,
)
SUMS = (INPUT_BIAS, DOWN_SAMPLE_BIAS, UP_SAMPLE_BIAS, UP_RES_BIAS) + tuple(
    block + piece for block in (DOWN, UP) for piece in (BIAS1, GAIN1, SHIFT1, BIAS2, GAIN2, SHIFT2)
)
NORMS = 4


def up_to(value, step):
    return -(-value // step) * step


def mm(left, right):
    return jnp.dot(left, right, preferred_element_type=F32)


def mm_nt(left, right):
    return lax.dot_general(left, right, (((1,), (1,)), ((), ())), preferred_element_type=F32)


def mm_tn(left, right):
    return lax.dot_general(left, right, (((0,), (0,)), ((), ())), preferred_element_type=F32)


def mish_pair(v):
    c = jnp.minimum(v, 20.0)
    e = jnp.exp(c)
    n = e * (e + 2.0)
    r = 1.0 / (n + 2.0)
    t = n * r
    return v * t, t + (4.0 * c) * (e * (1.0 + e)) * (r * r)


def fold(values):
    rows, cols = values.shape
    return jnp.sum(values.reshape(rows // 8, 8, cols), axis=0)


def pad_get(pad, h, start, size, stride=1):
    where = pl.ds(start, size, stride=stride) if stride > 1 else pl.ds(start, size)
    return jnp.concatenate([pad[0, h, where, :], pad[1, h, where, :]], axis=1)


def pad_set(pad, h, start, value, stride=1):
    size = value.shape[0]
    where = pl.ds(start, size, stride=stride) if stride > 1 else pl.ds(start, size)
    pad[0, h, where, :] = value[:, : D // 2]
    pad[1, h, where, :] = value[:, D // 2 :]


def group_sums(parts, ones):
    horizons = parts[0].shape[0]
    rows = 8 * horizons
    stacked = []
    for part in parts:
        part = part.reshape(rows, D)
        high = part.astype(BF16).astype(F32)
        rest = part - high
        mid = rest.astype(BF16).astype(F32)
        stacked += [high, mid, rest - mid]
    summed = mm(jnp.concatenate(stacked, axis=0).astype(BF16), ones)
    pieces = [summed[rows * i : rows * i + rows] for i in range(3 * len(parts))]
    return [
        jnp.sum((pieces[3 * i] + pieces[3 * i + 1] + pieces[3 * i + 2]).reshape(horizons, 8, D), axis=1)
        for i in range(len(parts))
    ]


def make_kernel(n, shard_rows, pad_rows, plan_in, plan_out, horizons, length):
    half = length // 2
    count_inv = 1.0 / (length * (D // GROUPS))
    total_rows = n * shard_rows
    strips = sorted({(low, rows) for low, rows, _ in plan_in})
    every = horizons * length
    halves = horizons * half
    chunks = [slice(i, i + CHUNK) for i in range(0, length, CHUNK)]
    groups = [range(g * n // 8, (g + 1) * n // 8) for g in range(8)]
    D1, D2, U1, U2 = range(4)

    def kernel(places_in, places_out, lens, scales, start, noise, emb, *rest):
        sources, rest = rest[: 2 * len(plan_in)], rest[2 * len(plan_in) :]
        targets, rest = rest[: 2 * len(plan_out)], rest[2 * len(plan_out) :]
        loss_out, *rest = rest
        run(places_in, places_out, lens, scales, start, noise, emb, sources, targets, loss_out, *rest)

    def run(
        places_in, places_out, lens, scales, start, noise, emb, sources, targets, loss_out,
        stage, flat, ones, padS, padR, padY, wide, slim, buf, extra, xt, xin,
        x_d1, x_d2, x_e, x_o, x_y, x_j, x_u2,
        xhat, mp, stats, consts, rstds, temb_d, temb_u, dtemb_d, dtemb_u,
        w_in, w_tf, w_ts, w_d1, w_dt, w_d2, w_ds, w_us, w_u1, w_ut, w_u2, w_res,
        t_d1, t_d2, t_ds, t_us, t_u1, t_u2,
        sem_in, sem_out,
    ):
        w = dict(zip(MATS, (w_tf, w_ts, w_d1, w_dt, w_d2, w_ds, w_us, w_u1, w_ut, w_u2, w_res)))

        def row(label):
            return flat[ROWS[label][0] : ROWS[label][0] + 1, :]

        def put(label, offset, value):
            first = ROWS[label][0] + offset
            flat[first : first + value.shape[0], :] = value

        def put_row(label, value):
            put(label, 0, jnp.sum(value.reshape(-1, D), axis=0, keepdims=True))

        def moves(plan, places):
            number = 0
            for i in range(2 * len(plan)):
                low_row, rows, blocks = plan[i % len(plan)]
                for b in range(len(blocks)):
                    yield i, b, pl.ds(low_row, rows), places[number]
                    number += 1

        for i, b, rows, s in moves(plan_in, places_in):
            pltpu.make_async_copy(sources[i].at[b], stage.at[s, rows, :], sem_in.at[s * 8 // n]).start()
        group_row = lax.broadcasted_iota(jnp.int32, (D, D), 0) // (D // GROUPS)
        group_col = lax.broadcasted_iota(jnp.int32, (D, D), 1) // (D // GROUPS)
        ones[...] = (group_row == group_col).astype(F32).astype(BF16)
        zero8 = jnp.zeros((8, D), F32)
        for pad, rows in ((padS, length), (padR, length), (padY, half)):
            for h in range(horizons):
                pad_set(pad, h, 0, zero8)
                pad_set(pad, h, rows + 8, zero8)
        dtemb_d[...] = jnp.zeros_like(dtemb_d)
        dtemb_u[...] = jnp.zeros_like(dtemb_u)
        for group in groups:
            for s in group:
                for low_row, rows in strips:
                    strip = stage.at[s, pl.ds(low_row, rows), :]
                    pltpu.make_async_copy(strip, strip, sem_in.at[s * 8 // n]).wait()
            for s in group:
                flat[s * shard_rows : s * shard_rows + pad_rows, :] = stage[s].astype(F32)
        for label in MATS:
            first, count = ROWS[label]
            for i in range(0, count, CHUNK):
                size = min(CHUNK, count - i)
                w[label][i : i + size, :] = flat[first + i : first + i + size, :].astype(BF16)
        for source, target, taps in ((w_d1, t_d1, K), (w_d2, t_d2, K), (w_us, t_us, 4), (w_u2, t_u2, K)):
            for k in range(taps):
                target[k * D : k * D + D, :] = source[k * D : k * D + D, :].T
        for k, source in enumerate((0, 2, 1)):
            t_ds[k * D : k * D + D, :] = w_ds[source * D : source * D + D, :].T
        for k in range(K):
            for j in range(2):
                t_u1[k * D : k * D + D, j * D : j * D + D] = w_u1[(2 * k + j) * D : (2 * k + j + 1) * D, :].T
        for j in range(2):
            t_u1[K * D : K * D + D, j * D : j * D + D] = w_res[j * D : j * D + D, :].T

        first = ROWS[HEAD_MAT][0]
        head_rows = flat[first : first + 8, :].astype(BF16)
        at_row = lax.broadcasted_iota(jnp.int32, (D, D), 0)
        at_col = lax.broadcasted_iota(jnp.int32, (D, D), 1)
        sub_row = lax.broadcasted_iota(jnp.int32, (8, D), 0)
        sub_col = lax.broadcasted_iota(jnp.int32, (8, D), 1)

        def picker(j):
            return ((at_col * CH + j) % D == at_row).astype(F32).astype(BF16)

        def picked(j):
            return (sub_col * CH + j) // D == sub_row

        head_t = zero8
        for j in range(CH):
            spread = mm(head_rows, picker(j))
            line = jnp.sum(jnp.where(picked(j), spread, 0.0), axis=0, keepdims=True)
            head_t = jnp.where(sub_row == j, line, head_t)
        head_b = head_t.astype(BF16)
        on_line = (sub_row == sub_col) & (sub_row < CH)
        head_bias = jnp.sum(jnp.where(on_line, row(HEAD_BIAS), 0.0), axis=1, keepdims=True)

        emb_b = emb[...]
        z1 = mm(emb_b, w_tf[...]) + row(TIME_FIRST_BIAS)
        t1, slope1 = mish_pair(z1)
        t1 = t1.astype(BF16)
        z2 = mm(t1, w_ts[...]) + row(TIME_SECOND_BIAS)
        t2, slope2 = mish_pair(z2)
        timing = t2.astype(BF16)
        temb_d[...] = mm(timing, w_dt[...]) + row(DOWN + TIME_BIAS)
        temb_u[...] = mm(timing, w_ut[...]) + row(UP + TIME_BIAS)

        def each(body):
            for h in range(horizons):
                body(h, h * length)

        def shifted(target, pad, step, offset, sign):
            def body(h, base):
                for k in range(K):
                    start = 8 + sign * (k - K // 2)
                    left = step * k + offset
                    for c in chunks:
                        target[pl.ds(base + c.start, CHUNK), left : left + D] = pad_get(
                            pad, h, start + c.start, CHUNK
                        ).astype(BF16)

            each(body)

        def norm_forward(layer, gain, shift, write):
            def add_up(h, base):
                total = zero8
                for c in chunks:
                    total = total + fold(buf[pl.ds(base + c.start, CHUNK), :])
                stats[0, h] = total

            each(add_up)
            (mean,) = group_sums([stats[0]], ones[...])
            consts[0, 0:horizons, :] = mean * count_inv

            def add_squares(h, base):
                mean = consts[0, pl.ds(h, 1), :]
                total = zero8
                for c in chunks:
                    off = buf[pl.ds(base + c.start, CHUNK), :] - mean
                    total = total + fold(off * off)
                stats[0, h] = total

            each(add_squares)
            (var,) = group_sums([stats[0]], ones[...])
            rstds[layer, 0:horizons, :] = lax.rsqrt(var * count_inv + 1e-05)

            def finish(h, base):
                mean = consts[0, pl.ds(h, 1), :]
                rstd = rstds[layer, pl.ds(h, 1), :]
                for c in chunks:
                    rows = pl.ds(base + c.start, CHUNK)
                    xh = (buf[rows, :] - mean) * rstd
                    value, slope = mish_pair(xh * gain + shift)
                    xhat[layer, rows, :] = xh
                    mp[layer, rows, :] = slope.astype(BF16)
                    write(h, rows, c.start, value)

            each(finish)

        def norm_backward(layer, block, second, source):
            gain = row(block + GAIN1 + second)

            def first_pass(h, base):
                one = two = plain = zero8
                for c in chunks:
                    rows = pl.ds(base + c.start, CHUNK)
                    value = source[rows, :]
                    dv = value * mp[layer, rows, :].astype(F32)
                    plain = plain + fold(value)
                    one = one + fold(dv)
                    two = two + fold(dv * xhat[layer, rows, :])
                    buf[rows, :] = dv
                stats[0, h] = one
                stats[1, h] = two
                stats[2, h] = plain

            each(first_pass)
            put_row(block + SHIFT1 + second, stats[0])
            put_row(block + GAIN1 + second, stats[1])
            mean1, mean2 = group_sums([stats[0] * gain, stats[1] * gain], ones[...])
            consts[0, 0:horizons, :] = mean1 * count_inv
            consts[1, 0:horizons, :] = mean2 * count_inv

            def second_pass(h, base):
                rstd = rstds[layer, pl.ds(h, 1), :]
                scale = rstd * gain
                mean1 = rstd * consts[0, pl.ds(h, 1), :]
                mean2 = rstd * consts[1, pl.ds(h, 1), :]
                total = zero8
                for c in chunks:
                    rows = pl.ds(base + c.start, CHUNK)
                    dc = buf[rows, :] * scale - mean1 - xhat[layer, rows, :] * mean2
                    pad_set(padR, h, c.start + 8, dc)
                    total = total + fold(dc)
                stats[0, h] = total

            each(second_pass)
            put_row(block + BIAS1 + second, stats[0])

        def low(value):
            return value.astype(BF16).astype(F32)

        def weight_grads(source, width, dy, targets):
            rows = source.shape[0]
            for j in range(width // D):
                xt[j * D : j * D + D, 0:rows] = source[:, j * D : j * D + D].T
            for label, offset, left in targets:
                put(label, offset, mm(xt[0:width, 0:rows], dy[:, left : left + D]))

        frame = lax.broadcasted_iota(jnp.int32, (HEAD, length), 1)
        for h in range(horizons):
            at = slice(h * length, h * length + length)
            noisy = scales[h] * start[:, at] + scales[horizons + h] * noise[:, at]
            noisy = jnp.where(frame < lens[h], noisy, 0.0)
            taps = []
            for k in range(K):
                shift = k - K // 2
                moved = pltpu.roll(noisy, -shift % length, 1) if shift else noisy
                taps.append(jnp.where((frame + shift >= 0) & (frame + shift < length), moved, 0.0))
            taps.append(jnp.zeros_like(noisy))
            xin[:, at] = jnp.concatenate(taps, axis=0).astype(BF16)
        first = ROWS[INPUT_CONV][0]
        taps = [jnp.where(sub_row < CH, flat[first + CH * k : first + CH * k + 8, :], 0.0) for k in range(K)]
        w_in[...] = jnp.concatenate(taps + [zero8], axis=0).astype(BF16)
        extra[...] = mm_tn(xin[...], w_in[...]) + row(INPUT_BIAS)

        def spread_entry(h, base):
            for c in chunks:
                rows = pl.ds(base + c.start, CHUNK)
                value = extra[rows, :]
                pad_set(padR, h, c.start + 8, value)
                x_d1[rows, :] = value.astype(BF16)

        each(spread_entry)
        shifted(slim, padR, D, 0, 1)
        buf[...] = mm(slim[...], w_d1[...]) + row(DOWN + BIAS1)

        def with_time(temb, target):
            def write(h, rows, start, value):
                value = value + temb[pl.ds(h, 1), :]
                pad_set(padR, h, start + 8, value)
                target[rows, :] = value.astype(BF16)

            return write

        norm_forward(D1, row(DOWN + GAIN1), row(DOWN + SHIFT1), with_time(temb_d, x_d2))
        shifted(slim, padR, D, 0, 1)
        buf[...] = mm(slim[...], w_d2[...]) + row(DOWN + BIAS2)

        def write_skip(h, rows, start, value):
            pad_set(padS, h, start + 8, value + extra[rows, :])

        norm_forward(D2, row(DOWN + GAIN2), row(DOWN + SHIFT2), write_skip)

        def cut(h, base):
            rows = pl.ds(h * half, half)
            slim[rows, 0:D] = pad_get(padS, h, 7, half, 2).astype(BF16)
            even = pad_get(padS, h, 8, half, 2).astype(BF16)
            odd = pad_get(padS, h, 9, half, 2).astype(BF16)
            slim[rows, D : 2 * D] = even
            slim[rows, 2 * D : 3 * D] = odd
            x_e[rows, :] = even
            x_o[rows, :] = odd

        each(cut)
        buf[0:halves, :] = mm(slim[0:halves, 0 : 3 * D], w_ds[...]) + row(DOWN_SAMPLE_BIAS)

        def around(h, base):
            rows = pl.ds(h * half, half)
            coarse = buf[rows, :]
            pad_set(padY, h, 8, coarse)
            now = coarse.astype(BF16)
            x_y[rows, :] = now
            slim[rows, 0:D] = now
            slim[rows, D : 2 * D] = pad_get(padY, h, 7, half).astype(BF16)
            slim[rows, 2 * D : 3 * D] = pad_get(padY, h, 9, half).astype(BF16)

        each(around)
        up_bias = row(UP_SAMPLE_BIAS)
        low_half = slice(0, halves)
        buf[0:halves, :] = (
            mm(slim[low_half, 0:D], w_us[D : 2 * D, :]) + mm(slim[low_half, D : 2 * D], w_us[3 * D : 4 * D, :]) + up_bias
        )
        buf[halves:every, :] = (
            mm(slim[low_half, 2 * D : 3 * D], w_us[0:D, :]) + mm(slim[low_half, 0:D], w_us[2 * D : 3 * D, :]) + up_bias
        )

        def interleave(h, base):
            start = h * half
            pad_set(padR, h, 8, buf[pl.ds(start, half), :], 2)
            pad_set(padR, h, 9, buf[pl.ds(halves + start, half), :], 2)

        each(interleave)

        shifted(wide, padR, 2 * D, 0, 1)
        shifted(wide, padS, 2 * D, D, 1)
        middle = 2 * (K // 2) * D
        x_j[...] = wide[:, middle : middle + 2 * D]
        extra[...] = mm(wide[:, middle : middle + 2 * D], w_res[...]) + row(UP_RES_BIAS)
        buf[...] = mm(wide[...], w_u1[...]) + row(UP + BIAS1)
        norm_forward(U1, row(UP + GAIN1), row(UP + SHIFT1), with_time(temb_u, x_u2))
        shifted(slim, padR, D, 0, 1)
        buf[...] = mm(slim[...], w_u2[...]) + row(UP + BIAS2)
        top_at = slice((K + 1) * D, (K + 2) * D)

        def write_top(h, rows, start, value):
            wide[rows, top_at] = (value + extra[rows, :]).astype(BF16)

        norm_forward(U2, row(UP + GAIN2), row(UP + SHIFT2), write_top)

        top = wide[:, top_at]
        error = mm_nt(head_b, top) + head_bias - noise[...]
        channel = lax.broadcasted_iota(jnp.int32, (HEAD, length), 0)
        error = jnp.concatenate(
            [
                jnp.where((frame < lens[h]) & (channel < CH), error[:, h * length : h * length + length], 0.0)
                for h in range(horizons)
            ],
            axis=1,
        )
        loss_out[...] = jnp.sum(error * error, axis=1, keepdims=True) + jnp.zeros((HEAD, 128), F32)
        error = 2.0 * error
        head_sum = jnp.sum(error, axis=1, keepdims=True)
        error = error.astype(BF16)
        dhead = mm(error, top)

        dtop = mm_tn(error, head_b).astype(BF16)
        wide[:, K * D : (K + 1) * D] = dtop
        extra[...] = dtop.astype(F32)
        norm_backward(U2, UP, CONV2, extra)
        put_row(UP_RES_BIAS, stats[2])
        shifted(slim, padR, D, 0, -1)
        buf[...] = low(mm(slim[...], t_u2[...]))
        weight_grads(x_u2, D, slim, [(UP + CONV2, k * D, k * D) for k in range(K)])
        norm_backward(U1, UP, 0, buf)
        dtemb_u[0:horizons, :] = jnp.sum(stats[2], axis=1)
        shifted(wide, padR, D, 0, -1)
        all_taps = slice(0, (K + 1) * D)
        buf[...] = low(mm(wide[:, all_taps], t_u1[:, :D]))
        extra[...] = low(mm(wide[:, all_taps], t_u1[:, D:]))
        weight_grads(
            x_j, 2 * D, wide, [(UP + CONV1, 2 * k * D, k * D) for k in range(K)] + [(UP_RES, 0, K * D)]
        )

        def cut_back(h, base):
            total = zero8
            for c in chunks:
                value = buf[pl.ds(base + c.start, CHUNK), :]
                pad_set(padR, h, c.start + 8, value)
                total = total + fold(value)
            stats[0, h] = total
            rows = pl.ds(h * half, half)
            for k in range(4):
                slim[rows, k * D : k * D + D] = pad_get(padR, h, 7 + k, half, 2).astype(BF16)

        each(cut_back)
        put_row(UP_SAMPLE_BIAS, stats[0])
        buf[low_half, :] = low(mm(slim[low_half, 0 : 4 * D], t_us[...]))
        weight_grads(x_y, D, slim.at[low_half, :], [(UP_SAMPLE, k * D, k * D) for k in range(4)])

        def around_back(h, base):
            start = h * half
            dcoarse = buf[pl.ds(start, half), :]
            pad_set(padY, h, 8, dcoarse)
            stats[0, h] = fold(dcoarse)
            rows = pl.ds(halves + start, half)
            slim[rows, 0:D] = pad_get(padY, h, 9, half).astype(BF16)
            slim[rows, D : 2 * D] = dcoarse.astype(BF16)

        each(around_back)
        put_row(DOWN_SAMPLE_BIAS, stats[0])
        high_half = slice(halves, every)
        buf[low_half, :] = low(mm(slim[high_half, D : 2 * D], t_ds[2 * D : 3 * D, :]))
        buf[high_half, :] = low(mm(slim[high_half, 0 : 2 * D], t_ds[0 : 2 * D, :]))
        weight_grads(x_o, D, slim.at[high_half, :], [(DOWN_SAMPLE, 0, 0), (DOWN_SAMPLE, 2 * D, D)])
        weight_grads(x_e, D, slim.at[high_half, :], [(DOWN_SAMPLE, D, D)])
        each(interleave)

        def add_skip(h, base):
            for c in chunks:
                rows = pl.ds(base + c.start, CHUNK)
                extra[rows, :] = extra[rows, :] + pad_get(padR, h, c.start + 8, CHUNK)

        each(add_skip)

        norm_backward(D2, DOWN, CONV2, extra)
        shifted(slim, padR, D, 0, -1)
        buf[...] = low(mm(slim[...], t_d2[...]))
        weight_grads(x_d2, D, slim, [(DOWN + CONV2, k * D, k * D) for k in range(K)])
        norm_backward(D1, DOWN, 0, buf)
        dtemb_d[0:horizons, :] = jnp.sum(stats[2], axis=1)
        shifted(slim, padR, D, 0, -1)
        buf[...] = low(mm(slim[...], t_d1[...]))
        weight_grads(x_d1, D, slim, [(DOWN + CONV1, k * D, k * D) for k in range(K)])

        def at_entry(h, base):
            total = zero8
            for c in chunks:
                rows = pl.ds(base + c.start, CHUNK)
                value = buf[rows, :] + extra[rows, :]
                total = total + fold(value)
                wide[rows, 0:D] = value.astype(BF16)
            stats[0, h] = total

        each(at_entry)
        put_row(INPUT_BIAS, stats[0])
        entry_grads = mm(xin[...], wide[:, 0:D])
        for k in range(K):
            put(INPUT_CONV, CH * k, entry_grads[HEAD * k : HEAD * k + CH])

        down_b = dtemb_d[...].astype(BF16)
        up_b = dtemb_u[...].astype(BF16)
        put(DOWN + TIME, 0, mm_tn(timing, down_b))
        put(UP + TIME, 0, mm_tn(timing, up_b))
        dtiming = low(mm_nt(down_b, w_dt[...]) + mm_nt(up_b, w_ut[...]))
        dz2 = dtiming * slope2
        dz2_b = dz2.astype(BF16)
        put(TIME_SECOND, 0, mm_tn(t1, dz2_b))
        dz1 = low(mm_nt(dz2_b, w_ts[...])) * slope1
        put(TIME_FIRST, 0, mm_tn(emb_b, dz1.astype(BF16)))
        put_row(TIME_FIRST_BIAS, dz1)
        put_row(TIME_SECOND_BIAS, dz2)
        put_row(DOWN + TIME_BIAS, dtemb_d[...])
        put_row(UP + TIME_BIAS, dtemb_u[...])

        tail = ROWS[HEAD_MAT][0]
        flat[tail : total_rows + 16, :] = jnp.zeros((total_rows + 16 - tail, D), F32)
        packed = zero8
        for j in range(CH):
            spread = jnp.where(picked(j), jnp.broadcast_to(dhead[j : j + 1, :], (8, D)), 0.0)
            packed = packed + mm_nt(spread.astype(BF16), picker(j))
        put(HEAD_MAT, 0, packed[:CH])
        put_row(HEAD_BIAS, jnp.where(on_line, head_sum, 0.0))

        for s in range(n):
            stage[s] = flat[s * shard_rows : s * shard_rows + pad_rows, :].astype(BF16)
        outward = [
            pltpu.make_async_copy(stage.at[s, rows, :], targets[i].at[b], sem_out)
            for i, b, rows, s in moves(plan_out, places_out)
        ]
        for move in outward:
            move.start()
        for move in outward:
            move.wait()

    vm = pltpu.VMEM
    scratch = [
        vm((n, pad_rows, D), BF16),
        vm((total_rows + pad_rows, D), F32),
        vm((D, D), BF16),
        vm((2, horizons, length + 16, D // 2), F32),
        vm((2, horizons, length + 16, D // 2), F32),
        vm((2, horizons, half + 16, D // 2), F32),
        vm((every, 2 * K * D), BF16),
        vm((every, K * D), BF16),
        vm((every, D), F32),
        vm((every, D), F32),
        vm((2 * D, every), BF16),
        vm(((K + 1) * HEAD, every), BF16),
        vm((every, D), BF16),
        vm((every, D), BF16),
        vm((halves, D), BF16),
        vm((halves, D), BF16),
        vm((halves, D), BF16),
        vm((every, 2 * D), BF16),
        vm((every, D), BF16),
        vm((NORMS, every, D), F32),
        vm((NORMS, every, D), BF16),
        vm((3, horizons, 8, D), F32),
        vm((2, 8, D), F32),
        vm((NORMS, 8, D), F32),
        vm((16, D), F32),
        vm((16, D), F32),
        vm((16, D), F32),
        vm((16, D), F32),
    ]
    scratch += [vm(((K + 1) * HEAD, D), BF16)]
    scratch += [vm((ROWS[label][1], D), BF16) for label in MATS]
    scratch += [
        vm((K * D, D), BF16),
        vm((K * D, D), BF16),
        vm((3 * D, D), BF16),
        vm((4 * D, D), BF16),
        vm(((K + 1) * D, 2 * D), BF16),
        vm((K * D, D), BF16),
        pltpu.SemaphoreType.DMA((8,)),
        pltpu.SemaphoreType.DMA,
    ]
    shapes = [jax.ShapeDtypeStruct((len(blocks), rows, D), BF16) for _, rows, blocks in plan_out] * 2
    shapes.append(jax.ShapeDtypeStruct((HEAD, 128), F32))
    smem = pl.BlockSpec(memory_space=pltpu.SMEM)
    local = pl.BlockSpec(memory_space=pltpu.VMEM)
    remote = pl.BlockSpec(memory_space=pl.ANY)
    flops = 6 * 2100000 * every
    return pl.pallas_call(
        kernel,
        out_shape=shapes,
        in_specs=[smem] * 4 + [local] * 3 + [remote] * (2 * len(plan_in)),
        out_specs=[remote] * (2 * len(plan_out)) + [local],
        scratch_shapes=scratch,
        compiler_params=pltpu.CompilerParams(vmem_limit_bytes=63 * 1024 * 1024),
        cost_estimate=pl.CostEstimate(flops=flops, bytes_accessed=10000000, transcendentals=3000000),
        name="step",
    )


def device_dims(n):
    known = {32: (4, 2, 2), 256: (4, 8, 4)}
    return known.get(n, (n // 2, 1, 1))


Z, Y, X, CORE = range(4)


class Ring:
    def __init__(self, n, rows):
        self.n = n
        self.dims = device_dims(n) + (2,)
        strides = [1]
        for size in self.dims[:0:-1]:
            strides.insert(0, strides[0] * size)
        self.strides = strides
        deep, tall, broad = self.dims[:3]
        self.square = tall == 2 and broad == 2 and deep % 2 == 0
        if self.square:
            self.cut = up_to(rows * 3 // 4, 16)
            self.half = deep // 2
            head = (0, self.cut)
            tail = (self.cut, rows - self.cut)
            full = range(deep)
            low, high, beside, above, own = (
                [(z, y, x) for z in zs]
                for zs, y, x in (
                    (range(self.half), 1, 1),
                    (range(self.half, deep), 1, 1),
                    (full, 0, 1),
                    (full, 1, 0),
                    (full, 0, 0),
                )
            )
            tails = tail + ([(z, y, x) for z in full for x in range(2) for y in range(2)],)
            rest = head + (beside + above + own,)
            self.plan_in = [head + (low,), head + (high,), tails, rest]
            self.plan_out = [head + (low + high,), tails, rest]
        else:
            places = [(z, y, x) for x in range(broad) for y in range(tall) for z in range(deep)]
            self.plan_in = self.plan_out = [(0, rows, places)]

    def moved(self, index, axis, step):
        at = index // self.strides[axis] % self.dims[axis]
        return index + ((at + step) % self.dims[axis] - at) * self.strides[axis]

    def send(self, values, *moves):
        def target(index):
            for axis, step in moves:
                index = self.moved(index, axis, step)
            return index

        return lax.ppermute(values, "batch", [(i, target(i)) for i in range(self.n)])

    def table(self, me, plan):
        places = [place + (core,) for core in range(2) for _, _, blocks in plan for place in blocks]
        result = jnp.zeros((len(places),), jnp.int32)
        for axis, (size, stride) in enumerate(zip(self.dims, self.strides)):
            step = np.array([place[axis] for place in places], np.int32)
            result = result + (me // stride + step) % size * stride
        return result

    def along(self, blocks, axis):
        size = self.dims[axis]
        if size == 1:
            return blocks
        return jnp.concatenate([blocks] + [self.send(blocks, (axis, size - step)) for step in range(1, size)], axis=0)

    def gather(self, own, small):
        if self.square:
            head = own[None, : self.cut]
            tail = own[None, self.cut :]
            tail_y = self.send(tail, (Y, 1))
            column = self.along(head, Z)
            pair = jnp.concatenate([tail, tail_y], axis=0)
            tails = jnp.concatenate([pair, self.send(pair, (X, 1))], axis=0)
            tails, column = lax.optimization_barrier((tails, column))
            head_x = self.send(column, (X, 1))
            head_y = self.send(column, (Y, 1))
            tails = self.along(tails, Z)
            head_x, head_y, tails, small = lax.optimization_barrier((head_x, head_y, tails, small))
            head_low = self.send(head_y[: self.half], (X, 1))
            head_high = self.send(head_x[self.half :], (Y, 1))
            rest = jnp.concatenate([head_x, head_y, column], axis=0)
            mine = [head_low, head_high, tails, rest]
        else:
            blocks = own[None]
            for axis in (Z, Y, X):
                blocks = self.along(blocks, axis)
            mine = [blocks]
        return mine + [self.send(blocks, (CORE, 1)) for blocks in mine], small

    def scatter(self, mine, away):
        first = self.send(away[0], (CORE, 1))
        first, away = lax.optimization_barrier((first, away[1:]))
        arrived = [first] + [self.send(blocks, (CORE, 1)) for blocks in away]
        pairs = list(zip(mine, arrived))

        def total(terms):
            return sum(term.astype(F32) for term in terms)

        def column(terms):
            deep = self.dims[Z]
            return [term[0] for term in terms] + [
                self.send(total(term[step] for term in terms).astype(BF16), (Z, step)) for step in range(1, deep)
            ]

        if not self.square:
            terms = list(pairs[0])
            for axis in (X, Y):
                size = self.dims[axis]
                terms = [term.reshape((size, term.shape[0] // size) + term.shape[1:]) for term in terms]
                arrived = [
                    self.send(total(term[step] for term in terms).astype(BF16), (axis, step)) for step in range(1, size)
                ]
                terms = [term[0] for term in terms] + arrived
            return total(column(terms))
        half = self.half
        deep = self.dims[Z]
        corner, tails, rest = pairs
        from_x = self.send(total(term[:half] for term in corner).astype(BF16), (X, 1))
        from_y = self.send(total(term[half:] for term in corner).astype(BF16), (Y, 1))
        tails, rest = lax.optimization_barrier((tails, rest))
        tail = total(column([term.reshape((deep, 4) + term.shape[1:]) for term in tails]))
        beside, above, own = ([term[deep * i : deep * i + deep] for term in rest] for i in range(3))
        nothing = jnp.zeros_like(from_x)
        from_y = jnp.concatenate([nothing, from_y], axis=0)
        from_x = jnp.concatenate([from_x, nothing], axis=0)
        got_x = self.send(total(beside + [from_y]).astype(BF16), (X, 1))
        got_y = self.send(total(above + [from_x]).astype(BF16), (Y, 1))
        tail, got_x, got_y = lax.optimization_barrier((tail, got_x, got_y))
        tail = tail[:2] + self.send(tail[2:].astype(BF16), (X, 1)).astype(F32)
        *head, last = column(own + [got_x, got_y])
        tail, last = lax.optimization_barrier((tail, last))
        tail = tail[0] + self.send(tail[1].astype(BF16), (Y, 1)).astype(F32)
        head = total(head + [last])
        return jnp.concatenate([head, tail], axis=0)

    def total(self, values):
        values = values + self.send(values, (CORE, 1))
        axes = (X, Y, Z)
        if self.square:
            beside = self.send(values, (X, 1))
            across = [self.send(values, (Y, 1)), self.send(values, (X, 1), (Y, 1))]
            values = (values + beside) + (across[0] + across[1])
            axes = (Z,)
        for axis in axes:
            size = self.dims[axis]
            if size == 4:
                one, two, three = (self.send(values, (axis, step)) for step in (1, 2, 3))
                values = (values + two) + (one + three)
                continue
            while size > 1:
                size //= 2
                values = values + self.send(values, (axis, size))
        return values


def prepare(trajectories, noise_draw, timesteps, lengths):
    horizons = trajectories.shape[0] * trajectories.shape[1]
    length = trajectories.shape[2]
    lens = lengths.reshape(horizons)
    times = timesteps.reshape(horizons).astype(F32)
    angle_now = ((times + 1.0) / DIFF + 0.008) / 1.008 * (math.pi / 2)
    angle_zero = 0.008 / 1.008 * (math.pi / 2)
    share = jnp.cos(angle_now) ** 2 / math.cos(angle_zero) ** 2
    scales = jnp.concatenate([jnp.sqrt(share), jnp.sqrt(1.0 - share)])
    half_width = TE // 2
    frequency = jnp.exp(-math.log(10000.0) * jnp.arange(half_width, dtype=F32) / (half_width - 1))
    angles = times[:, None] * frequency[None, :]
    embedding = jnp.concatenate([jnp.sin(angles), jnp.cos(angles)], axis=1).astype(BF16)
    embedding = jnp.pad(embedding, ((0, 16 - horizons), (0, 0)))

    def lined_up(values):
        values = jnp.transpose(values, (3, 0, 1, 2)).reshape(CH, horizons * length)
        return jnp.pad(values, ((0, HEAD - CH), (0, 0)))

    return [lens, scales, lined_up(trajectories), lined_up(noise_draw), embedding]


def update(scale, summed, params, moment1, moment2, ema_params):
    def kernel(scale, summed, params, moment1, moment2, ema_params, new_params, new_moment1, new_moment2, new_ema, low):
        clipped = summed[...] * scale[0]
        first = 0.9 * moment1[...] + 0.1 * clipped
        second = 0.95 * moment2[...] + 0.05 * clipped * clipped
        new_moment1[...] = first
        new_moment2[...] = second
        first_hat = first / (1.0 - 0.9**STEP)
        second_hat = second / (1.0 - 0.95**STEP)
        old = params[...]
        new = old - 0.01 * (first_hat / (jnp.sqrt(second_hat) + 1e-08) + 0.01 * old)
        new_params[...] = new
        new_ema[...] = 0.8 * ema_params[...] + 0.2 * new
        low[...] = new.astype(BF16)

    size = params.shape
    return pl.pallas_call(
        kernel,
        out_shape=[jax.ShapeDtypeStruct(size, F32)] * 4 + [jax.ShapeDtypeStruct(size, BF16)],
        in_specs=[pl.BlockSpec(memory_space=pltpu.SMEM)] + [pl.BlockSpec(memory_space=pltpu.VMEM)] * 5,
        out_specs=[pl.BlockSpec(memory_space=pltpu.VMEM)] * 5,
        compiler_params=pltpu.CompilerParams(vmem_limit_bytes=24 * 1024 * 1024),
        name="update",
    )(scale, summed, params, moment1, moment2, ema_params)


def solution(mesh):
    n = mesh.shape["batch"]

    def shards(params, moment1, moment2, ema_params, trajectories, noise_draw, timesteps, lengths):
        me = lax.axis_index("batch")
        shard_rows = params.shape[0] // D
        pad_rows = up_to(shard_rows, 16)
        ring = Ring(n, pad_rows)
        low_copy = jnp.pad(params.astype(BF16).reshape(shard_rows, D), ((0, pad_rows - shard_rows), (0, 0)))
        small = [ring.table(me, ring.plan_in), ring.table(me, ring.plan_out)]
        small += prepare(trajectories, noise_draw, timesteps, lengths)
        blocks, small = ring.gather(low_copy, small)
        horizons = trajectories.shape[0] * trajectories.shape[1]
        call = make_kernel(n, shard_rows, pad_rows, ring.plan_in, ring.plan_out, horizons, trajectories.shape[2])
        *sums, loss_parts = call(*small, *blocks)
        arrays = len(ring.plan_out)
        summed = ring.scatter(sums[:arrays], sums[arrays:])
        summed = summed[:shard_rows].reshape(-1)
        local_count = jnp.sum(lengths).astype(F32) * CH
        lane = jnp.arange(128)[None, :]
        scalars = jnp.where(lane == 0, jnp.sum(loss_parts[:, 0]), jnp.where(lane == 1, local_count, jnp.sum(summed * summed)))
        scalars = ring.total(jnp.broadcast_to(scalars, (8, 128)))
        loss_sum, frame_count, squares = scalars[0, 0], scalars[0, 1], scalars[0, 2]
        grad_norm = jnp.sqrt(squares) / frame_count
        scale = jnp.minimum(1.0, clip_limit / (grad_norm + 1e-06)) / frame_count
        return (*update(scale.reshape(1), summed, params, moment1, moment2, ema_params), grad_norm, loss_sum, frame_count)

    flat = P("batch")
    wide = P(None, "batch", None, None)
    narrow = P(None, "batch")
    return jax.shard_map(
        shards,
        mesh=mesh,
        in_specs=(flat, flat, flat, flat, wide, wide, narrow, narrow),
        out_specs=(flat, flat, flat, flat, flat, P(), P(), P()),
        check_vma=False,
    )
```

```python
import math

import jax
import jax.numpy as jnp
import numpy as np
from jax import lax
from jax.experimental import pallas as pl
from jax.experimental.pallas import tpu as pltpu
from jax.sharding import PartitionSpec as P

D = 256
TE = 128
CH = 6
GROUPS = 8
K = 5
DIFF = 256
STEP = 10

CHUNK = 64
HEAD = 8
clip_limit = 0.05

F32 = jnp.float32
BF16 = jnp.bfloat16


TIME_FIRST, TIME_FIRST_BIAS, TIME_SECOND, TIME_SECOND_BIAS, INPUT_CONV, INPUT_BIAS = range(6)
DOWN = 6
DOWN_SAMPLE, DOWN_SAMPLE_BIAS, UP_SAMPLE, UP_SAMPLE_BIAS = range(16, 20)
UP = 20
UP_RES, UP_RES_BIAS, HEAD_MAT, HEAD_BIAS = range(30, 34)
CONV1, BIAS1, GAIN1, SHIFT1, TIME, TIME_BIAS, CONV2, BIAS2, GAIN2, SHIFT2 = range(10)


def layout():
    counts = [TE, 1, D, 1, K * CH, 1]
    counts += [K * D, 1, 1, 1, D, 1, K * D, 1, 1, 1]
    counts += [3 * D, 1, 4 * D, 1]
    counts += [2 * K * D, 1, 1, 1, D, 1, K * D, 1, 1, 1, 2 * D, 1]
    counts += [CH, 1]
    return [(sum(counts[:i]), count) for i, count in enumerate(counts)]


ROWS = layout()
MATS = (
    TIME_FIRST,
    TIME_SECOND,
    DOWN + CONV1,
    DOWN + TIME,
    DOWN + CONV2,
    DOWN_SAMPLE,
    UP_SAMPLE,
    UP + CONV1,
    UP + TIME,
    UP + CONV2,
    UP_RES,
)
SUMS = (INPUT_BIAS, DOWN_SAMPLE_BIAS, UP_SAMPLE_BIAS, UP_RES_BIAS) + tuple(
    block + piece for block in (DOWN, UP) for piece in (BIAS1, GAIN1, SHIFT1, BIAS2, GAIN2, SHIFT2)
)
NORMS = 4


def up_to(value, step):
    return -(-value // step) * step


def mm(left, right):
    return jnp.dot(left, right, preferred_element_type=F32)


def mm_nt(left, right):
    return lax.dot_general(left, right, (((1,), (1,)), ((), ())), preferred_element_type=F32)


def mm_tn(left, right):
    return lax.dot_general(left, right, (((0,), (0,)), ((), ())), preferred_element_type=F32)


def mish_pair(v):
    c = jnp.minimum(v, 20.0)
    e = jnp.exp(c)
    n = e * (e + 2.0)
    r = 1.0 / (n + 2.0)
    t = n * r
    return v * t, t + (4.0 * c) * (e * (1.0 + e)) * (r * r)


def fold(values):
    rows, cols = values.shape
    return jnp.sum(values.reshape(rows // 8, 8, cols), axis=0)


def pad_get(pad, h, start, size, stride=1):
    where = pl.ds(start, size, stride=stride) if stride > 1 else pl.ds(start, size)
    return jnp.concatenate([pad[0, h, where, :], pad[1, h, where, :]], axis=1)


def pad_set(pad, h, start, value, stride=1):
    size = value.shape[0]
    where = pl.ds(start, size, stride=stride) if stride > 1 else pl.ds(start, size)
    pad[0, h, where, :] = value[:, : D // 2]
    pad[1, h, where, :] = value[:, D // 2 :]


def group_sums(parts, ones):
    horizons = parts[0].shape[0]
    rows = 8 * horizons
    stacked = []
    for part in parts:
        part = part.reshape(rows, D)
        high = part.astype(BF16).astype(F32)
        rest = part - high
        mid = rest.astype(BF16).astype(F32)
        stacked += [high, mid, rest - mid]
    summed = mm(jnp.concatenate(stacked, axis=0).astype(BF16), ones)
    pieces = [summed[rows * i : rows * i + rows] for i in range(3 * len(parts))]
    return [
        jnp.sum((pieces[3 * i] + pieces[3 * i + 1] + pieces[3 * i + 2]).reshape(horizons, 8, D), axis=1)
        for i in range(len(parts))
    ]


def make_kernel(n, shard_rows, pad_rows, plan_in, plan_out, horizons, length):
    half = length // 2
    count_inv = 1.0 / (length * (D // GROUPS))
    total_rows = n * shard_rows
    strips = sorted({(low, rows) for low, rows, _ in plan_in})
    every = horizons * length
    halves = horizons * half
    chunks = [slice(i, i + CHUNK) for i in range(0, length, CHUNK)]
    groups = [range(g * n // 8, (g + 1) * n // 8) for g in range(8)]
    D1, D2, U1, U2 = range(4)
    parts = 2 if horizons % 2 == 0 else 1

    def kernel(places_in, places_out, lens, scales, start, noise, emb, *rest):
        sources, rest = rest[: 2 * len(plan_in)], rest[2 * len(plan_in) :]
        targets, rest = rest[: 2 * len(plan_out)], rest[2 * len(plan_out) :]
        loss_out, *rest = rest
        run(places_in, places_out, lens, scales, start, noise, emb, sources, targets, loss_out, *rest)

    def run(
        places_in, places_out, lens, scales, start, noise, emb, sources, targets, loss_out,
        stage, flat, ones, padS, padR, padY, wide, slim, buf, extra, xt, xin,
        x_d1, x_d2, x_e, x_o, x_y, x_j, x_u2,
        xhat, mp, rstds, temb_d, temb_u, dtemb_d, dtemb_u,
        w_in, w_tf, w_ts, w_d1, w_dt, w_d2, w_ds, w_us, w_u1, w_ut, w_u2, w_res,
        t_d1, t_d2, t_ds, t_us, t_u1, t_u2,
        sem_in, sem_out,
    ):
        w = dict(zip(MATS, (w_tf, w_ts, w_d1, w_dt, w_d2, w_ds, w_us, w_u1, w_ut, w_u2, w_res)))

        def row(label):
            return flat[ROWS[label][0] : ROWS[label][0] + 1, :]

        def put(label, offset, value):
            first = ROWS[label][0] + offset
            flat[first : first + value.shape[0], :] = value

        def put_row(label, value):
            put(label, 0, jnp.sum(value.reshape(-1, D), axis=0, keepdims=True))

        def moves(plan, places):
            number = 0
            for i in range(2 * len(plan)):
                low_row, rows, blocks = plan[i % len(plan)]
                for b in range(len(blocks)):
                    yield i, b, pl.ds(low_row, rows), places[number]
                    number += 1

        for i, b, rows, s in moves(plan_in, places_in):
            pltpu.make_async_copy(sources[i].at[b], stage.at[s, rows, :], sem_in.at[s * 8 // n]).start()
        group_row = lax.broadcasted_iota(jnp.int32, (D, D), 0) // (D // GROUPS)
        group_col = lax.broadcasted_iota(jnp.int32, (D, D), 1) // (D // GROUPS)
        ones[...] = (group_row == group_col).astype(F32).astype(BF16)
        zero8 = jnp.zeros((8, D), F32)
        for pad, rows in ((padS, length), (padR, length), (padY, half)):
            for h in range(horizons):
                pad_set(pad, h, 0, zero8)
                pad_set(pad, h, rows + 8, zero8)
        dtemb_d[...] = jnp.zeros_like(dtemb_d)
        dtemb_u[...] = jnp.zeros_like(dtemb_u)
        for group in groups:
            for s in group:
                for low_row, rows in strips:
                    strip = stage.at[s, pl.ds(low_row, rows), :]
                    pltpu.make_async_copy(strip, strip, sem_in.at[s * 8 // n]).wait()
            for s in group:
                flat[s * shard_rows : s * shard_rows + pad_rows, :] = stage[s].astype(F32)
        for label in MATS:
            first, count = ROWS[label]
            for i in range(0, count, CHUNK):
                size = min(CHUNK, count - i)
                w[label][i : i + size, :] = flat[first + i : first + i + size, :].astype(BF16)
        for source, target, taps in ((w_d1, t_d1, K), (w_d2, t_d2, K), (w_us, t_us, 4), (w_u2, t_u2, K)):
            for k in range(taps):
                target[k * D : k * D + D, :] = source[k * D : k * D + D, :].T
        for k, source in enumerate((0, 2, 1)):
            t_ds[k * D : k * D + D, :] = w_ds[source * D : source * D + D, :].T
        for k in range(K):
            for j in range(2):
                t_u1[k * D : k * D + D, j * D : j * D + D] = w_u1[(2 * k + j) * D : (2 * k + j + 1) * D, :].T
        for j in range(2):
            t_u1[K * D : K * D + D, j * D : j * D + D] = w_res[j * D : j * D + D, :].T

        first = ROWS[HEAD_MAT][0]
        head_rows = flat[first : first + 8, :].astype(BF16)
        at_row = lax.broadcasted_iota(jnp.int32, (D, D), 0)
        at_col = lax.broadcasted_iota(jnp.int32, (D, D), 1)
        sub_row = lax.broadcasted_iota(jnp.int32, (8, D), 0)
        sub_col = lax.broadcasted_iota(jnp.int32, (8, D), 1)

        def picker(j):
            return ((at_col * CH + j) % D == at_row).astype(F32).astype(BF16)

        def picked(j):
            return (sub_col * CH + j) // D == sub_row

        head_t = zero8
        for j in range(CH):
            spread = mm(head_rows, picker(j))
            line = jnp.sum(jnp.where(picked(j), spread, 0.0), axis=0, keepdims=True)
            head_t = jnp.where(sub_row == j, line, head_t)
        head_b = head_t.astype(BF16)
        on_line = (sub_row == sub_col) & (sub_row < CH)
        head_bias = jnp.sum(jnp.where(on_line, row(HEAD_BIAS), 0.0), axis=1, keepdims=True)

        emb_b = emb[...]
        z1 = mm(emb_b, w_tf[...]) + row(TIME_FIRST_BIAS)
        t1, slope1 = mish_pair(z1)
        t1 = t1.astype(BF16)
        z2 = mm(t1, w_ts[...]) + row(TIME_SECOND_BIAS)
        t2, slope2 = mish_pair(z2)
        timing = t2.astype(BF16)
        temb_d[...] = mm(timing, w_dt[...]) + row(DOWN + TIME_BIAS)
        temb_u[...] = mm(timing, w_ut[...]) + row(UP + TIME_BIAS)

        share = horizons // parts
        some = share * length

        def rows_of(part):
            return slice(part * some, (part + 1) * some)

        def horizons_of(part):
            return [(h, h * length) for h in range(part * share, (part + 1) * share)]

        def halves_of(part):
            return [(h, part * some + (h - part * share) * half, h * half) for h in range(part * share, (part + 1) * share)]

        def rows_at(base, c):
            return slice(base + c.start, base + c.stop)

        def shifted(target, pad, step, offset, sign, part):
            for h, base in horizons_of(part):
                for k in range(K):
                    begin = 8 + sign * (k - K // 2)
                    left = step * k + offset
                    for c in chunks:
                        target[rows_at(base, c), left : left + D] = pad_get(pad, h, begin + c.start, CHUNK).astype(BF16)

        def norm_forward(layer, part, gain, shift, write):
            mine = horizons_of(part)
            totals = []
            for h, base in mine:
                total = zero8
                for c in chunks:
                    total = total + fold(buf[rows_at(base, c), :])
                totals.append(total)
            (mean,) = group_sums([jnp.stack(totals)], ones[...])
            mean = mean * count_inv
            totals = []
            for i, (h, base) in enumerate(mine):
                total = zero8
                for c in chunks:
                    off = buf[rows_at(base, c), :] - mean[i : i + 1]
                    total = total + fold(off * off)
                totals.append(total)
            (var,) = group_sums([jnp.stack(totals)], ones[...])
            rstd = lax.rsqrt(var * count_inv + 1e-05)
            rstds[layer, part, 0:share, :] = rstd
            for i, (h, base) in enumerate(mine):
                for c in chunks:
                    rows = rows_at(base, c)
                    xh = (buf[rows, :] - mean[i : i + 1]) * rstd[i : i + 1]
                    value, slope = mish_pair(xh * gain + shift)
                    xhat[layer, rows, :] = xh
                    mp[layer, rows, :] = slope.astype(BF16)
                    write(h, rows, c.start, value)

        pending = {}

        def put_sums(label, part, totals):
            pending[label] = sum(totals, pending.get(label, zero8))
            if part == parts - 1:
                put_row(label, pending[label])

        def norm_backward(layer, part, block, second, source):
            gain = gains[layer]
            mine = horizons_of(part)
            ones_, twos, plains = [], [], []
            for h, base in mine:
                one = two = plain = zero8
                for c in chunks:
                    rows = rows_at(base, c)
                    value = source[rows, :]
                    dv = value * mp[layer, rows, :].astype(F32)
                    plain = plain + fold(value)
                    one = one + fold(dv)
                    two = two + fold(dv * xhat[layer, rows, :])
                    buf[rows, :] = dv
                ones_.append(one)
                twos.append(two)
                plains.append(plain)
            put_sums(block + SHIFT1 + second, part, ones_)
            put_sums(block + GAIN1 + second, part, twos)
            mean1, mean2 = group_sums([jnp.stack(ones_) * gain, jnp.stack(twos) * gain], ones[...])
            rstd = rstds[layer, part, 0:share, :]
            scale = rstd * gain
            mean1 = rstd * (mean1 * count_inv)
            mean2 = rstd * (mean2 * count_inv)
            totals = []
            for i, (h, base) in enumerate(mine):
                total = zero8
                for c in chunks:
                    rows = rows_at(base, c)
                    dc = buf[rows, :] * scale[i : i + 1] - mean1[i : i + 1] - xhat[layer, rows, :] * mean2[i : i + 1]
                    pad_set(padR, h, c.start + 8, dc)
                    total = total + fold(dc)
                totals.append(total)
            put_sums(block + BIAS1 + second, part, totals)
            return plains

        def low(value):
            return value.astype(BF16).astype(F32)

        def weight_grads(source, slot, width, dy, targets):
            rows = source.shape[0]
            for j in range(width // D):
                xt[slot + j * D : slot + j * D + D, 0:rows] = source[:, j * D : j * D + D].T
            for label, offset, left in targets:
                put(label, offset, mm(xt[slot : slot + width, 0:rows], dy[:, left : left + D]))

        gains = [row(block + gain) for block in (DOWN, UP) for gain in (GAIN1, GAIN2)]
        shifts = [row(block + shift) for block in (DOWN, UP) for shift in (SHIFT1, SHIFT2)]
        frame = lax.broadcasted_iota(jnp.int32, (HEAD, length), 1)
        first = ROWS[INPUT_CONV][0]
        taps = [jnp.where(sub_row < CH, flat[first + CH * k : first + CH * k + 8, :], 0.0) for k in range(K)]
        w_in[...] = jnp.concatenate(taps + [zero8], axis=0).astype(BF16)
        input_bias, bias_d1, bias_d2, bias_ds, bias_us, bias_u1, bias_u2, bias_res = (
            row(label)
            for label in (
                INPUT_BIAS,
                DOWN + BIAS1,
                DOWN + BIAS2,
                DOWN_SAMPLE_BIAS,
                UP_SAMPLE_BIAS,
                UP + BIAS1,
                UP + BIAS2,
                UP_RES_BIAS,
            )
        )

        def entry(part):
            for h, base in horizons_of(part):
                at = slice(base, base + length)
                noisy = scales[h] * start[:, at] + scales[horizons + h] * noise[:, at]
                noisy = jnp.where(frame < lens[h], noisy, 0.0)
                taps = []
                for k in range(K):
                    shift = k - K // 2
                    moved = pltpu.roll(noisy, -shift % length, 1) if shift else noisy
                    taps.append(jnp.where((frame + shift >= 0) & (frame + shift < length), moved, 0.0))
                taps.append(jnp.zeros_like(noisy))
                xin[:, at] = jnp.concatenate(taps, axis=0).astype(BF16)
            extra[rows_of(part), :] = mm_tn(xin[:, rows_of(part)], w_in[...]) + input_bias
            for h, base in horizons_of(part):
                for c in chunks:
                    value = extra[rows_at(base, c), :]
                    pad_set(padR, h, c.start + 8, value)
                    x_d1[rows_at(base, c), :] = value.astype(BF16)
            shifted(slim, padR, D, 0, 1, part)

        def conv_d1(part):
            buf[rows_of(part), :] = mm(slim[rows_of(part), :], w_d1[...]) + bias_d1

        def with_time(temb, target):
            def write(h, rows, begin, value):
                value = value + temb[h : h + 1, :]
                pad_set(padR, h, begin + 8, value)
                target[rows, :] = value.astype(BF16)

            return write

        def norm_d1(part):
            norm_forward(D1, part, gains[D1], shifts[D1], with_time(temb_d, x_d2))
            shifted(slim, padR, D, 0, 1, part)

        def conv_d2(part):
            buf[rows_of(part), :] = mm(slim[rows_of(part), :], w_d2[...]) + bias_d2

        def write_skip(h, rows, begin, value):
            pad_set(padS, h, begin + 8, value + extra[rows, :])

        def norm_d2(part):
            norm_forward(D2, part, gains[D2], shifts[D2], write_skip)
            for h, at, among in halves_of(part):
                rows = slice(at, at + half)
                even = pad_get(padS, h, 8, half, 2).astype(BF16)
                odd = pad_get(padS, h, 9, half, 2).astype(BF16)
                slim[rows, 0:D] = pad_get(padS, h, 7, half, 2).astype(BF16)
                slim[rows, D : 2 * D] = even
                slim[rows, 2 * D : 3 * D] = odd
                x_e[among : among + half, :] = even
                x_o[among : among + half, :] = odd

        def low_half(part):
            return slice(part * some, part * some + some // 2)

        def high_half(part):
            return slice(part * some + some // 2, (part + 1) * some)

        def interleave(part):
            for h, at, _ in halves_of(part):
                pad_set(padR, h, 8, buf[at : at + half, :], 2)
                pad_set(padR, h, 9, buf[some // 2 + at : some // 2 + at + half, :], 2)

        def middle_forward(part):
            here = low_half(part)
            buf[here, :] = mm(slim[here, 0 : 3 * D], w_ds[...]) + bias_ds
            for h, at, among in halves_of(part):
                rows = slice(at, at + half)
                coarse = buf[rows, :]
                pad_set(padY, h, 8, coarse)
                now = coarse.astype(BF16)
                x_y[among : among + half, :] = now
                slim[rows, 0:D] = now
                slim[rows, D : 2 * D] = pad_get(padY, h, 7, half).astype(BF16)
                slim[rows, 2 * D : 3 * D] = pad_get(padY, h, 9, half).astype(BF16)
            now, before, after = (slim[here, k * D : k * D + D] for k in range(3))
            buf[here, :] = mm(now, w_us[D : 2 * D, :]) + mm(before, w_us[3 * D : 4 * D, :]) + bias_us
            buf[high_half(part), :] = mm(after, w_us[0:D, :]) + mm(now, w_us[2 * D : 3 * D, :]) + bias_us
            interleave(part)
            shifted(wide, padR, 2 * D, 0, 1, part)
            shifted(wide, padS, 2 * D, D, 1, part)

        def conv_u1(part):
            rows = rows_of(part)
            middle = 2 * (K // 2) * D
            x_j[rows, :] = wide[rows, middle : middle + 2 * D]
            extra[rows, :] = mm(wide[rows, middle : middle + 2 * D], w_res[...]) + bias_res
            buf[rows, :] = mm(wide[rows, :], w_u1[...]) + bias_u1

        def norm_u1(part):
            norm_forward(U1, part, gains[U1], shifts[U1], with_time(temb_u, x_u2))
            shifted(slim, padR, D, 0, 1, part)

        def conv_u2(part):
            buf[rows_of(part), :] = mm(slim[rows_of(part), :], w_u2[...]) + bias_u2

        top_at = slice((K + 1) * D, (K + 2) * D)

        def write_top(h, rows, begin, value):
            wide[rows, top_at] = (value + extra[rows, :]).astype(BF16)

        loss_terms, head_sums, dheads = [], [], []

        def norm_u2(part):
            norm_forward(U2, part, gains[U2], shifts[U2], write_top)
            rows = rows_of(part)
            top = wide[rows, top_at]
            error = mm_nt(head_b, top) + head_bias - noise[:, rows]
            channel = lax.broadcasted_iota(jnp.int32, (HEAD, length), 0)
            pieces = []
            for i, (h, base) in enumerate(horizons_of(part)):
                mine = error[:, i * length : (i + 1) * length]
                pieces.append(jnp.where((frame < lens[h]) & (channel < CH), mine, 0.0))
            error = jnp.concatenate(pieces, axis=1)
            loss_terms.append(jnp.sum(error * error, axis=1, keepdims=True))
            error = 2.0 * error
            head_sums.append(jnp.sum(error, axis=1, keepdims=True))
            error = error.astype(BF16)
            dheads.append(mm(error, top))
            dtop = mm_tn(error, head_b).astype(BF16)
            wide[rows, K * D : (K + 1) * D] = dtop
            extra[rows, :] = dtop.astype(F32)

        def back_u2(part):
            put_sums(UP_RES_BIAS, part, norm_backward(U2, part, UP, CONV2, extra))
            shifted(slim, padR, D, 0, -1, part)

        def conv_back_u2(part):
            buf[rows_of(part), :] = low(mm(slim[rows_of(part), :], t_u2[...]))

        def time_sums(target, part, plains):
            for (h, base), plain in zip(horizons_of(part), plains):
                target[h : h + 1, :] = jnp.sum(plain, axis=0, keepdims=True)

        def back_u1(part):
            time_sums(dtemb_u, part, norm_backward(U1, part, UP, 0, buf))
            shifted(wide, padR, D, 0, -1, part)

        def conv_back_u1(part):
            rows = rows_of(part)
            buf[rows, :] = low(mm(wide[rows, 0 : (K + 1) * D], t_u1[:, :D]))
            extra[rows, :] = low(mm(wide[rows, 0 : (K + 1) * D], t_u1[:, D:]))

        right = (K + 1) * D

        def middle_back(part):
            totals = []
            for h, base in horizons_of(part):
                total = zero8
                for c in chunks:
                    value = buf[rows_at(base, c), :]
                    pad_set(padR, h, c.start + 8, value)
                    total = total + fold(value)
                totals.append(total)
            put_sums(UP_SAMPLE_BIAS, part, totals)
            size = share * half
            for h, at, among in halves_of(part):
                for k in range(4):
                    left = right + k * D
                    wide[among : among + half, left : left + D] = pad_get(padR, h, 7 + k, half, 2).astype(BF16)
            mine = slice(part * size, (part + 1) * size)
            buf[low_half(part), :] = low(mm(wide[mine, right : right + 4 * D], t_us[...]))
            totals = []
            for h, at, among in halves_of(part):
                dcoarse = buf[at : at + half, :]
                pad_set(padY, h, 8, dcoarse)
                totals.append(fold(dcoarse))
                rows = slice(halves + among, halves + among + half)
                wide[rows, right : right + D] = pad_get(padY, h, 9, half).astype(BF16)
                wide[rows, right + D : right + 2 * D] = dcoarse.astype(BF16)
            put_sums(DOWN_SAMPLE_BIAS, part, totals)
            mine = slice(halves + part * size, halves + (part + 1) * size)
            buf[low_half(part), :] = low(mm(wide[mine, right + D : right + 2 * D], t_ds[2 * D : 3 * D, :]))
            buf[high_half(part), :] = low(mm(wide[mine, right : right + 2 * D], t_ds[0 : 2 * D, :]))
            interleave(part)
            for h, base in horizons_of(part):
                for c in chunks:
                    rows = rows_at(base, c)
                    extra[rows, :] = extra[rows, :] + pad_get(padR, h, c.start + 8, CHUNK)

        def back_d2(part):
            norm_backward(D2, part, DOWN, CONV2, extra)
            shifted(slim, padR, D, 0, -1, part)

        def conv_back_d2(part):
            buf[rows_of(part), :] = low(mm(slim[rows_of(part), :], t_d2[...]))

        def back_d1(part):
            time_sums(dtemb_d, part, norm_backward(D1, part, DOWN, 0, buf))
            shifted(wide, padR, D, 0, -1, part)

        def conv_back_d1(part):
            buf[rows_of(part), :] = low(mm(wide[rows_of(part), 0 : K * D], t_d1[...]))

        def at_entry(part):
            totals = []
            for h, base in horizons_of(part):
                total = zero8
                for c in chunks:
                    rows = rows_at(base, c)
                    value = buf[rows, :] + extra[rows, :]
                    total = total + fold(value)
                    slim[rows, 0:D] = value.astype(BF16)
                totals.append(total)
            put_sums(INPUT_BIAS, part, totals)

        def grads_u2():
            weight_grads(x_u2, 0, D, slim, [(UP + CONV2, k * D, k * D) for k in range(K)])

        def grads_u1():
            targets = [(UP + CONV1, 2 * k * D, k * D) for k in range(K)] + [(UP_RES, 0, K * D)]
            weight_grads(x_j, 0, 2 * D, wide, targets)

        def grads_middle():
            low_rows, high_rows = slice(0, halves), slice(halves, every)
            weight_grads(x_y, 0, D, wide.at[low_rows, :], [(UP_SAMPLE, k * D, right + k * D) for k in range(4)])
            weight_grads(
                x_o, D, D, wide.at[high_rows, :], [(DOWN_SAMPLE, 0, right), (DOWN_SAMPLE, 2 * D, right + D)]
            )
            weight_grads(x_e, 0, D, wide.at[high_rows, :], [(DOWN_SAMPLE, D, right + D)])

        def grads_d2():
            weight_grads(x_d2, D, D, slim, [(DOWN + CONV2, k * D, k * D) for k in range(K)])

        def grads_d1():
            weight_grads(x_d1, 0, D, wide, [(DOWN + CONV1, k * D, k * D) for k in range(K)])

        steps = [
            entry, conv_d1, norm_d1, conv_d2, norm_d2, middle_forward, conv_u1, norm_u1, conv_u2, norm_u2,
            back_u2, conv_back_u2, back_u1, conv_back_u1, middle_back,
            back_d2, conv_back_d2, back_d1, conv_back_d1, at_entry,
        ]
        beside = {back_u1: grads_u2, middle_back: grads_u1, conv_back_d2: grads_middle, back_d1: grads_d2}
        for i in range(len(steps) + parts - 1):
            for part in range(parts):
                if 0 <= i - part < len(steps):
                    steps[i - part](part)
            if i < len(steps) and steps[i] in beside:
                beside[steps[i]]()
        grads_d1()
        loss_out[...] = sum(loss_terms) + jnp.zeros((HEAD, 128), F32)
        head_sum = sum(head_sums)
        dhead = sum(dheads)
        entry_grads = mm(xin[...], slim[:, 0:D])
        for k in range(K):
            put(INPUT_CONV, CH * k, entry_grads[HEAD * k : HEAD * k + CH])

        down_b = dtemb_d[...].astype(BF16)
        up_b = dtemb_u[...].astype(BF16)
        put(DOWN + TIME, 0, mm_tn(timing, down_b))
        put(UP + TIME, 0, mm_tn(timing, up_b))
        dtiming = low(mm_nt(down_b, w_dt[...]) + mm_nt(up_b, w_ut[...]))
        dz2 = dtiming * slope2
        dz2_b = dz2.astype(BF16)
        put(TIME_SECOND, 0, mm_tn(t1, dz2_b))
        dz1 = low(mm_nt(dz2_b, w_ts[...])) * slope1
        put(TIME_FIRST, 0, mm_tn(emb_b, dz1.astype(BF16)))
        put_row(TIME_FIRST_BIAS, dz1)
        put_row(TIME_SECOND_BIAS, dz2)
        put_row(DOWN + TIME_BIAS, dtemb_d[...])
        put_row(UP + TIME_BIAS, dtemb_u[...])

        tail = ROWS[HEAD_MAT][0]
        flat[tail : total_rows + 16, :] = jnp.zeros((total_rows + 16 - tail, D), F32)
        packed = zero8
        for j in range(CH):
            spread = jnp.where(picked(j), jnp.broadcast_to(dhead[j : j + 1, :], (8, D)), 0.0)
            packed = packed + mm_nt(spread.astype(BF16), picker(j))
        put(HEAD_MAT, 0, packed[:CH])
        put_row(HEAD_BIAS, jnp.where(on_line, head_sum, 0.0))

        for s in range(n):
            stage[s] = flat[s * shard_rows : s * shard_rows + pad_rows, :].astype(BF16)
        outward = [
            pltpu.make_async_copy(stage.at[s, rows, :], targets[i].at[b], sem_out)
            for i, b, rows, s in moves(plan_out, places_out)
        ]
        for move in outward:
            move.start()
        for move in outward:
            move.wait()

    vm = pltpu.VMEM
    scratch = [
        vm((n, pad_rows, D), BF16),
        vm((total_rows + pad_rows, D), F32),
        vm((D, D), BF16),
        vm((2, horizons, length + 16, D // 2), F32),
        vm((2, horizons, length + 16, D // 2), F32),
        vm((2, horizons, half + 16, D // 2), F32),
        vm((every, 2 * K * D), BF16),
        vm((every, K * D), BF16),
        vm((every, D), F32),
        vm((every, D), F32),
        vm((2 * D, every), BF16),
        vm(((K + 1) * HEAD, every), BF16),
        vm((every, D), BF16),
        vm((every, D), BF16),
        vm((halves, D), BF16),
        vm((halves, D), BF16),
        vm((halves, D), BF16),
        vm((every, 2 * D), BF16),
        vm((every, D), BF16),
        vm((NORMS, every, D), F32),
        vm((NORMS, every, D), BF16),
        vm((NORMS, parts, 8, D), F32),
        vm((16, D), F32),
        vm((16, D), F32),
        vm((16, D), F32),
        vm((16, D), F32),
    ]
    scratch += [vm(((K + 1) * HEAD, D), BF16)]
    scratch += [vm((ROWS[label][1], D), BF16) for label in MATS]
    scratch += [
        vm((K * D, D), BF16),
        vm((K * D, D), BF16),
        vm((3 * D, D), BF16),
        vm((4 * D, D), BF16),
        vm(((K + 1) * D, 2 * D), BF16),
        vm((K * D, D), BF16),
        pltpu.SemaphoreType.DMA((8,)),
        pltpu.SemaphoreType.DMA,
    ]
    shapes = [jax.ShapeDtypeStruct((len(blocks), rows, D), BF16) for _, rows, blocks in plan_out] * 2
    shapes.append(jax.ShapeDtypeStruct((HEAD, 128), F32))
    smem = pl.BlockSpec(memory_space=pltpu.SMEM)
    local = pl.BlockSpec(memory_space=pltpu.VMEM)
    remote = pl.BlockSpec(memory_space=pl.ANY)
    flops = 6 * 2100000 * every
    return pl.pallas_call(
        kernel,
        out_shape=shapes,
        in_specs=[smem] * 4 + [local] * 3 + [remote] * (2 * len(plan_in)),
        out_specs=[remote] * (2 * len(plan_out)) + [local],
        scratch_shapes=scratch,
        compiler_params=pltpu.CompilerParams(vmem_limit_bytes=63 * 1024 * 1024),
        cost_estimate=pl.CostEstimate(flops=flops, bytes_accessed=10000000, transcendentals=3000000),
        name="step",
    )


def device_dims(n):
    known = {32: (4, 2, 2), 256: (4, 8, 4)}
    return known.get(n, (n // 2, 1, 1))


Z, Y, X, CORE = range(4)


class Ring:
    def __init__(self, n, rows):
        self.n = n
        self.dims = device_dims(n) + (2,)
        strides = [1]
        for size in self.dims[:0:-1]:
            strides.insert(0, strides[0] * size)
        self.strides = strides
        deep, tall, broad = self.dims[:3]
        self.square = tall == 2 and broad == 2 and deep % 2 == 0
        if self.square:
            self.cut = up_to(rows * 3 // 4, 16)
            self.half = deep // 2
            head = (0, self.cut)
            tail = (self.cut, rows - self.cut)
            full = range(deep)
            low, high, beside, above, own = (
                [(z, y, x) for z in zs]
                for zs, y, x in (
                    (range(self.half), 1, 1),
                    (range(self.half, deep), 1, 1),
                    (full, 0, 1),
                    (full, 1, 0),
                    (full, 0, 0),
                )
            )
            tails = tail + ([(z, y, x) for z in full for x in range(2) for y in range(2)],)
            rest = head + (beside + above + own,)
            self.plan_in = [head + (low,), head + (high,), tails, rest]
            self.plan_out = [head + (low + high,), tails, rest]
        else:
            places = [(z, y, x) for x in range(broad) for y in range(tall) for z in range(deep)]
            self.plan_in = self.plan_out = [(0, rows, places)]

    def moved(self, index, axis, step):
        at = index // self.strides[axis] % self.dims[axis]
        return index + ((at + step) % self.dims[axis] - at) * self.strides[axis]

    def send(self, values, *moves):
        def target(index):
            for axis, step in moves:
                index = self.moved(index, axis, step)
            return index

        return lax.ppermute(values, "batch", [(i, target(i)) for i in range(self.n)])

    def table(self, me, plan):
        places = [place + (core,) for core in range(2) for _, _, blocks in plan for place in blocks]
        result = jnp.zeros((len(places),), jnp.int32)
        for axis, (size, stride) in enumerate(zip(self.dims, self.strides)):
            step = np.array([place[axis] for place in places], np.int32)
            result = result + (me // stride + step) % size * stride
        return result

    def along(self, blocks, axis):
        size = self.dims[axis]
        if size == 1:
            return blocks
        return jnp.concatenate([blocks] + [self.send(blocks, (axis, size - step)) for step in range(1, size)], axis=0)

    def gather(self, own, small):
        if self.square:
            head = own[None, : self.cut]
            tail = own[None, self.cut :]
            tail_y = self.send(tail, (Y, 1))
            column = self.along(head, Z)
            pair = jnp.concatenate([tail, tail_y], axis=0)
            tails = jnp.concatenate([pair, self.send(pair, (X, 1))], axis=0)
            tails, column = lax.optimization_barrier((tails, column))
            head_x = self.send(column, (X, 1))
            head_y = self.send(column, (Y, 1))
            tails = [tails] + [self.send(tails, (Z, self.dims[Z] - step)) for step in range(1, self.dims[Z])]
            early = tails[1 : self.half] + tails[self.half + 1 :]
            head_x, head_y, early, small = lax.optimization_barrier((head_x, head_y, early, small))
            head_low = self.send(head_y[: self.half], (X, 1))
            head_high = self.send(head_x[self.half :], (Y, 1))
            late, head_low, head_high = lax.optimization_barrier((tails[self.half], head_low, head_high))
            tails = jnp.concatenate(tails[:1] + early[: self.half - 1] + [late] + early[self.half - 1 :], axis=0)
            rest = jnp.concatenate([head_x, head_y, column], axis=0)
            mine = [head_low, head_high, tails, rest]
        else:
            blocks = own[None]
            for axis in (Z, Y, X):
                blocks = self.along(blocks, axis)
            mine = [blocks]
        return mine + [self.send(blocks, (CORE, 1)) for blocks in mine], small

    def scatter(self, mine, away):
        first = self.send(away[0], (CORE, 1))
        first, away = lax.optimization_barrier((first, away[1:]))
        arrived = [first] + [self.send(blocks, (CORE, 1)) for blocks in away]
        pairs = list(zip(mine, arrived))

        def total(terms):
            return sum(term.astype(F32) for term in terms)

        def column(terms):
            deep = self.dims[Z]
            return [term[0] for term in terms] + [
                self.send(total(term[step] for term in terms).astype(BF16), (Z, step)) for step in range(1, deep)
            ]

        if not self.square:
            terms = list(pairs[0])
            for axis in (X, Y):
                size = self.dims[axis]
                terms = [term.reshape((size, term.shape[0] // size) + term.shape[1:]) for term in terms]
                arrived = [
                    self.send(total(term[step] for term in terms).astype(BF16), (axis, step)) for step in range(1, size)
                ]
                terms = [term[0] for term in terms] + arrived
            return total(column(terms))
        half = self.half
        deep = self.dims[Z]
        corner, tails, rest = pairs
        from_x = self.send(total(term[:half] for term in corner).astype(BF16), (X, 1))
        from_y = self.send(total(term[half:] for term in corner).astype(BF16), (Y, 1))
        tails, rest = lax.optimization_barrier((tails, rest))
        tail = column([term.reshape((deep, 4) + term.shape[1:]) for term in tails])
        at = len(tails) + half - 1
        rest, tail[at] = lax.optimization_barrier((rest, tail[at]))
        tail = total(tail)
        beside, above, own = ([term[deep * i : deep * i + deep] for term in rest] for i in range(3))
        nothing = jnp.zeros_like(from_x)
        from_y = jnp.concatenate([nothing, from_y], axis=0)
        from_x = jnp.concatenate([from_x, nothing], axis=0)
        got_x = self.send(total(beside + [from_y]).astype(BF16), (X, 1))
        got_y = self.send(total(above + [from_x]).astype(BF16), (Y, 1))
        tail, got_x, got_y = lax.optimization_barrier((tail, got_x, got_y))
        tail = tail[:2] + self.send(tail[2:].astype(BF16), (X, 1)).astype(F32)
        *head, last = column(own + [got_x, got_y])
        tail, last = lax.optimization_barrier((tail, last))
        tail = tail[0] + self.send(tail[1].astype(BF16), (Y, 1)).astype(F32)
        head = total(head + [last])
        return jnp.concatenate([head, tail], axis=0)

    def total(self, values, beside):
        arrived, beside = lax.optimization_barrier((self.send(values, (CORE, 1)), beside))
        values = values + arrived
        axes = (X, Y, Z)
        if self.square:
            other = self.send(values, (X, 1))
            across = [self.send(values, (Y, 1)), self.send(values, (X, 1), (Y, 1))]
            values = (values + other) + (across[0] + across[1])
            axes = (Z,)
        for axis in axes:
            size = self.dims[axis]
            if size == 4:
                one, two, three = (self.send(values, (axis, step)) for step in (1, 2, 3))
                values = (values + two) + (one + three)
                continue
            while size > 1:
                size //= 2
                values = values + self.send(values, (axis, size))
        return values, beside


def prepare(trajectories, noise_draw, timesteps, lengths):
    horizons = trajectories.shape[0] * trajectories.shape[1]
    length = trajectories.shape[2]
    lens = lengths.reshape(horizons)
    times = timesteps.reshape(horizons).astype(F32)
    angle_now = ((times + 1.0) / DIFF + 0.008) / 1.008 * (math.pi / 2)
    angle_zero = 0.008 / 1.008 * (math.pi / 2)
    share = jnp.cos(angle_now) ** 2 / math.cos(angle_zero) ** 2
    scales = jnp.concatenate([jnp.sqrt(share), jnp.sqrt(1.0 - share)])
    half_width = TE // 2
    frequency = jnp.exp(-math.log(10000.0) * jnp.arange(half_width, dtype=F32) / (half_width - 1))
    angles = times[:, None] * frequency[None, :]
    embedding = jnp.concatenate([jnp.sin(angles), jnp.cos(angles)], axis=1).astype(BF16)
    embedding = jnp.pad(embedding, ((0, 16 - horizons), (0, 0)))

    def lined_up(values):
        values = jnp.transpose(values, (3, 0, 1, 2)).reshape(CH, horizons * length)
        return jnp.pad(values, ((0, HEAD - CH), (0, 0)))

    return [lens, scales, lined_up(trajectories), lined_up(noise_draw), embedding]


def update(scale, summed, params, moment1, moment2, ema_params):
    def kernel(scale, summed, params, moment1, moment2, ema_params, new_params, new_moment1, new_moment2, new_ema, low):
        clipped = summed[...] * scale[0]
        first = 0.9 * moment1[...] + 0.1 * clipped
        second = 0.95 * moment2[...] + 0.05 * clipped * clipped
        new_moment1[...] = first
        new_moment2[...] = second
        first_hat = first / (1.0 - 0.9**STEP)
        second_hat = second / (1.0 - 0.95**STEP)
        old = params[...]
        new = old - 0.01 * (first_hat / (jnp.sqrt(second_hat) + 1e-08) + 0.01 * old)
        new_params[...] = new
        new_ema[...] = 0.8 * ema_params[...] + 0.2 * new
        low[...] = new.astype(BF16)

    size = params.shape
    return pl.pallas_call(
        kernel,
        out_shape=[jax.ShapeDtypeStruct(size, F32)] * 4 + [jax.ShapeDtypeStruct(size, BF16)],
        in_specs=[pl.BlockSpec(memory_space=pltpu.SMEM)] + [pl.BlockSpec(memory_space=pltpu.VMEM)] * 5,
        out_specs=[pl.BlockSpec(memory_space=pltpu.VMEM)] * 5,
        compiler_params=pltpu.CompilerParams(vmem_limit_bytes=24 * 1024 * 1024),
        name="update",
    )(scale, summed, params, moment1, moment2, ema_params)


def solution(mesh):
    n = mesh.shape["batch"]

    def shards(params, moment1, moment2, ema_params, trajectories, noise_draw, timesteps, lengths):
        me = lax.axis_index("batch")
        shard_rows = params.shape[0] // D
        pad_rows = up_to(shard_rows, 16)
        ring = Ring(n, pad_rows)
        low_copy = jnp.pad(params.astype(BF16).reshape(shard_rows, D), ((0, pad_rows - shard_rows), (0, 0)))
        small = [ring.table(me, ring.plan_in), ring.table(me, ring.plan_out)]
        small += prepare(trajectories, noise_draw, timesteps, lengths)
        blocks, small = ring.gather(low_copy, small)
        horizons = trajectories.shape[0] * trajectories.shape[1]
        call = make_kernel(n, shard_rows, pad_rows, ring.plan_in, ring.plan_out, horizons, trajectories.shape[2])
        *sums, loss_parts = call(*small, *blocks)
        arrays = len(ring.plan_out)
        summed = ring.scatter(sums[:arrays], sums[arrays:])
        summed = summed[:shard_rows]
        local_count = jnp.sum(lengths).astype(F32) * CH
        lane = jnp.arange(128)[None, :]
        scalars = jnp.where(lane == 0, jnp.sum(loss_parts[:, 0]), jnp.where(lane == 1, local_count, jnp.sum(summed * summed)))
        scalars, summed = ring.total(jnp.broadcast_to(scalars, (8, 128)), summed.reshape(-1))
        loss_sum, frame_count, squares = scalars[0, 0], scalars[0, 1], scalars[0, 2]
        grad_norm = jnp.sqrt(squares) / frame_count
        scale = jnp.minimum(1.0, clip_limit / (grad_norm + 1e-06)) / frame_count
        return (*update(scale.reshape(1), summed, params, moment1, moment2, ema_params), grad_norm, loss_sum, frame_count)

    flat = P("batch")
    wide = P(None, "batch", None, None)
    narrow = P(None, "batch")
    return jax.shard_map(
        shards,
        mesh=mesh,
        in_specs=(flat, flat, flat, flat, wide, wide, narrow, narrow),
        out_specs=(flat, flat, flat, flat, flat, P(), P(), P()),
        check_vma=False,
    )
```

```python
import math

import jax
import jax.numpy as jnp
import numpy as np
from jax import lax
from jax.experimental import pallas as pl
from jax.experimental.pallas import tpu as pltpu
from jax.sharding import PartitionSpec as P

D = 256
TE = 128
CH = 6
GROUPS = 8
K = 5
DIFF = 256
STEP = 10

CHUNK = 64
HEAD = 8
clip_limit = 0.05

F32 = jnp.float32
BF16 = jnp.bfloat16


TIME_FIRST, TIME_FIRST_BIAS, TIME_SECOND, TIME_SECOND_BIAS, INPUT_CONV, INPUT_BIAS = range(6)
DOWN = 6
DOWN_SAMPLE, DOWN_SAMPLE_BIAS, UP_SAMPLE, UP_SAMPLE_BIAS = range(16, 20)
UP = 20
UP_RES, UP_RES_BIAS, HEAD_MAT, HEAD_BIAS = range(30, 34)
CONV1, BIAS1, GAIN1, SHIFT1, TIME, TIME_BIAS, CONV2, BIAS2, GAIN2, SHIFT2 = range(10)


def layout():
    counts = [TE, 1, D, 1, K * CH, 1]
    counts += [K * D, 1, 1, 1, D, 1, K * D, 1, 1, 1]
    counts += [3 * D, 1, 4 * D, 1]
    counts += [2 * K * D, 1, 1, 1, D, 1, K * D, 1, 1, 1, 2 * D, 1]
    counts += [CH, 1]
    return [(sum(counts[:i]), count) for i, count in enumerate(counts)]


ROWS = layout()
MATS = (
    TIME_FIRST,
    TIME_SECOND,
    DOWN + CONV1,
    DOWN + TIME,
    DOWN + CONV2,
    DOWN_SAMPLE,
    UP_SAMPLE,
    UP + CONV1,
    UP + TIME,
    UP + CONV2,
    UP_RES,
)
SUMS = (INPUT_BIAS, DOWN_SAMPLE_BIAS, UP_SAMPLE_BIAS, UP_RES_BIAS) + tuple(
    block + piece for block in (DOWN, UP) for piece in (BIAS1, GAIN1, SHIFT1, BIAS2, GAIN2, SHIFT2)
)
NORMS = 4


def up_to(value, step):
    return -(-value // step) * step


def mm(left, right):
    return jnp.dot(left, right, preferred_element_type=F32)


def mm_nt(left, right):
    return lax.dot_general(left, right, (((1,), (1,)), ((), ())), preferred_element_type=F32)


def mm_tn(left, right):
    return lax.dot_general(left, right, (((0,), (0,)), ((), ())), preferred_element_type=F32)


def mish_pair(v):
    c = jnp.minimum(v, 20.0)
    e = jnp.exp(c)
    n = e * (e + 2.0)
    r = 1.0 / (n + 2.0)
    t = n * r
    return v * t, t + (4.0 * c) * (e * (1.0 + e)) * (r * r)


def fold(values):
    rows, cols = values.shape
    return jnp.sum(values.reshape(rows // 8, 8, cols), axis=0)


def pad_get(pad, h, start, size, stride=1):
    where = pl.ds(start, size, stride=stride) if stride > 1 else pl.ds(start, size)
    return jnp.concatenate([pad[0, h, where, :], pad[1, h, where, :]], axis=1)


def pad_set(pad, h, start, value, stride=1):
    size = value.shape[0]
    where = pl.ds(start, size, stride=stride) if stride > 1 else pl.ds(start, size)
    pad[0, h, where, :] = value[:, : D // 2]
    pad[1, h, where, :] = value[:, D // 2 :]


def group_sums(parts, ones):
    horizons = parts[0].shape[0]
    rows = 8 * horizons
    stacked = []
    for part in parts:
        part = part.reshape(rows, D)
        high = part.astype(BF16).astype(F32)
        rest = part - high
        mid = rest.astype(BF16).astype(F32)
        stacked += [high, mid, rest - mid]
    summed = mm(jnp.concatenate(stacked, axis=0).astype(BF16), ones)
    pieces = [summed[rows * i : rows * i + rows] for i in range(3 * len(parts))]
    return [
        jnp.sum((pieces[3 * i] + pieces[3 * i + 1] + pieces[3 * i + 2]).reshape(horizons, 8, D), axis=1)
        for i in range(len(parts))
    ]


def make_kernel(n, shard_rows, pad_rows, plan_in, plan_out, horizons, length):
    half = length // 2
    count_inv = 1.0 / (length * (D // GROUPS))
    total_rows = n * shard_rows
    strips = sorted({(low, rows) for low, rows, _ in plan_in})
    every = horizons * length
    halves = horizons * half
    chunks = [slice(i, i + CHUNK) for i in range(0, length, CHUNK)]
    groups = [range(g * n // 8, (g + 1) * n // 8) for g in range(8)]
    D1, D2, U1, U2 = range(4)
    parts = 2 if horizons % 2 == 0 else 1

    def kernel(places_in, places_out, lens, scales, start, noise, emb, *rest):
        sources, rest = rest[: 2 * len(plan_in)], rest[2 * len(plan_in) :]
        targets, rest = rest[: 2 * len(plan_out)], rest[2 * len(plan_out) :]
        loss_out, *rest = rest
        run(places_in, places_out, lens, scales, start, noise, emb, sources, targets, loss_out, *rest)

    def run(
        places_in, places_out, lens, scales, start, noise, emb, sources, targets, loss_out,
        stage, flat, ones, padS, padR, padY, wide, slim, buf, extra, xt, xin,
        x_d1, x_d2, x_e, x_o, x_y, x_j, x_u2,
        xhat, mp, rstds, temb_d, temb_u, dtemb_d, dtemb_u,
        w_in, w_tf, w_ts, w_d1, w_dt, w_d2, w_ds, w_us, w_u1, w_ut, w_u2, w_res,
        t_d1, t_d2, t_ds, t_us, t_u1, t_u2,
        sem_in, sem_out,
    ):
        w = dict(zip(MATS, (w_tf, w_ts, w_d1, w_dt, w_d2, w_ds, w_us, w_u1, w_ut, w_u2, w_res)))

        def row(label):
            return flat[ROWS[label][0] : ROWS[label][0] + 1, :]

        def put(label, offset, value):
            first = ROWS[label][0] + offset
            flat[first : first + value.shape[0], :] = value

        def put_row(label, value):
            put(label, 0, jnp.sum(value.reshape(-1, D), axis=0, keepdims=True))

        def moves(plan, places):
            number = 0
            for i in range(2 * len(plan)):
                low_row, rows, blocks = plan[i % len(plan)]
                for b in range(len(blocks)):
                    yield i, b, pl.ds(low_row, rows), places[number]
                    number += 1

        for i, b, rows, s in moves(plan_in, places_in):
            pltpu.make_async_copy(sources[i].at[b], stage.at[s, rows, :], sem_in.at[s * 8 // n]).start()
        group_row = lax.broadcasted_iota(jnp.int32, (D, D), 0) // (D // GROUPS)
        group_col = lax.broadcasted_iota(jnp.int32, (D, D), 1) // (D // GROUPS)
        ones[...] = (group_row == group_col).astype(F32).astype(BF16)
        zero8 = jnp.zeros((8, D), F32)
        for pad, rows in ((padS, length), (padR, length), (padY, half)):
            for h in range(horizons):
                pad_set(pad, h, 0, zero8)
                pad_set(pad, h, rows + 8, zero8)
        dtemb_d[...] = jnp.zeros_like(dtemb_d)
        dtemb_u[...] = jnp.zeros_like(dtemb_u)
        for group in groups:
            for s in group:
                for low_row, rows in strips:
                    strip = stage.at[s, pl.ds(low_row, rows), :]
                    pltpu.make_async_copy(strip, strip, sem_in.at[s * 8 // n]).wait()
            for s in group:
                flat[s * shard_rows : s * shard_rows + pad_rows, :] = stage[s].astype(F32)
        for label in MATS:
            first, count = ROWS[label]
            for i in range(0, count, CHUNK):
                size = min(CHUNK, count - i)
                w[label][i : i + size, :] = flat[first + i : first + i + size, :].astype(BF16)
        for source, target, taps in ((w_d1, t_d1, K), (w_d2, t_d2, K), (w_us, t_us, 4), (w_u2, t_u2, K)):
            for k in range(taps):
                target[k * D : k * D + D, :] = source[k * D : k * D + D, :].T
        for k, source in enumerate((0, 2, 1)):
            t_ds[k * D : k * D + D, :] = w_ds[source * D : source * D + D, :].T
        for k in range(K):
            for j in range(2):
                t_u1[k * D : k * D + D, j * D : j * D + D] = w_u1[(2 * k + j) * D : (2 * k + j + 1) * D, :].T
        for j in range(2):
            t_u1[K * D : K * D + D, j * D : j * D + D] = w_res[j * D : j * D + D, :].T

        first = ROWS[HEAD_MAT][0]
        head_rows = flat[first : first + 8, :].astype(BF16)
        at_row = lax.broadcasted_iota(jnp.int32, (D, D), 0)
        at_col = lax.broadcasted_iota(jnp.int32, (D, D), 1)
        sub_row = lax.broadcasted_iota(jnp.int32, (8, D), 0)
        sub_col = lax.broadcasted_iota(jnp.int32, (8, D), 1)

        def picker(j):
            return ((at_col * CH + j) % D == at_row).astype(F32).astype(BF16)

        def picked(j):
            return (sub_col * CH + j) // D == sub_row

        head_t = zero8
        for j in range(CH):
            spread = mm(head_rows, picker(j))
            line = jnp.sum(jnp.where(picked(j), spread, 0.0), axis=0, keepdims=True)
            head_t = jnp.where(sub_row == j, line, head_t)
        head_b = head_t.astype(BF16)
        on_line = (sub_row == sub_col) & (sub_row < CH)
        head_bias = jnp.sum(jnp.where(on_line, row(HEAD_BIAS), 0.0), axis=1, keepdims=True)

        emb_b = emb[...]
        z1 = mm(emb_b, w_tf[...]) + row(TIME_FIRST_BIAS)
        t1, slope1 = mish_pair(z1)
        t1 = t1.astype(BF16)
        z2 = mm(t1, w_ts[...]) + row(TIME_SECOND_BIAS)
        t2, slope2 = mish_pair(z2)
        timing = t2.astype(BF16)
        temb_d[...] = mm(timing, w_dt[...]) + row(DOWN + TIME_BIAS)
        temb_u[...] = mm(timing, w_ut[...]) + row(UP + TIME_BIAS)

        share = horizons // parts
        some = share * length

        def rows_of(part):
            return slice(part * some, (part + 1) * some)

        def horizons_of(part):
            return [(h, h * length) for h in range(part * share, (part + 1) * share)]

        def halves_of(part):
            return [(h, part * some + (h - part * share) * half, h * half) for h in range(part * share, (part + 1) * share)]

        def rows_at(base, c):
            return slice(base + c.start, base + c.stop)

        def shifted(target, pad, step, offset, sign, part):
            for h, base in horizons_of(part):
                for k in range(K):
                    begin = 8 + sign * (k - K // 2)
                    left = step * k + offset
                    for c in chunks:
                        target[rows_at(base, c), left : left + D] = pad_get(pad, h, begin + c.start, CHUNK).astype(BF16)

        def norm_forward(layer, part, gain, shift, write):
            mine = horizons_of(part)
            totals = []
            for h, base in mine:
                total = zero8
                for c in chunks:
                    total = total + fold(buf[rows_at(base, c), :])
                totals.append(total)
            (mean,) = group_sums([jnp.stack(totals)], ones[...])
            mean = mean * count_inv
            totals = []
            for i, (h, base) in enumerate(mine):
                total = zero8
                for c in chunks:
                    off = buf[rows_at(base, c), :] - mean[i : i + 1]
                    total = total + fold(off * off)
                totals.append(total)
            (var,) = group_sums([jnp.stack(totals)], ones[...])
            rstd = lax.rsqrt(var * count_inv + 1e-05)
            rstds[layer, part, 0:share, :] = rstd
            for i, (h, base) in enumerate(mine):
                for c in chunks:
                    rows = rows_at(base, c)
                    xh = (buf[rows, :] - mean[i : i + 1]) * rstd[i : i + 1]
                    value, slope = mish_pair(xh * gain + shift)
                    xhat[layer, rows, :] = xh
                    mp[layer, rows, :] = slope.astype(BF16)
                    write(h, rows, c.start, value)

        pending = {}

        def put_sums(label, part, totals):
            pending[label] = sum(totals, pending.get(label, zero8))
            if part == parts - 1:
                put_row(label, pending[label])

        def norm_backward(layer, part, block, second, source):
            gain = gains[layer]
            mine = horizons_of(part)
            ones_, twos, plains = [], [], []
            for h, base in mine:
                one = two = plain = zero8
                for c in chunks:
                    rows = rows_at(base, c)
                    value = source[rows, :]
                    dv = value * mp[layer, rows, :].astype(F32)
                    plain = plain + fold(value)
                    one = one + fold(dv)
                    two = two + fold(dv * xhat[layer, rows, :])
                    buf[rows, :] = dv
                ones_.append(one)
                twos.append(two)
                plains.append(plain)
            put_sums(block + SHIFT1 + second, part, ones_)
            put_sums(block + GAIN1 + second, part, twos)
            mean1, mean2 = group_sums([jnp.stack(ones_) * gain, jnp.stack(twos) * gain], ones[...])
            rstd = rstds[layer, part, 0:share, :]
            scale = rstd * gain
            mean1 = rstd * (mean1 * count_inv)
            mean2 = rstd * (mean2 * count_inv)
            totals = []
            for i, (h, base) in enumerate(mine):
                total = zero8
                for c in chunks:
                    rows = rows_at(base, c)
                    dc = buf[rows, :] * scale[i : i + 1] - mean1[i : i + 1] - xhat[layer, rows, :] * mean2[i : i + 1]
                    pad_set(padR, h, c.start + 8, dc)
                    total = total + fold(dc)
                totals.append(total)
            put_sums(block + BIAS1 + second, part, totals)
            return plains

        def low(value):
            return value.astype(BF16).astype(F32)

        def weight_grads(source, slot, width, dy, targets):
            rows = source.shape[0]
            for j in range(width // D):
                xt[slot + j * D : slot + j * D + D, 0:rows] = source[:, j * D : j * D + D].T
            for label, offset, left in targets:
                put(label, offset, mm(xt[slot : slot + width, 0:rows], dy[:, left : left + D]))

        gains = [row(block + gain) for block in (DOWN, UP) for gain in (GAIN1, GAIN2)]
        shifts = [row(block + shift) for block in (DOWN, UP) for shift in (SHIFT1, SHIFT2)]
        frame = lax.broadcasted_iota(jnp.int32, (HEAD, length), 1)
        first = ROWS[INPUT_CONV][0]
        taps = [jnp.where(sub_row < CH, flat[first + CH * k : first + CH * k + 8, :], 0.0) for k in range(K)]
        w_in[...] = jnp.concatenate(taps + [zero8], axis=0).astype(BF16)
        input_bias, bias_d1, bias_d2, bias_ds, bias_us, bias_u1, bias_u2, bias_res = (
            row(label)
            for label in (
                INPUT_BIAS,
                DOWN + BIAS1,
                DOWN + BIAS2,
                DOWN_SAMPLE_BIAS,
                UP_SAMPLE_BIAS,
                UP + BIAS1,
                UP + BIAS2,
                UP_RES_BIAS,
            )
        )

        def entry(part):
            for h, base in horizons_of(part):
                at = slice(base, base + length)
                noisy = scales[h] * start[:, at] + scales[horizons + h] * noise[:, at]
                noisy = jnp.where(frame < lens[h], noisy, 0.0)
                taps = []
                for k in range(K):
                    shift = k - K // 2
                    moved = pltpu.roll(noisy, -shift % length, 1) if shift else noisy
                    taps.append(jnp.where((frame + shift >= 0) & (frame + shift < length), moved, 0.0))
                taps.append(jnp.zeros_like(noisy))
                xin[:, at] = jnp.concatenate(taps, axis=0).astype(BF16)
            extra[rows_of(part), :] = mm_tn(xin[:, rows_of(part)], w_in[...]) + input_bias
            for h, base in horizons_of(part):
                for c in chunks:
                    value = extra[rows_at(base, c), :]
                    pad_set(padR, h, c.start + 8, value)
                    x_d1[rows_at(base, c), :] = value.astype(BF16)
            shifted(slim, padR, D, 0, 1, part)

        def conv_d1(part):
            buf[rows_of(part), :] = mm(slim[rows_of(part), :], w_d1[...]) + bias_d1

        def with_time(temb, target):
            def write(h, rows, begin, value):
                value = value + temb[h : h + 1, :]
                pad_set(padR, h, begin + 8, value)
                target[rows, :] = value.astype(BF16)

            return write

        def norm_d1(part):
            norm_forward(D1, part, gains[D1], shifts[D1], with_time(temb_d, x_d2))
            shifted(slim, padR, D, 0, 1, part)

        def conv_d2(part):
            buf[rows_of(part), :] = mm(slim[rows_of(part), :], w_d2[...]) + bias_d2

        def write_skip(h, rows, begin, value):
            pad_set(padS, h, begin + 8, value + extra[rows, :])

        def norm_d2(part):
            norm_forward(D2, part, gains[D2], shifts[D2], write_skip)
            for h, at, among in halves_of(part):
                rows = slice(at, at + half)
                even = pad_get(padS, h, 8, half, 2).astype(BF16)
                odd = pad_get(padS, h, 9, half, 2).astype(BF16)
                slim[rows, 0:D] = pad_get(padS, h, 7, half, 2).astype(BF16)
                slim[rows, D : 2 * D] = even
                slim[rows, 2 * D : 3 * D] = odd
                x_e[among : among + half, :] = even
                x_o[among : among + half, :] = odd

        def low_half(part):
            return slice(part * some, part * some + some // 2)

        def high_half(part):
            return slice(part * some + some // 2, (part + 1) * some)

        def interleave(part):
            for h, at, _ in halves_of(part):
                pad_set(padR, h, 8, buf[at : at + half, :], 2)
                pad_set(padR, h, 9, buf[some // 2 + at : some // 2 + at + half, :], 2)

        def middle_forward(part):
            here = low_half(part)
            buf[here, :] = mm(slim[here, 0 : 3 * D], w_ds[...]) + bias_ds
            for h, at, among in halves_of(part):
                rows = slice(at, at + half)
                coarse = buf[rows, :]
                pad_set(padY, h, 8, coarse)
                now = coarse.astype(BF16)
                x_y[among : among + half, :] = now
                slim[rows, 0:D] = now
                slim[rows, D : 2 * D] = pad_get(padY, h, 7, half).astype(BF16)
                slim[rows, 2 * D : 3 * D] = pad_get(padY, h, 9, half).astype(BF16)
            now, before, after = (slim[here, k * D : k * D + D] for k in range(3))
            buf[here, :] = mm(now, w_us[D : 2 * D, :]) + mm(before, w_us[3 * D : 4 * D, :]) + bias_us
            buf[high_half(part), :] = mm(after, w_us[0:D, :]) + mm(now, w_us[2 * D : 3 * D, :]) + bias_us
            interleave(part)
            shifted(wide, padR, 2 * D, 0, 1, part)
            shifted(wide, padS, 2 * D, D, 1, part)

        def conv_u1(part):
            rows = rows_of(part)
            middle = 2 * (K // 2) * D
            x_j[rows, :] = wide[rows, middle : middle + 2 * D]
            extra[rows, :] = mm(wide[rows, middle : middle + 2 * D], w_res[...]) + bias_res
            buf[rows, :] = mm(wide[rows, :], w_u1[...]) + bias_u1

        def norm_u1(part):
            norm_forward(U1, part, gains[U1], shifts[U1], with_time(temb_u, x_u2))
            shifted(slim, padR, D, 0, 1, part)

        def conv_u2(part):
            buf[rows_of(part), :] = mm(slim[rows_of(part), :], w_u2[...]) + bias_u2

        top_at = slice((K + 1) * D, (K + 2) * D)

        def write_top(h, rows, begin, value):
            wide[rows, top_at] = (value + extra[rows, :]).astype(BF16)

        loss_terms, head_sums, dheads = [], [], []

        def norm_u2(part):
            norm_forward(U2, part, gains[U2], shifts[U2], write_top)
            rows = rows_of(part)
            top = wide[rows, top_at]
            error = mm_nt(head_b, top) + head_bias - noise[:, rows]
            channel = lax.broadcasted_iota(jnp.int32, (HEAD, length), 0)
            pieces = []
            for i, (h, base) in enumerate(horizons_of(part)):
                mine = error[:, i * length : (i + 1) * length]
                pieces.append(jnp.where((frame < lens[h]) & (channel < CH), mine, 0.0))
            error = jnp.concatenate(pieces, axis=1)
            loss_terms.append(jnp.sum(error * error, axis=1, keepdims=True))
            error = 2.0 * error
            head_sums.append(jnp.sum(error, axis=1, keepdims=True))
            error = error.astype(BF16)
            dheads.append(mm(error, top))
            dtop = mm_tn(error, head_b).astype(BF16)
            wide[rows, K * D : (K + 1) * D] = dtop
            extra[rows, :] = dtop.astype(F32)

        def back_u2(part):
            put_sums(UP_RES_BIAS, part, norm_backward(U2, part, UP, CONV2, extra))
            shifted(slim, padR, D, 0, -1, part)

        def conv_back_u2(part):
            buf[rows_of(part), :] = low(mm(slim[rows_of(part), :], t_u2[...]))

        def time_sums(target, part, plains):
            for (h, base), plain in zip(horizons_of(part), plains):
                target[h : h + 1, :] = jnp.sum(plain, axis=0, keepdims=True)

        def back_u1(part):
            time_sums(dtemb_u, part, norm_backward(U1, part, UP, 0, buf))
            shifted(wide, padR, D, 0, -1, part)

        def conv_back_u1(part):
            rows = rows_of(part)
            buf[rows, :] = low(mm(wide[rows, 0 : (K + 1) * D], t_u1[:, :D]))
            extra[rows, :] = low(mm(wide[rows, 0 : (K + 1) * D], t_u1[:, D:]))

        right = (K + 1) * D

        def middle_back(part):
            totals = []
            for h, base in horizons_of(part):
                total = zero8
                for c in chunks:
                    value = buf[rows_at(base, c), :]
                    pad_set(padR, h, c.start + 8, value)
                    total = total + fold(value)
                totals.append(total)
            put_sums(UP_SAMPLE_BIAS, part, totals)
            size = share * half
            for h, at, among in halves_of(part):
                for k in range(4):
                    left = right + k * D
                    wide[among : among + half, left : left + D] = pad_get(padR, h, 7 + k, half, 2).astype(BF16)
            mine = slice(part * size, (part + 1) * size)
            buf[low_half(part), :] = low(mm(wide[mine, right : right + 4 * D], t_us[...]))
            totals = []
            for h, at, among in halves_of(part):
                dcoarse = buf[at : at + half, :]
                pad_set(padY, h, 8, dcoarse)
                totals.append(fold(dcoarse))
                rows = slice(halves + among, halves + among + half)
                wide[rows, right : right + D] = pad_get(padY, h, 9, half).astype(BF16)
                wide[rows, right + D : right + 2 * D] = dcoarse.astype(BF16)
            put_sums(DOWN_SAMPLE_BIAS, part, totals)
            mine = slice(halves + part * size, halves + (part + 1) * size)
            buf[low_half(part), :] = low(mm(wide[mine, right + D : right + 2 * D], t_ds[2 * D : 3 * D, :]))
            buf[high_half(part), :] = low(mm(wide[mine, right : right + 2 * D], t_ds[0 : 2 * D, :]))
            interleave(part)
            for h, base in horizons_of(part):
                for c in chunks:
                    rows = rows_at(base, c)
                    extra[rows, :] = extra[rows, :] + pad_get(padR, h, c.start + 8, CHUNK)

        def back_d2(part):
            norm_backward(D2, part, DOWN, CONV2, extra)
            shifted(slim, padR, D, 0, -1, part)

        def conv_back_d2(part):
            buf[rows_of(part), :] = low(mm(slim[rows_of(part), :], t_d2[...]))

        def back_d1(part):
            time_sums(dtemb_d, part, norm_backward(D1, part, DOWN, 0, buf))
            shifted(wide, padR, D, 0, -1, part)

        def conv_back_d1(part):
            buf[rows_of(part), :] = low(mm(wide[rows_of(part), 0 : K * D], t_d1[...]))

        def at_entry(part):
            totals = []
            for h, base in horizons_of(part):
                total = zero8
                for c in chunks:
                    rows = rows_at(base, c)
                    value = buf[rows, :] + extra[rows, :]
                    total = total + fold(value)
                    slim[rows, 0:D] = value.astype(BF16)
                totals.append(total)
            put_sums(INPUT_BIAS, part, totals)

        def grads_u2():
            weight_grads(x_u2, 0, D, slim, [(UP + CONV2, k * D, k * D) for k in range(K)])

        def grads_u1():
            targets = [(UP + CONV1, 2 * k * D, k * D) for k in range(K)] + [(UP_RES, 0, K * D)]
            weight_grads(x_j, 0, 2 * D, wide, targets)

        def grads_middle():
            low_rows, high_rows = slice(0, halves), slice(halves, every)
            weight_grads(x_y, 0, D, wide.at[low_rows, :], [(UP_SAMPLE, k * D, right + k * D) for k in range(4)])
            weight_grads(
                x_o, D, D, wide.at[high_rows, :], [(DOWN_SAMPLE, 0, right), (DOWN_SAMPLE, 2 * D, right + D)]
            )
            weight_grads(x_e, 0, D, wide.at[high_rows, :], [(DOWN_SAMPLE, D, right + D)])

        def grads_d2():
            weight_grads(x_d2, D, D, slim, [(DOWN + CONV2, k * D, k * D) for k in range(K)])

        def grads_d1():
            weight_grads(x_d1, 0, D, wide, [(DOWN + CONV1, k * D, k * D) for k in range(K)])

        steps = [
            entry, conv_d1, norm_d1, conv_d2, norm_d2, middle_forward, conv_u1, norm_u1, conv_u2, norm_u2,
            back_u2, conv_back_u2, back_u1, conv_back_u1, middle_back,
            back_d2, conv_back_d2, back_d1, conv_back_d1, at_entry,
        ]
        beside = {back_u1: grads_u2, middle_back: grads_u1, conv_back_d2: grads_middle, back_d1: grads_d2}
        for i in range(len(steps) + parts - 1):
            for part in range(parts):
                if 0 <= i - part < len(steps):
                    steps[i - part](part)
            if i < len(steps) and steps[i] in beside:
                beside[steps[i]]()
        grads_d1()
        loss_out[...] = sum(loss_terms) + jnp.zeros((HEAD, 128), F32)
        head_sum = sum(head_sums)
        dhead = sum(dheads)
        entry_grads = mm(xin[...], slim[:, 0:D])
        for k in range(K):
            put(INPUT_CONV, CH * k, entry_grads[HEAD * k : HEAD * k + CH])

        down_b = dtemb_d[...].astype(BF16)
        up_b = dtemb_u[...].astype(BF16)
        put(DOWN + TIME, 0, mm_tn(timing, down_b))
        put(UP + TIME, 0, mm_tn(timing, up_b))
        dtiming = low(mm_nt(down_b, w_dt[...]) + mm_nt(up_b, w_ut[...]))
        dz2 = dtiming * slope2
        dz2_b = dz2.astype(BF16)
        put(TIME_SECOND, 0, mm_tn(t1, dz2_b))
        dz1 = low(mm_nt(dz2_b, w_ts[...])) * slope1
        put(TIME_FIRST, 0, mm_tn(emb_b, dz1.astype(BF16)))
        put_row(TIME_FIRST_BIAS, dz1)
        put_row(TIME_SECOND_BIAS, dz2)
        put_row(DOWN + TIME_BIAS, dtemb_d[...])
        put_row(UP + TIME_BIAS, dtemb_u[...])

        tail = ROWS[HEAD_MAT][0]
        flat[tail : total_rows + 16, :] = jnp.zeros((total_rows + 16 - tail, D), F32)
        packed = zero8
        for j in range(CH):
            spread = jnp.where(picked(j), jnp.broadcast_to(dhead[j : j + 1, :], (8, D)), 0.0)
            packed = packed + mm_nt(spread.astype(BF16), picker(j))
        put(HEAD_MAT, 0, packed[:CH])
        put_row(HEAD_BIAS, jnp.where(on_line, head_sum, 0.0))

        for s in range(n):
            stage[s] = flat[s * shard_rows : s * shard_rows + pad_rows, :].astype(BF16)
        outward = [
            pltpu.make_async_copy(stage.at[s, rows, :], targets[i].at[b], sem_out)
            for i, b, rows, s in moves(plan_out, places_out)
        ]
        for move in outward:
            move.start()
        for move in outward:
            move.wait()

    vm = pltpu.VMEM
    scratch = [
        vm((n, pad_rows, D), BF16),
        vm((total_rows + pad_rows, D), F32),
        vm((D, D), BF16),
        vm((2, horizons, length + 16, D // 2), F32),
        vm((2, horizons, length + 16, D // 2), F32),
        vm((2, horizons, half + 16, D // 2), F32),
        vm((every, 2 * K * D), BF16),
        vm((every, K * D), BF16),
        vm((every, D), F32),
        vm((every, D), F32),
        vm((2 * D, every), BF16),
        vm(((K + 1) * HEAD, every), BF16),
        vm((every, D), BF16),
        vm((every, D), BF16),
        vm((halves, D), BF16),
        vm((halves, D), BF16),
        vm((halves, D), BF16),
        vm((every, 2 * D), BF16),
        vm((every, D), BF16),
        vm((NORMS, every, D), F32),
        vm((NORMS, every, D), BF16),
        vm((NORMS, parts, 8, D), F32),
        vm((16, D), F32),
        vm((16, D), F32),
        vm((16, D), F32),
        vm((16, D), F32),
    ]
    scratch += [vm(((K + 1) * HEAD, D), BF16)]
    scratch += [vm((ROWS[label][1], D), BF16) for label in MATS]
    scratch += [
        vm((K * D, D), BF16),
        vm((K * D, D), BF16),
        vm((3 * D, D), BF16),
        vm((4 * D, D), BF16),
        vm(((K + 1) * D, 2 * D), BF16),
        vm((K * D, D), BF16),
        pltpu.SemaphoreType.DMA((8,)),
        pltpu.SemaphoreType.DMA,
    ]
    shapes = [jax.ShapeDtypeStruct((len(blocks), rows, D), BF16) for _, rows, blocks in plan_out] * 2
    shapes.append(jax.ShapeDtypeStruct((HEAD, 128), F32))
    smem = pl.BlockSpec(memory_space=pltpu.SMEM)
    local = pl.BlockSpec(memory_space=pltpu.VMEM)
    remote = pl.BlockSpec(memory_space=pl.ANY)
    flops = 6 * 2100000 * every
    return pl.pallas_call(
        kernel,
        out_shape=shapes,
        in_specs=[smem] * 4 + [local] * 3 + [remote] * (2 * len(plan_in)),
        out_specs=[remote] * (2 * len(plan_out)) + [local],
        scratch_shapes=scratch,
        compiler_params=pltpu.CompilerParams(vmem_limit_bytes=63 * 1024 * 1024),
        cost_estimate=pl.CostEstimate(flops=flops, bytes_accessed=10000000, transcendentals=3000000),
        name="step",
    )


def device_dims(n):
    known = {32: (4, 2, 2), 256: (4, 8, 4)}
    return known.get(n, (n // 2, 1, 1))


Z, Y, X, CORE = range(4)


class Ring:
    def __init__(self, n, rows):
        self.n = n
        self.dims = device_dims(n) + (2,)
        strides = [1]
        for size in self.dims[:0:-1]:
            strides.insert(0, strides[0] * size)
        self.strides = strides
        deep, tall, broad = self.dims[:3]
        self.square = tall == 2 and broad == 2 and deep % 2 == 0
        if self.square:
            self.cut = up_to(rows * 3 // 4, 16)
            self.half = deep // 2
            head = (0, self.cut)
            tail = (self.cut, rows - self.cut)
            full = range(deep)
            low, high, beside, above, own = (
                [(z, y, x) for z in zs]
                for zs, y, x in (
                    (range(self.half), 1, 1),
                    (range(self.half, deep), 1, 1),
                    (full, 0, 1),
                    (full, 1, 0),
                    (full, 0, 0),
                )
            )
            tails = tail + ([(z, y, x) for z in full for x in range(2) for y in range(2)],)
            rest = head + (beside + above + own,)
            self.plan_in = [head + (low,), head + (high,), tails, rest]
            self.plan_out = [head + (low + high,), tails, rest]
        else:
            places = [(z, y, x) for x in range(broad) for y in range(tall) for z in range(deep)]
            self.plan_in = self.plan_out = [(0, rows, places)]

    def moved(self, index, axis, step):
        at = index // self.strides[axis] % self.dims[axis]
        return index + ((at + step) % self.dims[axis] - at) * self.strides[axis]

    def send(self, values, *moves):
        def target(index):
            for axis, step in moves:
                index = self.moved(index, axis, step)
            return index

        return lax.ppermute(values, "batch", [(i, target(i)) for i in range(self.n)])

    def table(self, me, plan):
        places = [place + (core,) for core in range(2) for _, _, blocks in plan for place in blocks]
        result = jnp.zeros((len(places),), jnp.int32)
        for axis, (size, stride) in enumerate(zip(self.dims, self.strides)):
            step = np.array([place[axis] for place in places], np.int32)
            result = result + (me // stride + step) % size * stride
        return result

    def along(self, blocks, axis):
        size = self.dims[axis]
        if size == 1:
            return blocks
        return jnp.concatenate([blocks] + [self.send(blocks, (axis, size - step)) for step in range(1, size)], axis=0)

    def gather(self, own, small):
        if self.square:
            head = own[None, : self.cut]
            tail = own[None, self.cut :]
            tail_y = self.send(tail, (Y, 1))
            column = self.along(head, Z)
            pair = jnp.concatenate([tail, tail_y], axis=0)
            tails = jnp.concatenate([pair, self.send(pair, (X, 1))], axis=0)
            tails, column = lax.optimization_barrier((tails, column))
            head_x = self.send(column, (X, 1))
            head_y = self.send(column, (Y, 1))
            tails = [tails] + [self.send(tails, (Z, self.dims[Z] - step)) for step in range(1, self.dims[Z])]
            early = tails[1 : self.half] + tails[self.half + 1 :]
            head_x, head_y, early, small = lax.optimization_barrier((head_x, head_y, early, small))
            head_low = self.send(head_y[: self.half], (X, 1))
            head_high = self.send(head_x[self.half :], (Y, 1))
            late, head_low, head_high = lax.optimization_barrier((tails[self.half], head_low, head_high))
            tails = jnp.concatenate(tails[:1] + early[: self.half - 1] + [late] + early[self.half - 1 :], axis=0)
            rest = jnp.concatenate([head_x, head_y, column], axis=0)
            mine = [head_low, head_high, tails, rest]
        else:
            blocks = own[None]
            for axis in (Z, Y, X):
                blocks = self.along(blocks, axis)
            mine = [blocks]
        return mine + [self.send(blocks, (CORE, 1)) for blocks in mine], small

    def scatter(self, mine, away):
        first = self.send(away[0], (CORE, 1))
        first, away = lax.optimization_barrier((first, away[1:]))
        arrived = [first] + [self.send(blocks, (CORE, 1)) for blocks in away]
        pairs = list(zip(mine, arrived))

        def total(terms):
            return sum(term.astype(F32) for term in terms)

        def column(terms):
            deep = self.dims[Z]
            return [term[0] for term in terms] + [
                self.send(total(term[step] for term in terms).astype(BF16), (Z, step)) for step in range(1, deep)
            ]

        if not self.square:
            terms = list(pairs[0])
            for axis in (X, Y):
                size = self.dims[axis]
                terms = [term.reshape((size, term.shape[0] // size) + term.shape[1:]) for term in terms]
                arrived = [
                    self.send(total(term[step] for term in terms).astype(BF16), (axis, step)) for step in range(1, size)
                ]
                terms = [term[0] for term in terms] + arrived
            return total(column(terms))
        half = self.half
        deep = self.dims[Z]
        corner, tails, rest = pairs
        from_x = self.send(total(term[:half] for term in corner).astype(BF16), (X, 1))
        from_y = self.send(total(term[half:] for term in corner).astype(BF16), (Y, 1))
        tails, rest = lax.optimization_barrier((tails, rest))
        tail = column([term.reshape((deep, 4) + term.shape[1:]) for term in tails])
        at = len(tails) + half - 1
        rest, tail[at] = lax.optimization_barrier((rest, tail[at]))
        tail = total(tail)
        beside, above, own = ([term[deep * i : deep * i + deep] for term in rest] for i in range(3))
        nothing = jnp.zeros_like(from_x)
        from_y = jnp.concatenate([nothing, from_y], axis=0)
        from_x = jnp.concatenate([from_x, nothing], axis=0)
        got_x = self.send(total(beside + [from_y]).astype(BF16), (X, 1))
        got_y = self.send(total(above + [from_x]).astype(BF16), (Y, 1))
        tail, got_x, got_y = lax.optimization_barrier((tail, got_x, got_y))
        tail = tail[:2] + self.send(tail[2:].astype(BF16), (X, 1)).astype(F32)
        *head, last = column(own + [got_x, got_y])
        tail, last = lax.optimization_barrier((tail, last))
        tail = tail[0] + self.send(tail[1].astype(BF16), (Y, 1)).astype(F32)
        head = total(head + [last])
        return jnp.concatenate([head, tail], axis=0)

    def total(self, values, beside):
        arrived, beside = lax.optimization_barrier((self.send(values, (CORE, 1)), beside))
        values = values + arrived
        axes = (X, Y, Z)
        if self.square:
            other = self.send(values, (X, 1))
            across = [self.send(values, (Y, 1)), self.send(values, (X, 1), (Y, 1))]
            values = (values + other) + (across[0] + across[1])
            axes = (Z,)
        for axis in axes:
            size = self.dims[axis]
            if size == 4:
                one, two, three = (self.send(values, (axis, step)) for step in (1, 2, 3))
                values = (values + two) + (one + three)
                continue
            while size > 1:
                size //= 2
                values = values + self.send(values, (axis, size))
        return values, beside


def prepare(trajectories, noise_draw, timesteps, lengths):
    horizons = trajectories.shape[0] * trajectories.shape[1]
    length = trajectories.shape[2]
    lens = lengths.reshape(horizons)
    times = timesteps.reshape(horizons).astype(F32)
    angle_now = ((times + 1.0) / DIFF + 0.008) / 1.008 * (math.pi / 2)
    angle_zero = 0.008 / 1.008 * (math.pi / 2)
    share = jnp.cos(angle_now) ** 2 / math.cos(angle_zero) ** 2
    scales = jnp.concatenate([jnp.sqrt(share), jnp.sqrt(1.0 - share)])
    half_width = TE // 2
    frequency = jnp.exp(-math.log(10000.0) * jnp.arange(half_width, dtype=F32) / (half_width - 1))
    angles = times[:, None] * frequency[None, :]
    embedding = jnp.concatenate([jnp.sin(angles), jnp.cos(angles)], axis=1).astype(BF16)
    embedding = jnp.pad(embedding, ((0, 16 - horizons), (0, 0)))

    def lined_up(values):
        values = jnp.transpose(values, (3, 0, 1, 2)).reshape(CH, horizons * length)
        return jnp.pad(values, ((0, HEAD - CH), (0, 0)))

    return [lens, scales, lined_up(trajectories), lined_up(noise_draw), embedding]


def update(scale, summed, params, moment1, moment2, ema_params):
    def kernel(scale, summed, params, moment1, moment2, ema_params, new_params, new_moment1, new_moment2, new_ema, low):
        clipped = summed[...] * scale[0]
        first = 0.9 * moment1[...] + 0.1 * clipped
        second = 0.95 * moment2[...] + 0.05 * clipped * clipped
        new_moment1[...] = first
        new_moment2[...] = second
        first_hat = first / (1.0 - 0.9**STEP)
        second_hat = second / (1.0 - 0.95**STEP)
        old = params[...]
        new = old - 0.01 * (first_hat / (jnp.sqrt(second_hat) + 1e-08) + 0.01 * old)
        new_params[...] = new
        new_ema[...] = 0.8 * ema_params[...] + 0.2 * new
        low[...] = new.astype(BF16)

    clipped = summed * scale[0]
    first = 0.9 * moment1 + 0.1 * clipped
    second = 0.95 * moment2 + 0.05 * clipped * clipped
    first_hat = first / (1.0 - 0.9**STEP)
    second_hat = second / (1.0 - 0.95**STEP)
    new = params - 0.01 * (first_hat / (jnp.sqrt(second_hat) + 1e-08) + 0.01 * params)
    return new, first, second, 0.8 * ema_params + 0.2 * new, new.astype(BF16)


def solution(mesh):
    n = mesh.shape["batch"]

    def shards(params, moment1, moment2, ema_params, trajectories, noise_draw, timesteps, lengths):
        me = lax.axis_index("batch")
        shard_rows = params.shape[0] // D
        pad_rows = up_to(shard_rows, 16)
        ring = Ring(n, pad_rows)
        low_copy = jnp.pad(params.astype(BF16).reshape(shard_rows, D), ((0, pad_rows - shard_rows), (0, 0)))
        small = [ring.table(me, ring.plan_in), ring.table(me, ring.plan_out)]
        small += prepare(trajectories, noise_draw, timesteps, lengths)
        blocks, small = ring.gather(low_copy, small)
        horizons = trajectories.shape[0] * trajectories.shape[1]
        call = make_kernel(n, shard_rows, pad_rows, ring.plan_in, ring.plan_out, horizons, trajectories.shape[2])
        *sums, loss_parts = call(*small, *blocks)
        arrays = len(ring.plan_out)
        summed = ring.scatter(sums[:arrays], sums[arrays:])
        summed = summed[:shard_rows]
        local_count = jnp.sum(lengths).astype(F32) * CH
        lane = jnp.arange(128)[None, :]
        scalars = jnp.where(lane == 0, jnp.sum(loss_parts[:, 0]), jnp.where(lane == 1, local_count, jnp.sum(summed * summed)))
        scalars, summed = ring.total(jnp.broadcast_to(scalars, (8, 128)), summed.reshape(-1))
        loss_sum, frame_count, squares = scalars[0, 0], scalars[0, 1], scalars[0, 2]
        grad_norm = jnp.sqrt(squares) / frame_count
        scale = jnp.minimum(1.0, clip_limit / (grad_norm + 1e-06)) / frame_count
        return (*update(scale.reshape(1), summed, params, moment1, moment2, ema_params), grad_norm, loss_sum, frame_count)

    flat = P("batch")
    wide = P(None, "batch", None, None)
    narrow = P(None, "batch")
    return jax.shard_map(
        shards,
        mesh=mesh,
        in_specs=(flat, flat, flat, flat, wide, wide, narrow, narrow),
        out_specs=(flat, flat, flat, flat, flat, P(), P(), P()),
        check_vma=False,
    )
```
